128 devices in a mesh: gx: 8 (over y, core), gy: 4 (over z), af: 4 (over x).
Axes of the slice: x: 4, y: 4, z: 4, core: 2. Of those that a mesh axis runs over, the one named last changes fastest.
Arguments:
- press_matrix: float32 [8, 64, 2048], P(None, 'gx', ('gy', 'af')), may hold values from -1.5 to 1.5
- cond_matrix: float32 [8, 64, 2048], P(None, 'gx', ('gy', 'af')), may hold values from 0.05 to 0.5
- accum_matrix: float32 [8, 64, 2048], P(None, 'gx', ('gy', 'af')), may hold values from 0.5 to 2
- press_frac: float32 [512, 256], P(('gx', 'gy', 'af')), may hold values from -1.5 to 1.5
- accum_frac: float32 [512, 256], P(('gx', 'gy', 'af')), may hold values from 0.3 to 1
- trans_chain: float32 [512, 256], P(('gx', 'gy', 'af')), may hold values from 0.1 to 1
- couple_mf: float32 [512, 256], P(('gx', 'gy', 'af')), may hold values from 0.7 to 1.4
- couple_fm: float32 [512, 256], P(('gx', 'gy', 'af')), may hold values from 0.6 to 1.2
- conn_tile: int32 [512, 256], P(('gx', 'gy', 'af')), may hold values from 0 to 127, as said below
- conn_layer: int32 [512, 256], P(('gx', 'gy', 'af')), may hold values from 0 to 7
- conn_cell: int32 [512, 256], P(('gx', 'gy', 'af')), may hold values from 0 to 1023
- inter_delta: int32 [512], P(('gx', 'gy', 'af')), may hold values from 0 to 4, as said below
- inter_from: int32 [512], P(('gx', 'gy', 'af')), may hold values from 0 to 255
- inter_to: int32 [512], P(('gx', 'gy', 'af')), may hold values from 0 to 255
- inter_trans: float32 [512], P(('gx', 'gy', 'af')), may hold values from 0.5 to 2
- well_tile: int32 [32], replicated, may hold values from 0 to 127
- well_cell: int32 [32], replicated, may hold values from 0 to 1023
- well_rate: float32 [32], replicated, may hold values from -8 to 8
Outputs:
- res_matrix: float32 [8, 64, 2048], P(None, 'gx', ('gy', 'af'))
- res_fracture: float32 [512, 256], P(('gx', 'gy', 'af'))
- adj_matrix: float32 [8, 64, 2048], P(None, 'gx', ('gy', 'af'))
- adj_fracture: float32 [512, 256], P(('gx', 'gy', 'af'))
The draws below stay inside these ranges and needn't reach their ends.
Inputs may be any that keep to these rules, and one draw needn't show every extreme that they name: `conn_tile`: in each aligned run of 1024 segments (blocks k * 4 to (k + 1) * 4 - 1), at most 16 segments lie in cells of one tile; in every draw some tile holds exactly 16 segments of every such run. b + inter_delta(b) never passes the last block; the value 4 is reached.
All inputs are finite; a program needn't handle non-finite values.
Results may differ from the reference program's by a relative error of at most 0.00013.
Values sent between devices are 32-bit elements; how exact they have to be, the bound alone decides.
No kernel may reach another device: no remote copies, remote signals or barrier semaphores. Data moves between devices by JAX's collectives and lax.ppermute only.
A program may use at most 64 MiB of HBM per device.

```python
import math
import jax
import jax.numpy as jnp
from jax import lax

CX = 8
CY = 128
NZ = 8
FB_DEV = 4
BLOCK = 256
NW = 32
ITERS = 8
NTILE = 128
NX = 64
NY = 2048
NFB = 512
SEG_DEV = 1024
CAP = 16
N_GY = 4
N_AF = 4


def draw_conn_tile(key, part):
    key_level = jax.random.fold_in(key, 11)
    key_heavy = jax.random.fold_in(key, 12)
    key_noise = jax.random.fold_in(key, 13)
    key_order = jax.random.fold_in(key, 14)
    levels = jax.random.randint(key_level, (NTILE, NTILE), 0, 4)
    heavy = jax.random.randint(key_heavy, (), 0, NTILE)
    owner_ids = jnp.arange(NTILE)
    levels = jnp.where(owner_ids[None, :] == heavy, 15, levels)
    slot_ids = jnp.arange(NTILE * CAP)
    slot_owner = slot_ids // CAP
    noise = jax.random.randint(key_noise, (NTILE, NTILE * CAP), 0, 128)
    scores = (levels[:, slot_owner] * 128 + noise) * (NTILE * CAP) + slot_ids[None, :]
    chosen = lax.top_k(scores, SEG_DEV)[1]
    owners = chosen // CAP
    owners = jax.random.permutation(key_order, owners, axis=1, independent=True)
    return owners.reshape(NFB, BLOCK).astype(jnp.int32)


def draw_inter_delta(key, part):
    raw = jax.random.randint(jax.random.fold_in(key, 23), (NFB,), 0, FB_DEV + 1)
    block_ids = jnp.arange(NFB)
    raw = jnp.where(block_ids == 0, FB_DEV, raw)
    return jnp.minimum(raw, NFB - 1 - block_ids).astype(jnp.int32)


def touch_ends(result, own_key, low, largest):
    shape = result.shape
    index_at = [jax.random.randint(jax.random.fold_in(own_key, axis), (), 0, shape[axis]) for axis in range(len(shape))]
    result = result.at[tuple(index_at)].set(low)
    longest = shape.index(max(shape))
    index_at[longest] = (index_at[longest] + 1) % shape[longest]
    return result.at[tuple(index_at)].set(largest)


def steps_of(key, dims, pieces, low, top_value):
    def one(axis_at, blocks):
        steps = jax.random.uniform(jax.random.fold_in(jax.random.fold_in(key, 6), axis_at), (blocks,), jnp.float32, low / len(pieces), top_value / len(pieces))
        return jnp.repeat(jnp.exp(steps), dims[axis_at] // blocks).reshape((-1,) + (1,) * (len(dims) - axis_at - 1))

    gain = one(*pieces[0])
    for cut in pieces[1:]:
        gain = gain * one(*cut)
    return gain


def centred(rng, shape, scale, limit, split=(), held_as=jnp.bfloat16):
    drawn = jax.random.normal(rng, shape, jnp.float32) * scale
    if len(split) > 0:
        drawn = steps_of(rng, shape, split, -0.22, 0.18) * drawn
    return jnp.clip(drawn, min=-limit, max=limit).astype(held_as)


def setup_inputs(seed: int = 0) -> dict:
    seeds = jax.random.split(jax.random.key(seed), 19)
    return {
        "press_matrix": centred(seeds[0], (NZ, NX, NY), 0.25, 1.5, ((1, 8), (2, 16)), jnp.float32),
        "cond_matrix": jnp.clip(jnp.exp(math.log(0.5) - 2.3025851 * jax.random.uniform(seeds[1], (NZ, NX, NY), jnp.float32) ** steps_of(seeds[1], (NZ, NX, NY), ((1, 8), (2, 16)), -0.2, 0.2)), 0.05, 0.5),
        "accum_matrix": jnp.clip(jnp.exp(math.log(2.0) - 1.3862944 * jax.random.uniform(seeds[2], (NZ, NX, NY), jnp.float32) ** steps_of(seeds[2], (NZ, NX, NY), ((1, 8), (2, 16)), -0.2, 0.2)), 0.5, 2.0),
        "press_frac": centred(seeds[3], (NFB, BLOCK), 0.25, 1.5, ((0, 128),), jnp.float32),
        "accum_frac": jnp.clip(jnp.exp(math.log(1.0) - 1.2039728 * jax.random.uniform(seeds[4], (NFB, BLOCK), jnp.float32) ** steps_of(seeds[4], (NFB, BLOCK), ((0, 128),), -0.2, 0.2)), 0.3, 1.0),
        "trans_chain": jnp.clip(jnp.exp(math.log(1.0) - 2.3025851 * jax.random.uniform(seeds[5], (NFB, BLOCK), jnp.float32) ** steps_of(seeds[5], (NFB, BLOCK), ((0, 128),), -0.2, 0.2)), 0.1, 1.0),
        "couple_mf": jnp.clip(jnp.exp(math.log(1.4) - 0.6931472 * jax.random.uniform(seeds[6], (NFB, BLOCK), jnp.float32) ** steps_of(seeds[6], (NFB, BLOCK), ((0, 128),), -0.2, 0.2)), 0.7, 1.4),
        "couple_fm": jnp.clip(jnp.exp(math.log(1.2) - 0.6931472 * jax.random.uniform(seeds[7], (NFB, BLOCK), jnp.float32) ** steps_of(seeds[7], (NFB, BLOCK), ((0, 128),), -0.2, 0.2)), 0.6, 1.2),
        "conn_tile": draw_conn_tile(jax.random.fold_in(seeds[18], 71), 0),
        "conn_layer": touch_ends(jax.random.randint(seeds[9], (NFB, BLOCK), 0, NZ), jax.random.fold_in(seeds[9], 1), 0, NZ - 1).astype(jnp.int32),
        "conn_cell": touch_ends(jax.random.randint(seeds[10], (NFB, BLOCK), 0, CX * CY), jax.random.fold_in(seeds[10], 1), 0, (CX * CY) - 1).astype(jnp.int32),
        "inter_delta": draw_inter_delta(jax.random.fold_in(seeds[18], 71), 0),
        "inter_from": touch_ends(jax.random.randint(seeds[12], (NFB,), 0, BLOCK), jax.random.fold_in(seeds[12], 1), 0, BLOCK - 1).astype(jnp.int32),
        "inter_to": touch_ends(jax.random.randint(seeds[13], (NFB,), 0, BLOCK), jax.random.fold_in(seeds[13], 1), 0, BLOCK - 1).astype(jnp.int32),
        "inter_trans": jnp.clip(jnp.exp(math.log(2.0) - 1.3862944 * jax.random.uniform(seeds[14], (NFB,), jnp.float32) ** steps_of(seeds[14], (NFB,), ((0, 128),), -0.2, 0.2)), 0.5, 2.0),
        "well_tile": touch_ends(jax.random.randint(seeds[15], (NW,), 0, NTILE), jax.random.fold_in(seeds[15], 1), 0, NTILE - 1).astype(jnp.int32),
        "well_cell": touch_ends(jax.random.randint(seeds[16], (NW,), 0, CX * CY), jax.random.fold_in(seeds[16], 1), 0, (CX * CY) - 1).astype(jnp.int32),
        "well_rate": centred(seeds[17], (NW,), 2.0, 8.0, (), jnp.float32),
    }


vertical_factor = 0.5


def harmonic(first, second):
    return 2.0 * first * second / (first + second)


def reference(press_matrix, cond_matrix, accum_matrix, press_frac, accum_frac, trans_chain, couple_mf, couple_fm, conn_tile, conn_layer, conn_cell, inter_delta, inter_from, inter_to, inter_trans, well_tile, well_cell, well_rate):
    tiles_y = N_GY * N_AF
    pad_x = jnp.pad(cond_matrix, ((0, 0), (1, 1), (0, 0)))
    trans_x = harmonic(pad_x[:, :-1], pad_x[:, 1:])
    pad_y = jnp.pad(cond_matrix, ((0, 0), (0, 0), (1, 1)))
    trans_y = harmonic(pad_y[:, :, :-1], pad_y[:, :, 1:])
    trans_z = vertical_factor * harmonic(cond_matrix[:-1], cond_matrix[1:])
    zero_layer = jnp.zeros((1, NX, NY), jnp.float32)
    diag_matrix = accum_matrix + trans_x[:, 1:] + trans_x[:, :-1] + trans_y[:, :, 1:] + trans_y[:, :, :-1]
    diag_matrix = diag_matrix + jnp.concatenate([trans_z, zero_layer]) + jnp.concatenate([zero_layer, trans_z])

    def stencil(field):
        field_x = jnp.pad(field, ((0, 0), (1, 1), (0, 0)))
        field_y = jnp.pad(field, ((0, 0), (0, 0), (1, 1)))
        total = trans_x[:, 1:] * field_x[:, 2:] + trans_x[:, :-1] * field_x[:, :-2]
        total = total + trans_y[:, :, 1:] * field_y[:, :, 2:] + trans_y[:, :, :-1] * field_y[:, :, :-2]
        total = total + jnp.concatenate([trans_z * field[1:], zero_layer]) + jnp.concatenate([zero_layer, trans_z * field[:-1]])
        return total

    position = jnp.arange(BLOCK)
    trans_next = jnp.where(position[None, :] < BLOCK - 1, trans_chain, 0.0)
    zero_col = jnp.zeros((NFB, 1), jnp.float32)
    trans_prev = jnp.concatenate([zero_col, trans_next[:, :-1]], axis=1)
    diag_frac = accum_frac + trans_next + trans_prev + couple_fm

    def chain(field):
        upper = jnp.concatenate([field[:, 1:], zero_col], axis=1)
        lower = jnp.concatenate([zero_col, field[:, :-1]], axis=1)
        return trans_next * upper + trans_prev * lower

    row_x = (conn_tile // tiles_y) * CX + conn_cell // CY
    col_y = (conn_tile % tiles_y) * CY + conn_cell % CY

    def gather_cells(field):
        return field[conn_layer, row_x, col_y]

    def scatter_cells(values):
        return jnp.zeros((NZ, NX, NY), jnp.float32).at[conn_layer, row_x, col_y].add(values)

    partner_row = jnp.arange(NFB, dtype=jnp.int32) + inter_delta
    from_hot = (position[None, :] == inter_from[:, None]).astype(jnp.float32)

    def forward_cross(field):
        picked = field[partner_row, inter_to]
        return from_hot * (inter_trans * picked)[:, None]

    def adjoint_cross(field):
        picked = inter_trans * jnp.sum(from_hot * field, axis=1)
        return jnp.zeros((NFB, BLOCK), jnp.float32).at[partner_row, inter_to].add(picked)

    well_x = (well_tile // tiles_y) * CX + well_cell // CY
    well_y = (well_tile % tiles_y) * CY + well_cell % CY
    source_plane = jnp.zeros((NX, NY), jnp.float32).at[well_x, well_y].add(well_rate)
    source = jnp.broadcast_to(source_plane[None], (NZ, NX, NY))

    res_matrix = diag_matrix * press_matrix - stencil(press_matrix) - scatter_cells(couple_mf * press_frac) - source
    res_fracture = diag_frac * press_frac - chain(press_frac) - couple_fm * gather_cells(press_matrix) - forward_cross(press_frac)

    adj_matrix = res_matrix / diag_matrix
    adj_fracture = res_fracture / diag_frac
    for sweep_index in range(ITERS - 1):
        image_matrix = diag_matrix * adj_matrix - stencil(adj_matrix) - scatter_cells(couple_fm * adj_fracture)
        image_fracture = diag_frac * adj_fracture - chain(adj_fracture) - couple_mf * gather_cells(adj_matrix) - adjoint_cross(adj_fracture)
        adj_matrix = adj_matrix + (res_matrix - image_matrix) / diag_matrix
        adj_fracture = adj_fracture + (res_fracture - image_fracture) / diag_frac
    return res_matrix, res_fracture, adj_matrix, adj_fracture
```

```python
import jax
import jax.numpy as jnp
from jax import lax
from jax.experimental import pallas as pl
from jax.experimental.pallas import tpu as pltpu
from jax.sharding import PartitionSpec as P

ITERS = 8
CAP = 16
TILES = 128
ROWS = 64
EXT = 24
LAYERS = 8
SLOTS = CAP * TILES
ALL = ("gx", "gy", "af")
YA = ("gy", "af")
f32 = jnp.float32
bf16 = jnp.bfloat16
i32 = jnp.int32


def iota(shape, axis):
    return lax.broadcasted_iota(i32, shape, axis)


def parts(value):
    high = value.astype(bf16)
    return high, (value - high.astype(f32)).astype(bf16)


def dot_nn(a, b):
    return lax.dot_general(a, b, (((1,), (0,)), ((), ())), preferred_element_type=f32)


def dot_nt(a, b):
    return lax.dot_general(a, b, (((1,), (1,)), ((), ())), preferred_element_type=f32)


def dot_tn(a, b):
    return lax.dot_general(a, b, (((0,), (0,)), ((), ())), preferred_element_type=f32)


def as_row(rows):
    return jnp.concatenate([rows[i : i + 1] for i in range(rows.shape[0])], axis=1)


def as_rows(row):
    return jnp.concatenate([row[:, i : i + 128] for i in range(0, row.shape[1], 128)], axis=0)


def total(value):
    return jnp.sum(jnp.sum(value, axis=1, keepdims=True), axis=0, keepdims=True)


def fold(value):
    return jnp.concatenate([value[:, :128], value[:, 128:]], axis=0)


def unfold(value):
    return jnp.concatenate([value[:4], value[4:]], axis=1)


def seg_code():
    row = iota((8, 128), 0)
    return (row % 4) * 256 + (row // 4) * 128 + iota((8, 128), 1)


def chain(tnext, field):
    lane = iota((8, 128), 1)
    ahead = pltpu.roll(field, 127, 1)
    ahead = jnp.where(lane == 127, pltpu.roll(ahead, 4, 0), ahead)
    behind = pltpu.roll(tnext * field, 1, 1)
    behind = jnp.where(lane == 0, pltpu.roll(behind, 4, 0), behind)
    return tnext * ahead + behind


def owner_hot(owner_row):
    return (iota((TILES, 1024), 0) == owner_row).astype(bf16)


def rank_mask(rank_row):
    return iota((CAP, 1024), 0) == rank_row


def to_slots(values, hot, mask):
    halves = ([], [])
    for value in values:
        row = as_row(value)
        for half, part in zip(halves, parts(row)):
            half.append(jnp.where(mask, part.astype(f32), 0.0).astype(bf16))
    both = jnp.concatenate([jnp.concatenate(half, axis=0) for half in halves], axis=1)
    return dot_nt(both, jnp.concatenate([hot, hot], axis=1))


def from_slots(table, hot, mask):
    high, low = parts(table)
    rows = dot_nn(jnp.concatenate([high, low], axis=1), jnp.concatenate([hot, hot], axis=0))
    return as_rows(jnp.sum(jnp.where(mask, rows, 0.0), axis=0, keepdims=True))


def cell_hot(index_row):
    columns = (iota((128, SLOTS), 0) == (index_row & 127)).astype(bf16)
    return columns, iota((ROWS, SLOTS), 0) == (index_row >> 7)


def scatter(tables, columns, mask):
    stacked = []
    for table in tables:
        for part in parts(as_row(table)):
            stacked.append(jnp.where(mask, part.astype(f32), 0.0).astype(bf16))
    sums = dot_nt(jnp.concatenate(stacked, axis=0), columns)
    return [
        (sums[2 * i * ROWS : (2 * i + 1) * ROWS] + sums[(2 * i + 1) * ROWS : (2 * i + 2) * ROWS]).reshape(LAYERS, 8, 128)
        for i in range(len(tables))
    ]


def gather(fields, columns, mask):
    stacked = []
    for field in fields:
        stacked.extend(parts(field.reshape(ROWS, 128)))
    rows = dot_nn(jnp.concatenate(stacked, axis=0), columns)
    out = []
    for i in range(len(fields)):
        both = rows[2 * i * ROWS : (2 * i + 1) * ROWS] + rows[(2 * i + 1) * ROWS : (2 * i + 2) * ROWS]
        out.append(as_rows(jnp.sum(jnp.where(mask, both, 0.0), axis=0, keepdims=True)))
    return out


def faces_of(field):
    rows = iota((16, 128), 0)
    lanes = iota((16, 128), 1)
    pick = (((rows == 0) & (lanes == 0)) | ((rows == 1) & (lanes == 127))).astype(bf16)
    both = dot_nt(jnp.concatenate([pick, pick], axis=1), jnp.concatenate(parts(field), axis=1))
    return both[0:1], both[1:2]


def columns_of(left, right):
    width = left.shape[1]
    held = [part.astype(f32) for row in (left, right) for part in parts(row)]
    held = jnp.concatenate(held + [jnp.zeros((12, width), f32)], axis=0).astype(bf16)
    rows = iota((16, 128), 0)
    lanes = iota((16, 128), 1)
    place = (((rows < 2) & (lanes == 0)) | ((rows >= 2) & (rows < 4) & (lanes == 127))).astype(bf16)
    return dot_tn(held, place)


def up_x(v):
    return jnp.concatenate([v[:, 1:], jnp.zeros_like(v[:, :1])], axis=1)


def down_x(v):
    return jnp.concatenate([jnp.zeros_like(v[:, :1]), v[:, :-1]], axis=1)


def up_z(v):
    return jnp.concatenate([v[1:], jnp.zeros_like(v[:1])], axis=0)


def down_z(v):
    return jnp.concatenate([jnp.zeros_like(v[:1]), v[:-1]], axis=0)


def up_y(v, halo):
    return jnp.where(iota(v.shape, 2) == 127, halo, pltpu.roll(v, 127, 2))


def down_y(v, first):
    return jnp.where(iota(v.shape, 2) == 0, first, pltpu.roll(v, 1, 2))


def stencil(tx, ty, tz, ty_first, field, halo):
    out = tx * up_x(field) + down_x(tx * field)
    out = out + ty * up_y(field, halo) + down_y(ty * field, ty_first * halo)
    return out + tz * up_z(field) + down_z(tz * field)


def harmonic(first, second):
    both = first + second
    return jnp.where(both > 0.0, 2.0 * first * second / jnp.where(both > 0.0, both, 1.0), 0.0)


def read_faces(me, got_ref, start, width):
    along = me & 15
    before = got_ref[jnp.maximum(me - 1, 0), :, start : start + width]
    after = got_ref[jnp.minimum(me + 1, TILES - 1), :, start : start + width]
    return jnp.where(along > 0, before, 0.0), jnp.where(along < 15, after, 0.0)


def put_faces(me, out_ref, start, first, last):
    width = first.shape[1]
    out_ref[jnp.maximum(me - 1, 0), :, start : start + width] = first
    out_ref[jnp.minimum(me + 1, TILES - 1), :, start : start + width] = last


def edge_codes(delta_ref, to_ref, b):
    block = b + delta_ref[b]
    code = block * 256 + to_ref[b]
    return jnp.where(block < 4, code, -1), jnp.where(block >= 4, code - 1024, -1)


def spread(rows, shift):
    lane = iota(rows.shape, 1)
    inside = (lane >= shift) if shift > 0 else (lane < TILES + shift)
    return jnp.where(inside, pltpu.roll(rows, shift % TILES, 1), 0.0)


def store_slots(out_ref, rows):
    for i in range(0, rows.shape[0], 128):
        out_ref[:, 0, i : i + 128] = rows[i : i + 128].T


def load_slots(got_ref, count):
    return jnp.concatenate([got_ref[:, 0, i : i + 128].T for i in range(0, count, 128)], axis=0)


def begin_kernel(
    me_ref, delta_ref, from_ref, to_ref, trans_ref,
    press_ref, cond_ref, left_ref, right_ref,
    press_frac_ref, follow_ref, accum_ref, chain_ref, mf_ref, fm_ref,
    tile_ref, layer_ref, cell_ref,
    out_ref, seg_ref,
):
    me = me_ref[0]
    code = seg_code()
    owner = fold(tile_ref[...])
    owner_row = as_row(owner)
    hot = owner_hot(owner_row)
    before = (iota((128, 128), 0) < iota((128, 128), 1)).astype(bf16)
    base = jnp.zeros((TILES, 1), f32)
    ranks = []
    for c in range(8):
        part = hot[:, c * 128 : (c + 1) * 128]
        wide = part.astype(f32)
        count = dot_nn(part, before) + base
        ranks.append(jnp.sum(wide * count, axis=0, keepdims=True))
        base = base + jnp.sum(wide, axis=1, keepdims=True)
    rank_row = jnp.concatenate(ranks, axis=1).astype(i32)
    rank = as_rows(rank_row)
    mask = rank_mask(rank_row)

    press = fold(press_frac_ref[...])
    follow = fold(follow_ref[...])
    fm = fold(fm_ref[...])
    mf = fold(mf_ref[...])
    last = code % 256 == 255
    tnext = jnp.where(last, 0.0, fold(chain_ref[...]))
    tprev = pltpu.roll(tnext, 1, 1)
    tprev = jnp.where(iota((8, 128), 1) == 0, pltpu.roll(tprev, 4, 0), tprev)
    diag = fold(accum_ref[...]) + tnext + tprev + fm
    inverse = 1.0 / diag
    partial = diag * press - chain(tnext, press)
    edges = []
    for b in range(4):
        here, there = edge_codes(delta_ref, to_ref, b)
        picked = total(jnp.where(code == here, press, 0.0) + jnp.where(code == there, follow, 0.0))
        at = code == b * 256 + from_ref[b]
        partial = partial - jnp.where(at, trans_ref[b] * picked, 0.0)
    first = inverse * partial
    weight = inverse * fm
    for b in range(4):
        here, there = edge_codes(delta_ref, to_ref, b)
        at = code == b * 256 + from_ref[b]
        edges.append(jnp.full((1, 128), there.astype(f32)))
        place = jnp.where(at, (owner * CAP + rank).astype(f32), 0.0)
        for value in (place, jnp.where(at, trans_ref[b] * first, 0.0), jnp.where(at, trans_ref[b] * weight, 0.0)):
            edges.append(jnp.broadcast_to(total(value), (1, 128)))
    where_cell = (fold(layer_ref[...]) * 1024 + fold(cell_ref[...]) + 1).astype(f32)
    slots = to_slots([where_cell, mf * press, fm * first, fm * weight], hot, mask)
    rows = jnp.concatenate([spread(slots, 16), slots, spread(slots, -16)] + edges + [jnp.zeros((48, 128), f32)], axis=0)
    store_slots(out_ref, rows)
    wide = [
        jnp.concatenate([left_ref[i], ref[...], right_ref[i]], axis=1).reshape(LAYERS * EXT, 128)
        for i, ref in enumerate((press_ref, cond_ref))
    ]
    put_faces(me, out_ref, 256, *faces_of(jnp.concatenate(wide, axis=0)))
    for i, value in enumerate((tnext, inverse, partial, fm, mf, owner.astype(f32), rank.astype(f32))):
        seg_ref[i] = value


def cells_kernel(
    me_ref, well_tile_ref, well_cell_ref, well_rate_ref,
    got_ref, press_ref, cond_ref, accum_ref, left_ref, right_ref,
    out_ref, cells_ref, field_ref, index_ref, edge_ref, res_ref,
):
    me = me_ref[0]
    slots = load_slots(got_ref, 256)
    press, cond, accum = (
        jnp.concatenate([left_ref[i], ref[...], right_ref[i]], axis=1)
        for i, ref in enumerate((press_ref, cond_ref, accum_ref))
    )
    sums = []
    for side in range(3):
        table = slots[side * 64 : side * 64 + 64]
        index = table[:CAP].astype(i32) - 1
        index_ref[side * CAP : side * CAP + CAP] = index
        columns, mask = cell_hot(as_row(index))
        sums.append(scatter([table[16:32], table[32:48], table[48:64]], columns, mask))
        if side == 1:
            own_columns, own_mask = columns, mask
    flow, first, weight = (jnp.concatenate([sums[side][i] for side in range(3)], axis=1) for i in range(3))

    halos = columns_of(*read_faces(me, got_ref, 256, 2 * LAYERS * EXT))
    press_halo = halos[: LAYERS * EXT].reshape(LAYERS, EXT, 128)
    cond_halo = halos[LAYERS * EXT :].reshape(LAYERS, EXT, 128)
    lane = iota((LAYERS, EXT, 128), 2)
    tx = harmonic(cond, up_x(cond))
    ty = harmonic(cond, up_y(cond, cond_halo))
    tz = 0.5 * harmonic(cond, up_z(cond))
    ty_first = jnp.where(lane == 0, harmonic(cond, cond_halo), 0.0)
    diag = accum + tx + down_x(tx) + ty + down_y(ty, ty_first) + tz + down_z(tz)
    inverse = jnp.where(diag > 0.0, 1.0 / jnp.where(diag > 0.0, diag, 1.0), 0.0)

    x0 = ((me >> 4) - 1) * 8
    y0 = (me & 15) * 128
    plane_x = iota((EXT, 128), 0) + x0
    plane_y = iota((EXT, 128), 1) + y0
    source = jnp.zeros((EXT, 128), f32)
    for w in range(well_tile_ref.shape[0]):
        tile = well_tile_ref[w]
        cell = well_cell_ref[w]
        at = (plane_x == (tile >> 4) * 8 + (cell >> 7)) & (plane_y == (tile & 15) * 128 + (cell & 127))
        source = source + jnp.where(at, well_rate_ref[w], 0.0)

    res = diag * press - stencil(tx, ty, tz, ty_first, press, press_halo) - flow - source[None]
    field = inverse * res
    for i, value in enumerate((tx, ty, tz, ty_first, inverse, res, first - weight * press)):
        cells_ref[i] = value
    field_ref[...] = field
    res_ref[...] = res[:, 8:16]
    before = got_ref[jnp.maximum(me - 1, 0), :, 128:256]
    edge_ref[...] = jnp.broadcast_to(jnp.where(me > 0, before, -1.0), (8, 128))

    taken = gather([press_ref[...], field[:, 8:16]], own_columns, own_mask)
    store_slots(out_ref, jnp.concatenate(taken + [spread(taken[0], 1), jnp.zeros((80, 128), f32)], axis=0))
    put_faces(me, out_ref, 128, *faces_of(field.reshape(LAYERS * EXT, 128)))


def edge_in(row, k, i):
    at = 64 + 4 * k + i
    return row[:, at : at + 1]


def step_kernel(
    first, final,
    me_ref, delta_ref, from_ref, to_ref, trans_ref,
    got_ref, cells_ref, field_ref, index_ref, edge_ref, seg_ref, *rest,
):
    me = me_ref[0]
    if not first:
        frac_ref, resf_ref, *rest = rest
    slots = load_slots(got_ref, 128)
    code = seg_code()
    code_f = code.astype(f32)
    tnext, inverse_f, partial, fm, mf, owner, rank = (seg_ref[i] for i in range(7))
    hot = owner_hot(as_row(owner.astype(i32)))
    mask = rank_mask(as_row(rank.astype(i32)))
    edge = edge_ref[0:1]

    if first:
        resf = partial - fm * from_slots(slots[0:16], hot, mask)
        frac = inverse_f * resf
        here = from_slots(slots[16:32], hot, mask)
    else:
        resf = resf_ref[...]
        frac = frac_ref[...]
        here = from_slots(slots[0:16], hot, mask)
    gain = resf + chain(tnext, frac) + mf * here
    for b in range(4):
        target, _ = edge_codes(delta_ref, to_ref, b)
        at = code == b * 256 + from_ref[b]
        term = trans_ref[b] * total(jnp.where(at, frac, 0.0))
        gain = gain + jnp.where(code == target, term, 0.0)
        if first:
            place = (iota((CAP, 128), 1) * CAP + iota((CAP, 128), 0)).astype(f32)
            there = total(jnp.where(place == edge_in(edge, b, 1), slots[32:48], 0.0))
            term = edge_in(edge, b, 2) - edge_in(edge, b, 3) * there
        else:
            term = got_ref[jnp.maximum(me - 1, 0), :, 64 + b : 65 + b]
        gain = gain + jnp.where(code_f == edge_in(edge, b, 0), term, 0.0)
    frac = inverse_f * gain

    tx, ty, tz, ty_first, inverse, res = (cells_ref[i] for i in range(6))
    field = field_ref[...]
    if first:
        flow = cells_ref[6]
        own_columns, own_mask = cell_hot(as_row(index_ref[CAP : 2 * CAP]))
    else:
        flow = []
        for side in range(3):
            columns, rows = cell_hot(as_row(index_ref[side * CAP : side * CAP + CAP]))
            flow.extend(scatter([slots[16 + side * CAP : 32 + side * CAP]], columns, rows))
            if side == 1:
                own_columns, own_mask = columns, rows
        flow = jnp.concatenate(flow, axis=1)
    halo = columns_of(*read_faces(me, got_ref, 128, LAYERS * EXT)).reshape(LAYERS, EXT, 128)
    field = inverse * (res + stencil(tx, ty, tz, ty_first, field, halo) + flow)

    if final:
        adj_matrix_ref, adj_fracture_ref = rest
        adj_matrix_ref[...] = field[:, 8:16]
        adj_fracture_ref[...] = unfold(frac)
        return
    out_ref, new_field_ref, new_frac_ref = rest[:3]
    if first:
        resf_out_ref, res_fracture_ref = rest[3:]
        resf_out_ref[...] = resf
        res_fracture_ref[...] = unfold(resf)
    new_field_ref[...] = field
    new_frac_ref[...] = frac
    taken = gather([field[:, 8:16]], own_columns, own_mask)
    terms = to_slots([fm * frac], hot, mask)
    edges = []
    for b in range(4):
        at = code == b * 256 + from_ref[b]
        edges.append(jnp.broadcast_to(trans_ref[b] * total(jnp.where(at, frac, 0.0)), (1, 128)))
    rows = taken + [spread(terms, 16), terms, spread(terms, -16)] + edges + [jnp.zeros((60, 128), f32)]
    store_slots(out_ref, jnp.concatenate(rows, axis=0))
    put_faces(me, out_ref, 128, *faces_of(field.reshape(LAYERS * EXT, 128)))


def call(kernel, name, scalars, arrays, outs):
    spec = [pl.BlockSpec(memory_space=pltpu.SMEM)] * len(scalars)
    spec += [pl.BlockSpec(memory_space=pltpu.VMEM)] * len(arrays)
    return pl.pallas_call(
        kernel,
        name=name,
        out_shape=[jax.ShapeDtypeStruct(shape, kind) for shape, kind in outs],
        in_specs=spec,
        out_specs=[pl.BlockSpec(memory_space=pltpu.VMEM)] * len(outs),
        compiler_params=pltpu.CompilerParams(vmem_limit_bytes=48 * 1024 * 1024),
    )(*scalars, *arrays)


def exchange(message):
    return lax.all_to_all(message, ALL, split_axis=0, concat_axis=0, tiled=True)


def passed(block, axis, distance):
    count = lax.axis_size(axis)
    return lax.ppermute(block, axis, [(i - distance, i) for i in range(count) if 0 <= i - distance < count])


def body(
    press_matrix, cond_matrix, accum_matrix, press_frac, accum_frac, trans_chain, couple_mf, couple_fm,
    conn_tile, conn_layer, conn_cell, inter_delta, inter_from, inter_to, inter_trans, well_tile, well_cell, well_rate,
):
    me = lax.axis_index(ALL).astype(i32).reshape(1)
    stacked = jnp.stack([press_matrix, cond_matrix, accum_matrix])
    left = passed(stacked, "gx", 1)
    right = passed(stacked, "gx", -1)
    follow = passed(press_frac, ALL, -1)
    edges = (inter_delta, inter_from, inter_to, inter_trans)
    wide = (LAYERS, EXT, 128)
    tile = (LAYERS, 8, 128)
    seg = (8, 128)

    message, segs = call(
        begin_kernel,
        "begin",
        (me, *edges),
        (press_matrix, cond_matrix, left, right, press_frac, follow, accum_frac, trans_chain, couple_mf, couple_fm,
         conn_tile, conn_layer, conn_cell),
        [((TILES, 1, 640), f32), ((7, *seg), f32)],
    )
    got = exchange(message)
    message, cells, field, index, edge, res_matrix = call(
        cells_kernel,
        "cells",
        (me, well_tile, well_cell, well_rate),
        (got, press_matrix, cond_matrix, accum_matrix, left, right),
        [((TILES, 1, 384), f32), ((7, *wide), f32), (wide, f32), ((48, 128), i32), (seg, f32), (tile, f32)],
    )
    got = exchange(message)

    def step(first, final, got, field, more, outs):
        def kernel(*refs):
            step_kernel(first, final, *refs)

        return call(kernel, "step", (me, *edges), (got, cells, field, index, edge, segs, *more), outs)

    going = [((TILES, 1, 384), f32), (wide, f32), (seg, f32)]
    message, field, frac, resf, res_fracture = step(
        True, False, got, field, (), going + [(seg, f32), ((4, 256), f32)]
    )
    for _ in range(ITERS - 3):
        got = exchange(message)
        message, field, frac = step(False, False, got, field, (frac, resf), going)
    got = exchange(message)
    adj_matrix, adj_fracture = step(False, True, got, field, (frac, resf), [(tile, f32), ((4, 256), f32)])
    return res_matrix, res_fracture, adj_matrix, adj_fracture


def solution(mesh):
    cells = P(None, "gx", YA)
    segs = P(ALL, None)
    blocks = P(ALL)
    in_specs = (cells,) * 3 + (segs,) * 8 + (blocks,) * 4 + (P(),) * 3
    return jax.shard_map(body, mesh=mesh, in_specs=in_specs, out_specs=(cells, segs, cells, segs), check_vma=False)
```

```python
import jax
import jax.numpy as jnp
from jax import lax
from jax.experimental import pallas as pl
from jax.experimental.pallas import tpu as pltpu
from jax.sharding import PartitionSpec as P

ITERS = 8
CAP = 16
TILES = 128
ROWS = 64
EXT = 24
LAYERS = 8
SLOTS = CAP * TILES
ALL = ("gx", "gy", "af")
YA = ("gy", "af")
f32 = jnp.float32
bf16 = jnp.bfloat16
i32 = jnp.int32


def iota(shape, axis):
    return lax.broadcasted_iota(i32, shape, axis)


def parts(value):
    high = value.astype(bf16)
    return high, (value - high.astype(f32)).astype(bf16)


def dot_nn(a, b):
    return lax.dot_general(a, b, (((1,), (0,)), ((), ())), preferred_element_type=f32)


def dot_nt(a, b):
    return lax.dot_general(a, b, (((1,), (1,)), ((), ())), preferred_element_type=f32)


def dot_tn(a, b):
    return lax.dot_general(a, b, (((0,), (0,)), ((), ())), preferred_element_type=f32)


def as_row(rows):
    return jnp.concatenate([rows[i : i + 1] for i in range(rows.shape[0])], axis=1)


def as_rows(row):
    return jnp.concatenate([row[:, i : i + 128] for i in range(0, row.shape[1], 128)], axis=0)


def total(value):
    return jnp.sum(jnp.sum(value, axis=1, keepdims=True), axis=0, keepdims=True)


def fold(value):
    return jnp.concatenate([value[:, :128], value[:, 128:]], axis=0)


def unfold(value):
    return jnp.concatenate([value[:4], value[4:]], axis=1)


def seg_code():
    row = iota((8, 128), 0)
    return (row % 4) * 256 + (row // 4) * 128 + iota((8, 128), 1)


def chain(tnext, field):
    lane = iota((8, 128), 1)
    ahead = pltpu.roll(field, 127, 1)
    ahead = jnp.where(lane == 127, pltpu.roll(ahead, 4, 0), ahead)
    behind = pltpu.roll(tnext * field, 1, 1)
    behind = jnp.where(lane == 0, pltpu.roll(behind, 4, 0), behind)
    return tnext * ahead + behind


def owner_hot(owner_row):
    return (iota((TILES, 1024), 0) == owner_row).astype(bf16)


def rank_mask(rank_row):
    return iota((CAP, 1024), 0) == rank_row


def to_slots(values, hot, mask):
    halves = ([], [])
    for value in values:
        row = as_row(value)
        for half, part in zip(halves, parts(row)):
            half.append(jnp.where(mask, part.astype(f32), 0.0).astype(bf16))
    both = jnp.concatenate([jnp.concatenate(half, axis=0) for half in halves], axis=1)
    return dot_nt(both, jnp.concatenate([hot, hot], axis=1))


def from_slots(table, hot, mask):
    high, low = parts(table)
    rows = dot_nn(jnp.concatenate([high, low], axis=1), jnp.concatenate([hot, hot], axis=0))
    return as_rows(jnp.sum(jnp.where(mask, rows, 0.0), axis=0, keepdims=True))


def cell_hot(index_row):
    count = index_row.shape[1]
    columns = (iota((128, count), 0) == (index_row & 127)).astype(bf16)
    return columns, iota((ROWS, count), 0) == (index_row >> 7)


def scatter(tables, columns, mask):
    stacked = []
    for table in tables:
        for part in parts(as_row(table)):
            stacked.append(jnp.where(mask, part.astype(f32), 0.0).astype(bf16))
    sums = dot_nt(jnp.concatenate(stacked, axis=0), columns)
    return [
        (sums[2 * i * ROWS : (2 * i + 1) * ROWS] + sums[(2 * i + 1) * ROWS : (2 * i + 2) * ROWS]).reshape(LAYERS, 8, 128)
        for i in range(len(tables))
    ]


def gather(fields, columns, mask):
    stacked = []
    for field in fields:
        stacked.extend(parts(field.reshape(ROWS, 128)))
    rows = dot_nn(jnp.concatenate(stacked, axis=0), columns)
    out = []
    for i in range(len(fields)):
        both = rows[2 * i * ROWS : (2 * i + 1) * ROWS] + rows[(2 * i + 1) * ROWS : (2 * i + 2) * ROWS]
        out.append(as_rows(jnp.sum(jnp.where(mask, both, 0.0), axis=0, keepdims=True)))
    return out


def faces_of(field):
    rows = iota((16, 128), 0)
    lanes = iota((16, 128), 1)
    pick = (((rows == 0) & (lanes == 0)) | ((rows == 1) & (lanes == 127))).astype(bf16)
    both = dot_nt(jnp.concatenate([pick, pick], axis=1), jnp.concatenate(parts(field), axis=1))
    return both[0:1], both[1:2]


def columns_of(left, right):
    width = left.shape[1]
    held = [part.astype(f32) for row in (left, right) for part in parts(row)]
    held = jnp.concatenate(held + [jnp.zeros((12, width), f32)], axis=0).astype(bf16)
    rows = iota((16, 128), 0)
    lanes = iota((16, 128), 1)
    place = (((rows < 2) & (lanes == 0)) | ((rows >= 2) & (rows < 4) & (lanes == 127))).astype(bf16)
    return dot_tn(held, place)


def up_x(v):
    return jnp.concatenate([v[:, 1:], jnp.zeros_like(v[:, :1])], axis=1)


def down_x(v):
    return jnp.concatenate([jnp.zeros_like(v[:, :1]), v[:, :-1]], axis=1)


def up_z(v):
    return jnp.concatenate([v[1:], jnp.zeros_like(v[:1])], axis=0)


def down_z(v):
    return jnp.concatenate([jnp.zeros_like(v[:1]), v[:-1]], axis=0)


def up_y(v, halo):
    return jnp.where(iota(v.shape, 2) == 127, halo, pltpu.roll(v, 127, 2))


def down_y(v, first):
    return jnp.where(iota(v.shape, 2) == 0, first, pltpu.roll(v, 1, 2))


def stencil(tx, ty, tz, ty_first, field, halo):
    out = tx * up_x(field) + down_x(tx * field)
    out = out + ty * up_y(field, halo) + down_y(ty * field, ty_first * halo)
    return out + tz * up_z(field) + down_z(tz * field)


def harmonic(first, second):
    both = first + second
    return jnp.where(both > 0.0, 2.0 * first * second / jnp.where(both > 0.0, both, 1.0), 0.0)


def read_faces(me, got_ref, start, width, across=0):
    along = me & 15
    line = (me >> 4) + across // 16
    inside = (line >= 0) & (line < 8)
    before = got_ref[jnp.clip(me + across - 1, 0, TILES - 1), :, start : start + width]
    after = got_ref[jnp.clip(me + across + 1, 0, TILES - 1), :, start : start + width]
    return jnp.where(inside & (along > 0), before, 0.0), jnp.where(inside & (along < 15), after, 0.0)


def put_faces(me, out_ref, start, first, last, across=0):
    width = first.shape[1]
    for at, face in ((me + across - 1, first), (me + across + 1, last)):
        out_ref[jnp.where((at >= 0) & (at < TILES), at, me), :, start : start + width] = face


def edge_codes(delta_ref, to_ref, b):
    block = b + delta_ref[b]
    code = block * 256 + to_ref[b]
    return jnp.where(block < 4, code, -1), jnp.where(block >= 4, code - 1024, -1)


def spread(rows, shift):
    lane = iota(rows.shape, 1)
    inside = (lane >= shift) if shift > 0 else (lane < TILES + shift)
    return jnp.where(inside, pltpu.roll(rows, shift % TILES, 1), 0.0)


def store_slots(out_ref, rows):
    for i in range(0, rows.shape[0], 128):
        part = rows[i : i + 128].T
        out_ref[:, 0, i : i + part.shape[1]] = part


def load_slots(got_ref, count):
    return jnp.concatenate([got_ref[:, 0, i : i + 128].T for i in range(0, count, 128)], axis=0)


def begin_kernel(me_ref, delta_ref, from_ref, to_ref, trans_ref, *refs):
    given, (out_ref, seg_ref), held, sems = refs[:10], refs[10:12], refs[12:22], refs[22]
    copies = [pltpu.make_async_copy(a, b, sems.at[i]) for i, (a, b) in enumerate(zip(given, held))]
    for copy in copies:
        copy.start()
    for copy in copies:
        copy.wait()
    tile_ref, layer_ref, cell_ref, press_frac_ref, accum_ref, chain_ref, mf_ref, fm_ref, press_ref, cond_ref = held
    me = me_ref[0]
    code = seg_code()
    owner = fold(tile_ref[...])
    owner_row = as_row(owner)
    hot = owner_hot(owner_row)
    before = (iota((128, 128), 0) < iota((128, 128), 1)).astype(bf16)
    base = jnp.zeros((TILES, 1), f32)
    ranks = []
    for c in range(8):
        part = hot[:, c * 128 : (c + 1) * 128]
        wide = part.astype(f32)
        count = dot_nn(part, before) + base
        ranks.append(jnp.sum(wide * count, axis=0, keepdims=True))
        base = base + jnp.sum(wide, axis=1, keepdims=True)
    rank_row = jnp.concatenate(ranks, axis=1).astype(i32)
    rank = as_rows(rank_row)
    mask = rank_mask(rank_row)

    press = fold(press_frac_ref[...])
    fm = fold(fm_ref[...])
    mf = fold(mf_ref[...])
    last = code % 256 == 255
    tnext = jnp.where(last, 0.0, fold(chain_ref[...]))
    tprev = pltpu.roll(tnext, 1, 1)
    tprev = jnp.where(iota((8, 128), 1) == 0, pltpu.roll(tprev, 4, 0), tprev)
    diag = fold(accum_ref[...]) + tnext + tprev + fm
    inverse = 1.0 / diag
    partial = diag * press - chain(tnext, press)
    for b in range(4):
        here, _ = edge_codes(delta_ref, to_ref, b)
        at = code == b * 256 + from_ref[b]
        partial = partial - jnp.where(at, trans_ref[b] * total(jnp.where(code == here, press, 0.0)), 0.0)
    where_cell = (fold(layer_ref[...]) * 1024 + fold(cell_ref[...]) + 1).astype(f32)
    slots = to_slots([where_cell, mf * press, fm * inverse * fm], hot, mask)
    place = (owner * CAP + rank).astype(f32)
    edges = []
    for b in range(4):
        _, there = edge_codes(delta_ref, to_ref, b)
        at = code == b * 256 + from_ref[b]
        gain = trans_ref[b] * inverse
        edges.append(jnp.full((1, 128), there.astype(f32)))
        for value in (place, where_cell, gain * fm, gain * partial, gain * trans_ref[b]):
            edges.append(jnp.broadcast_to(total(jnp.where(at, value, 0.0)), (1, 128)))
        edges.append(jnp.full((1, 128), trans_ref[b]))
        edges.append(jnp.zeros((1, 128), f32))
    rows = [spread(slots, 16), slots, spread(slots, -16)] + edges + [jnp.zeros((80, 128), f32)]
    store_slots(out_ref, jnp.concatenate(rows, axis=0))
    first_face, last_face = faces_of(jnp.concatenate([press_ref[...].reshape(ROWS, 128), cond_ref[...].reshape(ROWS, 128)], axis=0))
    for across in (-16, 0, 16):
        put_faces(me, out_ref, 256, first_face, last_face, across)
    for i, value in enumerate((tnext, inverse, partial, fm, mf, owner.astype(f32), rank.astype(f32), press)):
        seg_ref[i] = value


def edge_in(row, k, i):
    at = 16 + 8 * k + i
    return row[:, at : at + 1]


def cells_kernel(
    me_ref, well_tile_ref, well_cell_ref, well_rate_ref,
    got_ref, press_ref, cond_ref, accum_ref, left_ref, right_ref, seg_ref,
    out_ref, cells_ref, field_ref, index_ref, edge_ref, res_ref,
):
    me = me_ref[0]
    slots = load_slots(got_ref, 256)
    press, cond, accum = (
        jnp.concatenate([left_ref[i], ref[...], right_ref[i]], axis=1)
        for i, ref in enumerate((press_ref, cond_ref, accum_ref))
    )
    sums = []
    for side in range(3):
        table = slots[side * 48 : side * 48 + 48]
        index = table[:CAP].astype(i32) - 1
        index_ref[side * CAP : side * CAP + CAP] = index
        columns, mask = cell_hot(as_row(index))
        sums.append(scatter([table[16:32], table[32:48]], columns, mask))
        if side == 1:
            own_columns, own_mask = columns, mask
    flow, weight = (jnp.concatenate([sums[side][i] for side in range(3)], axis=1) for i in range(2))

    halos = [columns_of(*read_faces(me, got_ref, 256, 2 * ROWS, across)) for across in (-16, 0, 16)]
    press_halo = jnp.concatenate([halo[:ROWS].reshape(LAYERS, 8, 128) for halo in halos], axis=1)
    cond_halo = jnp.concatenate([halo[ROWS:].reshape(LAYERS, 8, 128) for halo in halos], axis=1)
    lane = iota((LAYERS, EXT, 128), 2)
    tx = harmonic(cond, up_x(cond))
    ty = harmonic(cond, up_y(cond, cond_halo))
    tz = 0.5 * harmonic(cond, up_z(cond))
    ty_first = jnp.where(lane == 0, harmonic(cond, cond_halo), 0.0)
    diag = accum + tx + down_x(tx) + ty + down_y(ty, ty_first) + tz + down_z(tz)
    inverse = jnp.where(diag > 0.0, 1.0 / jnp.where(diag > 0.0, diag, 1.0), 0.0)

    x0 = ((me >> 4) - 1) * 8
    y0 = (me & 15) * 128
    plane_x = iota((EXT, 128), 0) + x0
    plane_y = iota((EXT, 128), 1) + y0
    source = jnp.zeros((EXT, 128), f32)
    for w in range(well_tile_ref.shape[0]):
        tile = well_tile_ref[w]
        cell = well_cell_ref[w]
        at = (plane_x == (tile >> 4) * 8 + (cell >> 7)) & (plane_y == (tile & 15) * 128 + (cell & 127))
        source = source + jnp.where(at, well_rate_ref[w], 0.0)

    res = diag * press - stencil(tx, ty, tz, ty_first, press, press_halo) - flow - source[None]
    field = inverse * res
    for i, value in enumerate((tx, ty, tz, ty_first, inverse, res, weight * press)):
        cells_ref[i] = value
    field_ref[...] = field
    res_ref[...] = res[:, 8:16]

    code = seg_code().astype(f32)
    _, inverse_f, partial, fm, _, owner, rank, press_f = (seg_ref[i] for i in range(8))
    edge = jnp.where(me > 0, got_ref[jnp.maximum(me - 1, 0), :, 128:256], -1.0)
    lane = iota((1, 128), 1)
    cells, terms, picks = [], [], []
    for k in range(4):
        there = edge_in(edge, k, 0)
        picked = total(jnp.where(code == there, press_f, 0.0))
        at = (lane == (edge_in(edge, k, 1).astype(i32) >> 4)) & (there >= 0.0)
        cells.append(jnp.where(at, edge_in(edge, k, 2), 0.0))
        terms.append(jnp.where(at, -edge_in(edge, k, 3) * picked, 0.0))
        picks.append(jnp.broadcast_to(picked, (1, 128)))
        edge = jnp.where(lane == 16 + 8 * k + 4, edge - edge_in(edge, k, 5) * picked, edge)
    edge_ref[...] = jnp.broadcast_to(edge, (8, 128))
    late = jnp.concatenate(cells + terms, axis=0)
    hot = owner_hot(as_row(owner.astype(i32)))
    first = to_slots([fm * inverse_f * partial], hot, rank_mask(as_row(rank.astype(i32))))

    taken = gather([press_ref[...], field[:, 8:16]], own_columns, own_mask)
    rows = taken + [spread(taken[0], 1)]
    rows += [spread(first, 16), first, spread(first, -16), spread(late, 16), late, spread(late, -16)]
    store_slots(out_ref, jnp.concatenate(rows + picks + [jnp.zeros((4, 128), f32)], axis=0))
    put_faces(me, out_ref, 128, *faces_of(field.reshape(LAYERS * EXT, 128)))


def step_kernel(
    first, final,
    me_ref, delta_ref, from_ref, to_ref, trans_ref,
    got_ref, cells_ref, field_ref, index_ref, seg_ref, edge_ref, *rest,
):
    me = me_ref[0]
    if not first:
        frac_ref, resf_ref, *rest = rest
    slots = load_slots(got_ref, 128)
    code = seg_code()
    code_f = code.astype(f32)
    tnext, inverse_f, partial, fm, mf, owner, rank = (seg_ref[i] for i in range(7))
    hot = owner_hot(as_row(owner.astype(i32)))
    mask = rank_mask(as_row(rank.astype(i32)))
    edge = edge_ref[0:1]

    if first:
        resf = partial - fm * from_slots(slots[0:16], hot, mask)
        after = got_ref[jnp.minimum(me + 1, TILES - 1), :, 0:128]
        for b in range(4):
            _, there = edge_codes(delta_ref, to_ref, b)
            at = (code == b * 256 + from_ref[b]) & (there >= 0)
            resf = resf - jnp.where(at, trans_ref[b] * after[:, 120 + b : 121 + b], 0.0)
        frac = inverse_f * resf
        here = from_slots(slots[16:32], hot, mask)
    else:
        resf = resf_ref[...]
        frac = frac_ref[...]
        here = from_slots(slots[0:16], hot, mask)
    gain = resf + chain(tnext, frac) + mf * here
    before = got_ref[jnp.maximum(me - 1, 0), :, 64:256]
    for b in range(4):
        target, _ = edge_codes(delta_ref, to_ref, b)
        at = code == b * 256 + from_ref[b]
        term = trans_ref[b] * total(jnp.where(at, frac, 0.0))
        gain = gain + jnp.where(code == target, term, 0.0)
        if first:
            place = (iota((CAP, 128), 1) * CAP + iota((CAP, 128), 0)).astype(f32)
            there = total(jnp.where(place == edge_in(edge, b, 1), slots[32:48], 0.0))
            term = edge_in(edge, b, 4) - edge_in(edge, b, 3) * there
        else:
            term = before[:, EXT * b : EXT * b + 1]
        gain = gain + jnp.where(code_f == edge_in(edge, b, 0), term, 0.0)
    frac = inverse_f * gain

    tx, ty, tz, ty_first, inverse, res = (cells_ref[i] for i in range(6))
    field = field_ref[...]
    flow = []
    for side in range(3):
        index = index_ref[side * CAP : side * CAP + CAP]
        if first:
            late = slots[96 + 8 * side : 104 + 8 * side]
            index = jnp.concatenate([index, late[:4].astype(i32) - 1], axis=0)
            table = jnp.concatenate([slots[48 + side * CAP : 64 + side * CAP], late[4:]], axis=0)
        else:
            table = slots[16 + side * CAP : 32 + side * CAP]
        columns, rows = cell_hot(as_row(index))
        flow.extend(scatter([table], columns, rows))
        if side == 1:
            own_columns, own_mask = columns[:, :SLOTS], rows[:, :SLOTS]
    flow = jnp.concatenate(flow, axis=1)
    if first:
        flow = flow - cells_ref[6]
    halo = columns_of(*read_faces(me, got_ref, 128 if first else 64, LAYERS * EXT)).reshape(LAYERS, EXT, 128)
    field = inverse * (res + stencil(tx, ty, tz, ty_first, field, halo) + flow)

    if final:
        adj_matrix_ref, adj_fracture_ref = rest
        adj_matrix_ref[...] = field[:, 8:16]
        adj_fracture_ref[...] = unfold(frac)
        return
    out_ref, new_field_ref, new_frac_ref = rest[:3]
    if first:
        resf_out_ref, res_fracture_ref = rest[3:]
        resf_out_ref[...] = resf
        res_fracture_ref[...] = unfold(resf)
    new_field_ref[...] = field
    new_frac_ref[...] = frac
    taken = gather([field[:, 8:16]], own_columns, own_mask)
    terms = to_slots([fm * frac], hot, mask)
    store_slots(out_ref, jnp.concatenate(taken + [spread(terms, 16), terms, spread(terms, -16)], axis=0))
    begin, end = faces_of(field.reshape(LAYERS * EXT, 128))
    lane = iota(end.shape, 1)
    for b in range(4):
        at = code == b * 256 + from_ref[b]
        end = jnp.where(lane == EXT * b, trans_ref[b] * total(jnp.where(at, frac, 0.0)), end)
    put_faces(me, out_ref, 64, begin, end)


def call(kernel, name, scalars, arrays, outs, space=pltpu.VMEM, scratch=(), limit=48 * 1024 * 1024):
    spec = [pl.BlockSpec(memory_space=pltpu.SMEM)] * len(scalars)
    spec += [pl.BlockSpec(memory_space=space)] * len(arrays)
    return pl.pallas_call(
        kernel,
        name=name,
        out_shape=[jax.ShapeDtypeStruct(shape, kind) for shape, kind in outs],
        in_specs=spec,
        out_specs=[pl.BlockSpec(memory_space=pltpu.VMEM)] * len(outs),
        scratch_shapes=list(scratch),
        compiler_params=pltpu.CompilerParams(vmem_limit_bytes=limit),
    )(*scalars, *arrays)


def exchange(message):
    return lax.all_to_all(message, ALL, split_axis=0, concat_axis=0, tiled=True)


def passed(block, axis, distance):
    count = lax.axis_size(axis)
    return lax.ppermute(block, axis, [(i - distance, i) for i in range(count) if 0 <= i - distance < count])


def body(
    press_matrix, cond_matrix, accum_matrix, press_frac, accum_frac, trans_chain, couple_mf, couple_fm,
    conn_tile, conn_layer, conn_cell, inter_delta, inter_from, inter_to, inter_trans, well_tile, well_cell, well_rate,
):
    me = lax.axis_index(ALL).astype(i32).reshape(1)
    stacked = jnp.stack([press_matrix, cond_matrix, accum_matrix])
    left = passed(stacked, "gx", 1)
    right = passed(stacked, "gx", -1)
    edges = (inter_delta, inter_from, inter_to, inter_trans)
    wide = (LAYERS, EXT, 128)
    tile = (LAYERS, 8, 128)
    seg = (8, 128)

    given = (conn_tile, conn_layer, conn_cell, press_frac, accum_frac, trans_chain, couple_mf, couple_fm, press_matrix, cond_matrix)
    message, segs = call(
        begin_kernel,
        "begin",
        (me, *edges),
        given,
        [((TILES, 1, 384), f32), ((8, *seg), f32)],
        pl.ANY,
        [pltpu.VMEM(a.shape, a.dtype) for a in given] + [pltpu.SemaphoreType.DMA((len(given),))],
        64 * 1024 * 1024,
    )
    got = exchange(message)
    message, cells, field, index, edge, res_matrix = call(
        cells_kernel,
        "cells",
        (me, well_tile, well_cell, well_rate),
        (got, press_matrix, cond_matrix, accum_matrix, left, right, segs),
        [((TILES, 1, 384), f32), ((7, *wide), f32), (wide, f32), ((48, 128), i32), (seg, f32), (tile, f32)],
    )
    got = exchange(message)

    def step(first, final, got, field, more, outs):
        def kernel(*refs):
            step_kernel(first, final, *refs)

        return call(kernel, "step", (me, *edges), (got, cells, field, index, segs, edge, *more), outs)

    going = [((TILES, 1, 256), f32), (wide, f32), (seg, f32)]
    message, field, frac, resf, res_fracture = step(
        True, False, got, field, (), going + [(seg, f32), ((4, 256), f32)]
    )
    for _ in range(ITERS - 3):
        got = exchange(message)
        message, field, frac = step(False, False, got, field, (frac, resf), going)
    got = exchange(message)
    adj_matrix, adj_fracture = step(False, True, got, field, (frac, resf), [(tile, f32), ((4, 256), f32)])
    return res_matrix, res_fracture, adj_matrix, adj_fracture


def solution(mesh):
    cells = P(None, "gx", YA)
    segs = P(ALL, None)
    blocks = P(ALL)
    in_specs = (cells,) * 3 + (segs,) * 8 + (blocks,) * 4 + (P(),) * 3
    return jax.shard_map(body, mesh=mesh, in_specs=in_specs, out_specs=(cells, segs, cells, segs), check_vma=False)
```

```python
import jax
import jax.numpy as jnp
from jax import lax
from jax.experimental import pallas as pl
from jax.experimental.pallas import tpu as pltpu
from jax.sharding import PartitionSpec as P

ITERS = 8
CAP = 16
TILES = 128
ROWS = 64
EXT = 24
LAYERS = 8
SLOTS = CAP * TILES
ALL = ("gx", "gy", "af")
YA = ("gy", "af")
f32 = jnp.float32
bf16 = jnp.bfloat16
i32 = jnp.int32


def iota(shape, axis):
    return lax.broadcasted_iota(i32, shape, axis)


def parts(value):
    high = value.astype(bf16)
    return high, (value - high.astype(f32)).astype(bf16)


def dot_nn(a, b):
    return lax.dot_general(a, b, (((1,), (0,)), ((), ())), preferred_element_type=f32)


def dot_nt(a, b):
    return lax.dot_general(a, b, (((1,), (1,)), ((), ())), preferred_element_type=f32)


def dot_tn(a, b):
    return lax.dot_general(a, b, (((0,), (0,)), ((), ())), preferred_element_type=f32)


def as_row(rows):
    return jnp.concatenate([rows[i : i + 1] for i in range(rows.shape[0])], axis=1)


def as_rows(row):
    return jnp.concatenate([row[:, i : i + 128] for i in range(0, row.shape[1], 128)], axis=0)


def total(value):
    return jnp.sum(jnp.sum(value, axis=1, keepdims=True), axis=0, keepdims=True)


def fold(value):
    return jnp.concatenate([value[:, :128], value[:, 128:]], axis=0)


def unfold(value):
    return jnp.concatenate([value[:4], value[4:]], axis=1)


def seg_code():
    row = iota((8, 128), 0)
    return (row % 4) * 256 + (row // 4) * 128 + iota((8, 128), 1)


def chain(tnext, field):
    lane = iota((8, 128), 1)
    ahead = pltpu.roll(field, 127, 1)
    ahead = jnp.where(lane == 127, pltpu.roll(ahead, 4, 0), ahead)
    behind = pltpu.roll(tnext * field, 1, 1)
    behind = jnp.where(lane == 0, pltpu.roll(behind, 4, 0), behind)
    return tnext * ahead + behind


def owner_hot(owner_row):
    return (iota((TILES, 1024), 0) == owner_row).astype(bf16)


def rank_mask(rank_row):
    return iota((CAP, 1024), 0) == rank_row


def to_slots(values, hot, mask):
    halves = ([], [])
    for value in values:
        row = as_row(value)
        for half, part in zip(halves, parts(row)):
            half.append(jnp.where(mask, part.astype(f32), 0.0).astype(bf16))
    both = jnp.concatenate([jnp.concatenate(half, axis=0) for half in halves], axis=1)
    return dot_nt(both, jnp.concatenate([hot, hot], axis=1))


def look_up(table, row, lane):
    out = jnp.zeros(row.shape, f32)
    for r in range(table.shape[0]):
        picked = jnp.take_along_axis(jnp.broadcast_to(table[r : r + 1], row.shape), lane, axis=1, mode="promise_in_bounds")
        out = jnp.where(row == r, picked, out)
    return out


def find(table, index):
    return look_up(table, index >> 7, index & 127)


def cell_hot(index_row):
    count = index_row.shape[1]
    columns = iota((128, count), 0) == (index_row & 127)
    rows = iota((ROWS, count), 0) == (index_row >> 7)
    return columns.astype(bf16), rows.astype(bf16)


def scatter(tables, columns, rows):
    stacked = []
    for table in tables:
        for part in parts(table):
            row = as_row(part.astype(f32))
            tall = jnp.broadcast_to(row, (16, row.shape[1])).astype(bf16)
            stacked.append(rows * jnp.concatenate([tall] * (ROWS // 16), axis=0))
    sums = dot_nt(jnp.concatenate(stacked, axis=0), columns)
    return [
        (sums[2 * i * ROWS : (2 * i + 1) * ROWS] + sums[(2 * i + 1) * ROWS : (2 * i + 2) * ROWS]).reshape(LAYERS, 8, 128)
        for i in range(len(tables))
    ]


def faces_of(field):
    rows = iota((16, 128), 0)
    lanes = iota((16, 128), 1)
    pick = (((rows == 0) & (lanes == 0)) | ((rows == 1) & (lanes == 127))).astype(bf16)
    both = dot_nt(jnp.concatenate([pick, pick], axis=1), jnp.concatenate(parts(field), axis=1))
    return both[0:1], both[1:2]


def columns_of(left, right):
    width = left.shape[1]
    held = [part.astype(f32) for row in (left, right) for part in parts(row)]
    held = jnp.concatenate(held + [jnp.zeros((12, width), f32)], axis=0).astype(bf16)
    rows = iota((16, 128), 0)
    lanes = iota((16, 128), 1)
    place = (((rows < 2) & (lanes == 0)) | ((rows >= 2) & (rows < 4) & (lanes == 127))).astype(bf16)
    return dot_tn(held, place)


def up_x(v):
    return jnp.concatenate([v[:, 1:], jnp.zeros_like(v[:, :1])], axis=1)


def down_x(v):
    return jnp.concatenate([jnp.zeros_like(v[:, :1]), v[:, :-1]], axis=1)


def up_z(v):
    return jnp.concatenate([v[1:], jnp.zeros_like(v[:1])], axis=0)


def down_z(v):
    return jnp.concatenate([jnp.zeros_like(v[:1]), v[:-1]], axis=0)


def up_y(v, halo):
    return jnp.where(iota(v.shape, 2) == 127, halo, pltpu.roll(v, 127, 2))


def down_y(v, first):
    return jnp.where(iota(v.shape, 2) == 0, first, pltpu.roll(v, 1, 2))


def stencil(tx, ty, tz, ty_first, field, halo):
    out = tx * up_x(field) + down_x(tx * field)
    out = out + ty * up_y(field, halo) + down_y(ty * field, ty_first * halo)
    return out + tz * up_z(field) + down_z(tz * field)


def harmonic(first, second):
    both = first + second
    return jnp.where(both > 0.0, 2.0 * first * second / jnp.where(both > 0.0, both, 1.0), 0.0)


def read_faces(me, got_ref, start, width, across=0):
    along = me & 15
    line = (me >> 4) + across // 16
    inside = (line >= 0) & (line < 8)
    before = got_ref[jnp.clip(me + across - 1, 0, TILES - 1), :, start : start + width]
    after = got_ref[jnp.clip(me + across + 1, 0, TILES - 1), :, start : start + width]
    return jnp.where(inside & (along > 0), before, 0.0), jnp.where(inside & (along < 15), after, 0.0)


def put_faces(me, out_ref, start, first, last, across=0):
    width = first.shape[1]
    for at, face in ((me + across - 1, first), (me + across + 1, last)):
        out_ref[jnp.where((at >= 0) & (at < TILES), at, me), :, start : start + width] = face


def edge_codes(delta_ref, to_ref, b):
    block = b + delta_ref[b]
    code = block * 256 + to_ref[b]
    return jnp.where(block < 4, code, -1), jnp.where(block >= 4, code - 1024, -1)


def spread(rows, shift):
    lane = iota(rows.shape, 1)
    inside = (lane >= shift) if shift > 0 else (lane < TILES + shift)
    return jnp.where(inside, pltpu.roll(rows, shift % TILES, 1), 0.0)


def store_slots(out_ref, rows):
    for i in range(0, rows.shape[0], 128):
        part = rows[i : i + 128].T
        out_ref[:, 0, i : i + part.shape[1]] = part


def load_slots(got_ref, count):
    return jnp.concatenate([got_ref[:, 0, i : i + 128].T for i in range(0, count, 128)], axis=0)


def begin_kernel(
    me_ref, delta_ref, from_ref, to_ref, trans_ref, well_tile_ref, well_cell_ref, well_rate_ref, *refs
):
    given, (out_ref, seg_ref), held, sems = refs[:10], refs[10:12], refs[12:22], refs[22]
    copies = [pltpu.make_async_copy(a, b, sems.at[i]) for i, (a, b) in enumerate(zip(given, held))]
    for copy in copies:
        copy.start()
    for copy in copies:
        copy.wait()
    tile_ref, layer_ref, cell_ref, press_frac_ref, accum_ref, chain_ref, mf_ref, fm_ref, press_ref, cond_ref = held
    me = me_ref[0]
    code = seg_code()
    owner = fold(tile_ref[...])
    owner_row = as_row(owner)
    hot = owner_hot(owner_row)
    before = (iota((128, 128), 0) < iota((128, 128), 1)).astype(bf16)
    base = jnp.zeros((TILES, 1), f32)
    ranks = []
    for c in range(8):
        part = hot[:, c * 128 : (c + 1) * 128]
        wide = part.astype(f32)
        count = dot_nn(part, before) + base
        ranks.append(jnp.sum(wide * count, axis=0, keepdims=True))
        base = base + jnp.sum(wide, axis=1, keepdims=True)
    rank_row = jnp.concatenate(ranks, axis=1).astype(i32)
    rank = as_rows(rank_row)
    mask = rank_mask(rank_row)

    press = fold(press_frac_ref[...])
    fm = fold(fm_ref[...])
    mf = fold(mf_ref[...])
    last = code % 256 == 255
    tnext = jnp.where(last, 0.0, fold(chain_ref[...]))
    tprev = pltpu.roll(tnext, 1, 1)
    tprev = jnp.where(iota((8, 128), 1) == 0, pltpu.roll(tprev, 4, 0), tprev)
    diag = fold(accum_ref[...]) + tnext + tprev + fm
    inverse = 1.0 / diag
    partial = diag * press - chain(tnext, press)
    for b in range(4):
        here, _ = edge_codes(delta_ref, to_ref, b)
        at = code == b * 256 + from_ref[b]
        partial = partial - jnp.where(at, trans_ref[b] * total(jnp.where(code == here, press, 0.0)), 0.0)
    where_cell = (fold(layer_ref[...]) * 1024 + fold(cell_ref[...]) + 1).astype(f32)
    position = (iota((8, 128), 0) * 128 + iota((8, 128), 1) + 1).astype(f32)
    slots = to_slots([where_cell, mf * press, fm * inverse * fm, position], hot, mask)
    inverse_index, slots = slots[48:64], slots[:48]
    place = (owner * CAP + rank).astype(f32)
    edges = []
    for b in range(4):
        _, there = edge_codes(delta_ref, to_ref, b)
        at = code == b * 256 + from_ref[b]
        gain = trans_ref[b] * inverse
        edges.append(jnp.full((1, 128), there.astype(f32)))
        for value in (place, where_cell, gain * fm, gain * partial, gain * trans_ref[b]):
            edges.append(jnp.broadcast_to(total(jnp.where(at, value, 0.0)), (1, 128)))
        edges.append(jnp.full((1, 128), trans_ref[b]))
        edges.append(jnp.zeros((1, 128), f32))
    rows = [spread(slots, 16), slots, spread(slots, -16)] + edges + [jnp.zeros((80, 128), f32)]
    store_slots(out_ref, jnp.concatenate(rows, axis=0))
    first_face, last_face = faces_of(jnp.concatenate([press_ref[...].reshape(ROWS, 128), cond_ref[...].reshape(ROWS, 128)], axis=0))
    for across in (-16, 0, 16):
        put_faces(me, out_ref, 256, first_face, last_face, across)
    for i, value in enumerate((tnext, inverse, partial, fm, mf, owner.astype(f32), rank.astype(f32), press)):
        seg_ref[i] = value
    for i in range(2):
        seg_ref[8 + i] = inverse_index[8 * i : 8 * i + 8] - 1.0
    lane = iota((8, 128), 1)
    own = jnp.zeros((8, 128), f32)
    for b in range(4):
        here, there = edge_codes(delta_ref, to_ref, b)
        for i, value in enumerate((b * 256 + from_ref[b], here, there)):
            own = jnp.where(lane == 8 * b + i, value.astype(f32), own)
        own = jnp.where(lane == 8 * b + 3, trans_ref[b], own)
    seg_ref[10] = own
    plane_x = iota((EXT, 128), 0) + ((me >> 4) - 1) * 8
    plane_y = iota((EXT, 128), 1) + (me & 15) * 128
    source = jnp.zeros((EXT, 128), f32)
    for w in range(well_tile_ref.shape[0]):
        tile = well_tile_ref[w]
        cell = well_cell_ref[w]
        at = (plane_x == (tile >> 4) * 8 + (cell >> 7)) & (plane_y == (tile & 15) * 128 + (cell & 127))
        source = source + jnp.where(at, well_rate_ref[w], 0.0)
    for i in range(3):
        seg_ref[11 + i] = source[8 * i : 8 * i + 8]


def edge_in(row, k, i):
    at = 16 + 8 * k + i
    return row[:, at : at + 1]


def cells_kernel(
    me_ref,
    got_ref, middle_ref, inside_ref, across_ref, seg_ref,
    out_ref, cells_ref, field_ref, index_ref, columns_ref, rows_ref, edge_ref, res_ref,
):
    me = me_ref[0]
    slots = load_slots(got_ref, 256)
    even = ((me >> 4) & 1) == 0
    press, cond, accum = (
        jnp.concatenate([jnp.where(even, b, a), middle_ref[i], jnp.where(even, a, b)], axis=1)
        for i, a, b in ((i, inside_ref[i], across_ref[i]) for i in range(3))
    )
    sums = []
    for side in range(3):
        table = slots[side * 48 : side * 48 + 48]
        index = table[:CAP].astype(i32) - 1
        if side == 1:
            index_ref[...] = index
            own = index
        columns, rows = cell_hot(as_row(index))
        columns_ref[side] = columns
        rows_ref[side] = rows
        sums.append(scatter([table[16:32], table[32:48]], columns, rows))
    flow, weight = (jnp.concatenate([sums[side][i] for side in range(3)], axis=1) for i in range(2))

    halos = [columns_of(*read_faces(me, got_ref, 256, 2 * ROWS, across)) for across in (-16, 0, 16)]
    press_halo = jnp.concatenate([halo[:ROWS].reshape(LAYERS, 8, 128) for halo in halos], axis=1)
    cond_halo = jnp.concatenate([halo[ROWS:].reshape(LAYERS, 8, 128) for halo in halos], axis=1)
    lane = iota((LAYERS, EXT, 128), 2)
    tx = harmonic(cond, up_x(cond))
    ty = harmonic(cond, up_y(cond, cond_halo))
    tz = 0.5 * harmonic(cond, up_z(cond))
    ty_first = jnp.where(lane == 0, harmonic(cond, cond_halo), 0.0)
    diag = accum + tx + down_x(tx) + ty + down_y(ty, ty_first) + tz + down_z(tz)
    inverse = jnp.where(diag > 0.0, 1.0 / jnp.where(diag > 0.0, diag, 1.0), 0.0)

    source = jnp.concatenate([seg_ref[11 + i] for i in range(3)], axis=0)
    res = diag * press - stencil(tx, ty, tz, ty_first, press, press_halo) - flow - source[None]
    field = inverse * res
    for i, value in enumerate((tx, ty, tz, ty_first, inverse, res, weight * press)):
        cells_ref[i] = value
    field_ref[...] = field
    res_ref[...] = res[:, 8:16]

    code = seg_code().astype(f32)
    _, inverse_f, partial, fm, _, _, _, press_f = (seg_ref[i] for i in range(8))
    edge = jnp.where(me > 0, got_ref[jnp.maximum(me - 1, 0), :, 128:256], -1.0)
    lane = iota((1, 128), 1)
    cells, terms, picks = [], [], []
    for k in range(4):
        there = edge_in(edge, k, 0)
        picked = total(jnp.where(code == there, press_f, 0.0))
        at = (lane == (edge_in(edge, k, 1).astype(i32) >> 4)) & (there >= 0.0)
        cells.append(jnp.where(at, edge_in(edge, k, 2), 0.0))
        terms.append(jnp.where(at, -edge_in(edge, k, 3) * picked, 0.0))
        picks.append(jnp.broadcast_to(picked, (1, 128)))
        edge = jnp.where(lane == 16 + 8 * k + 4, edge - edge_in(edge, k, 5) * picked, edge)
    edge_ref[...] = jnp.broadcast_to(edge, (8, 128))
    late = jnp.concatenate(cells + terms, axis=0)
    position = jnp.concatenate([seg_ref[8], seg_ref[9]], axis=0).astype(i32)
    first = find(fm * inverse_f * partial, position)

    taken = [find(middle_ref[0].reshape(ROWS, 128), own), find(field[:, 8:16].reshape(ROWS, 128), own)]
    rows = taken + [spread(taken[0], 1)]
    rows += [spread(first, 16), first, spread(first, -16), spread(late, 16), late, spread(late, -16)]
    store_slots(out_ref, jnp.concatenate(rows + picks + [jnp.zeros((4, 128), f32)], axis=0))
    put_faces(me, out_ref, 128, *faces_of(field.reshape(LAYERS * EXT, 128)))


def step_kernel(
    first, final,
    me_ref,
    got_ref, cells_ref, field_ref, index_ref, columns_ref, rows_ref, seg_ref, edge_ref, *rest,
):
    me = me_ref[0]
    if not first:
        frac_ref, resf_ref, *rest = rest
    slots = load_slots(got_ref, 128)
    code = seg_code().astype(f32)
    tnext, inverse_f, partial, fm, mf, owner, rank = (seg_ref[i] for i in range(7))
    owner = owner.astype(i32)
    rank = rank.astype(i32)
    edge = edge_ref[0:1]
    own = seg_ref[10][0:1]
    starts, targets, nexts, factors = ([own[:, 8 * b + i : 8 * b + i + 1] for b in range(4)] for i in range(4))

    if first:
        resf = partial - fm * look_up(slots[0:16], rank, owner)
        after = got_ref[jnp.minimum(me + 1, TILES - 1), :, 0:128]
        for b in range(4):
            at = (code == starts[b]) & (nexts[b] >= 0.0)
            resf = resf - jnp.where(at, factors[b] * after[:, 120 + b : 121 + b], 0.0)
        frac = inverse_f * resf
        here = look_up(slots[16:32], rank, owner)
    else:
        resf = resf_ref[...]
        frac = frac_ref[...]
        here = look_up(slots[0:16], rank, owner)
    gain = resf + chain(tnext, frac) + mf * here
    before = got_ref[jnp.maximum(me - 1, 0), :, 64:256]
    for b in range(4):
        term = factors[b] * total(jnp.where(code == starts[b], frac, 0.0))
        gain = gain + jnp.where(code == targets[b], term, 0.0)
        if first:
            place = (iota((CAP, 128), 1) * CAP + iota((CAP, 128), 0)).astype(f32)
            there = total(jnp.where(place == edge_in(edge, b, 1), slots[32:48], 0.0))
            term = edge_in(edge, b, 4) - edge_in(edge, b, 3) * there
        else:
            term = before[:, EXT * b : EXT * b + 1]
        gain = gain + jnp.where(code == edge_in(edge, b, 0), term, 0.0)
    frac = inverse_f * gain

    tx, ty, tz, ty_first, inverse, res = (cells_ref[i] for i in range(6))
    field = field_ref[...]
    flow = []
    for side in range(3):
        if final and side != 1:
            flow.append(jnp.zeros((LAYERS, 8, 128), f32))
            continue
        start = (48 if first else 16) + side * CAP
        flow.extend(scatter([slots[start : start + CAP]], columns_ref[side], rows_ref[side]))
        if first:
            late = slots[96 + 8 * side : 104 + 8 * side]
            more = scatter([late[4:]], *cell_hot(as_row(late[:4].astype(i32) - 1)))
            flow[side] = flow[side] + more[0]
    flow = jnp.concatenate(flow, axis=1)
    if first:
        flow = flow - cells_ref[6]
    halo = columns_of(*read_faces(me, got_ref, 128 if first else 64, LAYERS * EXT)).reshape(LAYERS, EXT, 128)
    field = inverse * (res + stencil(tx, ty, tz, ty_first, field, halo) + flow)

    if final:
        adj_matrix_ref, adj_fracture_ref = rest
        adj_matrix_ref[...] = field[:, 8:16]
        adj_fracture_ref[...] = unfold(frac)
        return
    out_ref, new_field_ref, new_frac_ref = rest[:3]
    if first:
        resf_out_ref, res_fracture_ref = rest[3:]
        resf_out_ref[...] = resf
        res_fracture_ref[...] = unfold(resf)
    new_field_ref[...] = field
    new_frac_ref[...] = frac
    taken = [find(field[:, 8:16].reshape(ROWS, 128), index_ref[...])]
    terms = find(fm * frac, jnp.concatenate([seg_ref[8], seg_ref[9]], axis=0).astype(i32))
    store_slots(out_ref, jnp.concatenate(taken + [spread(terms, 16), terms, spread(terms, -16)], axis=0))
    begin, end = faces_of(field.reshape(LAYERS * EXT, 128))
    lane = iota(end.shape, 1)
    for b in range(4):
        end = jnp.where(lane == EXT * b, factors[b] * total(jnp.where(code == starts[b], frac, 0.0)), end)
    put_faces(me, out_ref, 64, begin, end)


def call(kernel, name, scalars, arrays, outs, space=pltpu.VMEM, scratch=(), limit=20 * 1024 * 1024):
    spec = [pl.BlockSpec(memory_space=pltpu.SMEM)] * len(scalars)
    spec += [pl.BlockSpec(memory_space=space)] * len(arrays)
    return pl.pallas_call(
        kernel,
        name=name,
        out_shape=[jax.ShapeDtypeStruct(shape, kind) for shape, kind in outs],
        in_specs=spec,
        out_specs=[pl.BlockSpec(memory_space=pltpu.VMEM)] * len(outs),
        scratch_shapes=list(scratch),
        compiler_params=pltpu.CompilerParams(vmem_limit_bytes=limit),
    )(*scalars, *arrays)


def exchange(message):
    return lax.all_to_all(message, ALL, split_axis=0, concat_axis=0, tiled=True)


def swapped(block, first):
    pairs = [(i, i + 1) for i in range(first, lax.axis_size("gx") - 1, 2)]
    return lax.ppermute(block, "gx", pairs + [(j, i) for i, j in pairs])


def body(
    press_matrix, cond_matrix, accum_matrix, press_frac, accum_frac, trans_chain, couple_mf, couple_fm,
    conn_tile, conn_layer, conn_cell, inter_delta, inter_from, inter_to, inter_trans, well_tile, well_cell, well_rate,
):
    me = lax.axis_index(ALL).astype(i32).reshape(1)
    stacked = jnp.stack([press_matrix, cond_matrix, accum_matrix])
    inside = swapped(stacked, 0)
    across = swapped(stacked, 1)
    wide = (LAYERS, EXT, 128)
    tile = (LAYERS, 8, 128)
    seg = (8, 128)

    given = (conn_tile, conn_layer, conn_cell, press_frac, accum_frac, trans_chain, couple_mf, couple_fm, press_matrix, cond_matrix)
    message, segs = call(
        begin_kernel,
        "begin",
        (me, inter_delta, inter_from, inter_to, inter_trans, well_tile, well_cell, well_rate),
        given,
        [((TILES, 1, 384), f32), ((14, *seg), f32)],
        pl.ANY,
        [pltpu.VMEM(a.shape, a.dtype) for a in given] + [pltpu.SemaphoreType.DMA((len(given),))],
        64 * 1024 * 1024,
    )
    got = exchange(message)
    message, cells, field, index, columns, rows, edge, res_matrix = call(
        cells_kernel,
        "cells",
        (me,),
        (got, stacked, inside, across, segs),
        [((TILES, 1, 384), f32), ((7, *wide), f32), (wide, f32), ((CAP, 128), i32), ((3, 128, SLOTS), bf16),
         ((3, ROWS, SLOTS), bf16), (seg, f32), (tile, f32)],
    )
    got = exchange(message)

    def step(first, final, got, field, more, outs):
        def kernel(*refs):
            step_kernel(first, final, *refs)

        return call(kernel, "step", (me,), (got, cells, field, index, columns, rows, segs, edge, *more), outs)

    going = [((TILES, 1, 256), f32), (wide, f32), (seg, f32)]
    message, field, frac, resf, res_fracture = step(
        True, False, got, field, (), going + [(seg, f32), ((4, 256), f32)]
    )
    for _ in range(ITERS - 3):
        got = exchange(message)
        message, field, frac = step(False, False, got, field, (frac, resf), going)
    got = exchange(message)
    adj_matrix, adj_fracture = step(False, True, got, field, (frac, resf), [(tile, f32), ((4, 256), f32)])
    return res_matrix, res_fracture, adj_matrix, adj_fracture


def solution(mesh):
    cells = P(None, "gx", YA)
    segs = P(ALL, None)
    blocks = P(ALL)
    in_specs = (cells,) * 3 + (segs,) * 8 + (blocks,) * 4 + (P(),) * 3
    return jax.shard_map(body, mesh=mesh, in_specs=in_specs, out_specs=(cells, segs, cells, segs), check_vma=False)
```

```python
import jax
import jax.numpy as jnp
from jax import lax
from jax.experimental import pallas as pl
from jax.experimental.pallas import tpu as pltpu
from jax.sharding import PartitionSpec as P

ITERS = 8
CAP = 16
TILES = 128
ROWS = 64
EXT = 24
LAYERS = 8
SLOTS = CAP * TILES
ALL = ("gx", "gy", "af")
YA = ("gy", "af")
BESIDE = (17, 1, -15, 15, -1, -17)
f32 = jnp.float32
bf16 = jnp.bfloat16
i32 = jnp.int32


def iota(shape, axis):
    return lax.broadcasted_iota(i32, shape, axis)


def parts(value):
    high = value.astype(bf16)
    return high, (value - high.astype(f32)).astype(bf16)


def dot_nn(a, b):
    return lax.dot_general(a, b, (((1,), (0,)), ((), ())), preferred_element_type=f32)


def dot_nt(a, b):
    return lax.dot_general(a, b, (((1,), (1,)), ((), ())), preferred_element_type=f32)


def dot_tn(a, b):
    return lax.dot_general(a, b, (((0,), (0,)), ((), ())), preferred_element_type=f32)


def as_row(rows):
    return jnp.concatenate([rows[i : i + 1] for i in range(rows.shape[0])], axis=1)


def as_rows(row):
    return jnp.concatenate([row[:, i : i + 128] for i in range(0, row.shape[1], 128)], axis=0)


def total(value):
    return jnp.sum(jnp.sum(value, axis=1, keepdims=True), axis=0, keepdims=True)


def fold(value):
    return jnp.concatenate([value[:, :128], value[:, 128:]], axis=0)


def unfold(value):
    return jnp.concatenate([value[:4], value[4:]], axis=1)


def seg_code():
    row = iota((8, 128), 0)
    return (row % 4) * 256 + (row // 4) * 128 + iota((8, 128), 1)


def chain(tnext, field):
    lane = iota((8, 128), 1)
    ahead = pltpu.roll(field, 127, 1)
    ahead = jnp.where(lane == 127, pltpu.roll(ahead, 4, 0), ahead)
    behind = pltpu.roll(tnext * field, 1, 1)
    behind = jnp.where(lane == 0, pltpu.roll(behind, 4, 0), behind)
    return tnext * ahead + behind


def owner_hot(owner_row):
    return (iota((TILES, 1024), 0) == owner_row).astype(bf16)


def rank_mask(rank_row):
    return iota((CAP, 1024), 0) == rank_row


def to_slots(values, hot, mask):
    halves = ([], [])
    for value in values:
        row = as_row(value)
        for half, part in zip(halves, parts(row)):
            half.append(jnp.where(mask, part.astype(f32), 0.0).astype(bf16))
    both = jnp.concatenate([jnp.concatenate(half, axis=0) for half in halves], axis=1)
    return dot_nt(both, jnp.concatenate([hot, hot], axis=1))


def look_up(table, row, lane):
    out = jnp.zeros(row.shape, f32)
    for r in range(table.shape[0]):
        picked = jnp.take_along_axis(jnp.broadcast_to(table[r : r + 1], row.shape), lane, axis=1, mode="promise_in_bounds")
        out = jnp.where(row == r, picked, out)
    return out


def find(table, index):
    return look_up(table, index >> 7, index & 127)


def cell_hot(index_row):
    count = index_row.shape[1]
    columns = iota((128, count), 0) == (index_row & 127)
    rows = iota((ROWS, count), 0) == (index_row >> 7)
    return columns.astype(bf16), rows.astype(bf16)


def scatter(tables, columns, rows):
    stacked = []
    for table in tables:
        for part in parts(table):
            row = as_row(part.astype(f32))
            tall = jnp.broadcast_to(row, (16, row.shape[1])).astype(bf16)
            stacked.append(rows * jnp.concatenate([tall] * (ROWS // 16), axis=0))
    sums = dot_nt(jnp.concatenate(stacked, axis=0), columns)
    return [
        (sums[2 * i * ROWS : (2 * i + 1) * ROWS] + sums[(2 * i + 1) * ROWS : (2 * i + 2) * ROWS]).reshape(LAYERS, 8, 128)
        for i in range(len(tables))
    ]


def faces_of(field):
    rows = iota((16, 128), 0)
    lanes = iota((16, 128), 1)
    pick = (((rows == 0) & (lanes == 0)) | ((rows == 1) & (lanes == 127))).astype(bf16)
    both = dot_nt(jnp.concatenate([pick, pick], axis=1), jnp.concatenate(parts(field), axis=1))
    return both[0:1], both[1:2]


def columns_of(left, right):
    width = left.shape[1]
    held = [part.astype(f32) for row in (left, right) for part in parts(row)]
    held = jnp.concatenate(held + [jnp.zeros((12, width), f32)], axis=0).astype(bf16)
    rows = iota((16, 128), 0)
    lanes = iota((16, 128), 1)
    place = (((rows < 2) & (lanes == 0)) | ((rows >= 2) & (rows < 4) & (lanes == 127))).astype(bf16)
    return dot_tn(held, place)


def up_x(v):
    return jnp.concatenate([v[:, 1:], jnp.zeros_like(v[:, :1])], axis=1)


def down_x(v):
    return jnp.concatenate([jnp.zeros_like(v[:, :1]), v[:, :-1]], axis=1)


def up_z(v):
    return jnp.concatenate([v[1:], jnp.zeros_like(v[:1])], axis=0)


def down_z(v):
    return jnp.concatenate([jnp.zeros_like(v[:1]), v[:-1]], axis=0)


def up_y(v, halo):
    return jnp.where(iota(v.shape, 2) == 127, halo, pltpu.roll(v, 127, 2))


def down_y(v, first):
    return jnp.where(iota(v.shape, 2) == 0, first, pltpu.roll(v, 1, 2))


def stencil(tx, ty, tz, ty_first, field, halo):
    out = tx * up_x(field) + down_x(tx * field)
    out = out + ty * up_y(field, halo) + down_y(ty * field, ty_first * halo)
    return out + tz * up_z(field) + down_z(tz * field)


def harmonic(first, second):
    both = first + second
    return jnp.where(both > 0.0, 2.0 * first * second / jnp.where(both > 0.0, both, 1.0), 0.0)


def read_faces(me, got_ref, start, width, across=0):
    along = me & 15
    line = (me >> 4) + across // 16
    inside = (line >= 0) & (line < 8)
    before = got_ref[jnp.clip(me + across - 1, 0, TILES - 1), :, start : start + width]
    after = got_ref[jnp.clip(me + across + 1, 0, TILES - 1), :, start : start + width]
    return jnp.where(inside & (along > 0), before, 0.0), jnp.where(inside & (along < 15), after, 0.0)


def put_faces(me, out_ref, start, first, last, across=0):
    width = first.shape[1]
    for at, face in ((me + across - 1, first), (me + across + 1, last)):
        out_ref[jnp.where((at >= 0) & (at < TILES), at, me), :, start : start + width] = face


def edge_codes(delta_ref, to_ref, b):
    block = b + delta_ref[b]
    code = block * 256 + to_ref[b]
    return jnp.where(block < 4, code, -1), jnp.where(block >= 4, code - 1024, -1)


def spread(rows, shift):
    lane = iota(rows.shape, 1)
    inside = (lane >= shift) if shift > 0 else (lane < TILES + shift)
    return jnp.where(inside, pltpu.roll(rows, shift % TILES, 1), 0.0)


def store_slots(out_ref, rows):
    for i in range(0, rows.shape[0], 128):
        part = rows[i : i + 128].T
        out_ref[:, 0, i : i + part.shape[1]] = part


def load_slots(got_ref, count):
    return jnp.concatenate([got_ref[:, 0, i : i + 128].T for i in range(0, count, 128)], axis=0)


def begin_kernel(
    me_ref, delta_ref, from_ref, to_ref, trans_ref, well_tile_ref, well_cell_ref, well_rate_ref, *refs
):
    given, (out_ref, seg_ref), held, sems = refs[:10], refs[10:12], refs[12:22], refs[22]
    copies = [pltpu.make_async_copy(a, b, sems.at[i]) for i, (a, b) in enumerate(zip(given, held))]
    for copy in copies:
        copy.start()
    for copy in copies:
        copy.wait()
    tile_ref, layer_ref, cell_ref, press_frac_ref, accum_ref, chain_ref, mf_ref, fm_ref, press_ref, cond_ref = held
    me = me_ref[0]
    code = seg_code()
    owner = fold(tile_ref[...])
    owner_row = as_row(owner)
    hot = owner_hot(owner_row)
    before = (iota((128, 128), 0) < iota((128, 128), 1)).astype(bf16)
    base = jnp.zeros((TILES, 1), f32)
    ranks = []
    for c in range(8):
        part = hot[:, c * 128 : (c + 1) * 128]
        wide = part.astype(f32)
        count = dot_nn(part, before) + base
        ranks.append(jnp.sum(wide * count, axis=0, keepdims=True))
        base = base + jnp.sum(wide, axis=1, keepdims=True)
    rank_row = jnp.concatenate(ranks, axis=1).astype(i32)
    rank = as_rows(rank_row)
    mask = rank_mask(rank_row)

    press = fold(press_frac_ref[...])
    fm = fold(fm_ref[...])
    mf = fold(mf_ref[...])
    last = code % 256 == 255
    tnext = jnp.where(last, 0.0, fold(chain_ref[...]))
    tprev = pltpu.roll(tnext, 1, 1)
    tprev = jnp.where(iota((8, 128), 1) == 0, pltpu.roll(tprev, 4, 0), tprev)
    diag = fold(accum_ref[...]) + tnext + tprev + fm
    inverse = 1.0 / diag
    partial = diag * press - chain(tnext, press)
    for b in range(4):
        here, _ = edge_codes(delta_ref, to_ref, b)
        at = code == b * 256 + from_ref[b]
        partial = partial - jnp.where(at, trans_ref[b] * total(jnp.where(code == here, press, 0.0)), 0.0)
    where_cell = (fold(layer_ref[...]) * 1024 + fold(cell_ref[...]) + 1).astype(f32)
    position = (iota((8, 128), 0) * 128 + iota((8, 128), 1) + 1).astype(f32)
    slots = to_slots([where_cell, mf * press, fm * inverse * fm, fm * inverse * mf, position], hot, mask)
    inverse_index, slots = slots[64:80], slots[:64]
    place = (owner * CAP + rank).astype(f32)
    edges = []
    for b in range(4):
        _, there = edge_codes(delta_ref, to_ref, b)
        at = code == b * 256 + from_ref[b]
        gain = trans_ref[b] * inverse
        edges.append(jnp.full((1, 128), there.astype(f32)))
        for value in (place, where_cell, gain * fm, gain * partial, gain * trans_ref[b], gain * mf, code.astype(f32), gain):
            edges.append(jnp.broadcast_to(total(jnp.where(at, value, 0.0)), (1, 128)))
        edges.append(jnp.zeros((3, 128), f32))
    rows = [spread(slots, 16), slots, spread(slots, -16)] + edges
    rows += [spread(slots[:CAP], shift) for shift in BESIDE] + [jnp.zeros((48, 128), f32)]
    store_slots(out_ref, jnp.concatenate(rows, axis=0))
    first_face, last_face = faces_of(jnp.concatenate([press_ref[...].reshape(ROWS, 128), cond_ref[...].reshape(ROWS, 128)], axis=0))
    for across in (-16, 0, 16):
        put_faces(me, out_ref, 384, first_face, last_face, across)
    for i, value in enumerate((tnext, inverse, partial, fm, mf, owner.astype(f32), rank.astype(f32), press)):
        seg_ref[i] = value
    for i in range(2):
        seg_ref[8 + i] = inverse_index[8 * i : 8 * i + 8] - 1.0
    lane = iota((8, 128), 1)
    own = jnp.zeros((8, 128), f32)
    for b in range(4):
        here, there = edge_codes(delta_ref, to_ref, b)
        for i, value in enumerate((b * 256 + from_ref[b], here, there)):
            own = jnp.where(lane == 8 * b + i, value.astype(f32), own)
        own = jnp.where(lane == 8 * b + 3, trans_ref[b], own)
    seg_ref[10] = own
    plane_x = iota((EXT, 128), 0) + ((me >> 4) - 1) * 8
    plane_y = iota((EXT, 128), 1) + (me & 15) * 128
    source = jnp.zeros((EXT, 128), f32)
    for w in range(well_tile_ref.shape[0]):
        tile = well_tile_ref[w]
        cell = well_cell_ref[w]
        at = (plane_x == (tile >> 4) * 8 + (cell >> 7)) & (plane_y == (tile & 15) * 128 + (cell & 127))
        source = source + jnp.where(at, well_rate_ref[w], 0.0)
    for i in range(3):
        seg_ref[11 + i] = source[8 * i : 8 * i + 8]
    seg_ref[14] = where_cell


def edge_in(row, k, i):
    at = 64 + 12 * k + i
    return row[:, at : at + 1]


def cells_kernel(
    me_ref,
    got_ref, middle_ref, inside_ref, across_ref, seg_ref,
    out_ref, cells_ref, field_ref, index_ref, columns_ref, rows_ref, edge_ref, beside_ref, res_ref,
):
    me = me_ref[0]
    slots = load_slots(got_ref, 384)
    even = ((me >> 4) & 1) == 0
    press, cond, accum = (
        jnp.concatenate([jnp.where(even, b, a), middle_ref[i], jnp.where(even, a, b)], axis=1)
        for i, a, b in ((i, inside_ref[i], across_ref[i]) for i in range(3))
    )
    sums = []
    for side in range(3):
        table = slots[side * 64 : side * 64 + 64]
        index = table[:CAP].astype(i32) - 1
        if side == 1:
            index_ref[...] = index
            own = index
        columns, rows = cell_hot(as_row(index))
        columns_ref[side] = columns
        rows_ref[side] = rows
        sums.append(scatter([table[16:32], table[32:48], table[48:64]], columns, rows))
    flow, weight, mirror = (jnp.concatenate([sums[side][i] for side in range(3)], axis=1) for i in range(3))
    beside = slots[240:336].astype(i32) - 1
    along = me & 15
    for i, (there, column) in enumerate(((along > 0, 127), (along < 15, 0))):
        part = beside[48 * i : 48 * i + 48]
        beside_ref[48 * i : 48 * i + 48] = jnp.where(there & (part >= 0) & ((part & 127) == column), part >> 7, -1)

    halos = [columns_of(*read_faces(me, got_ref, 384, 2 * ROWS, across)) for across in (-16, 0, 16)]
    press_halo = jnp.concatenate([halo[:ROWS].reshape(LAYERS, 8, 128) for halo in halos], axis=1)
    cond_halo = jnp.concatenate([halo[ROWS:].reshape(LAYERS, 8, 128) for halo in halos], axis=1)
    lane = iota((LAYERS, EXT, 128), 2)
    tx = harmonic(cond, up_x(cond))
    ty = harmonic(cond, up_y(cond, cond_halo))
    tz = 0.5 * harmonic(cond, up_z(cond))
    ty_first = jnp.where(lane == 0, harmonic(cond, cond_halo), 0.0)
    diag = accum + tx + down_x(tx) + ty + down_y(ty, ty_first) + tz + down_z(tz)
    inverse = jnp.where(diag > 0.0, 1.0 / jnp.where(diag > 0.0, diag, 1.0), 0.0)

    source = jnp.concatenate([seg_ref[11 + i] for i in range(3)], axis=0)
    res = diag * press - stencil(tx, ty, tz, ty_first, press, press_halo) - flow - source[None]
    field = inverse * res
    for i, value in enumerate((tx, ty, tz, ty_first, inverse, res, weight * press, mirror)):
        cells_ref[i] = value
    field_ref[...] = field
    res_ref[...] = res[:, 8:16]

    code = seg_code().astype(f32)
    _, inverse_f, partial, fm, _, owner, _, press_f = (seg_ref[i] for i in range(8))
    edge = jnp.where(me > 0, got_ref[jnp.maximum(me - 1, 0), :, 128:256], -1.0)
    lane = iota((1, 128), 1)
    cells, terms, picks, found = [], [], [], []
    for k in range(4):
        there = edge_in(edge, k, 0)
        picked = total(jnp.where(code == there, press_f, 0.0))
        at = (lane == (edge_in(edge, k, 1).astype(i32) >> 4)) & (there >= 0.0)
        cells.append(jnp.where(at, edge_in(edge, k, 2), 0.0))
        terms.append(jnp.where(at, -edge_in(edge, k, 3) * picked, 0.0))
        picks.append(jnp.broadcast_to(picked, (1, 128)))
        found.append([total(jnp.where(code == there, value, 0.0)) for value in (owner, seg_ref[14], fm * inverse_f)])
        edge = jnp.where(lane == 64 + 12 * k + 4, edge - edge_in(edge, k, 5) * picked, edge)
    edge_ref[...] = jnp.broadcast_to(edge, (8, 128))
    late = jnp.concatenate(cells + terms, axis=0)
    position = jnp.concatenate([seg_ref[8], seg_ref[9]], axis=0).astype(i32)
    first = find(fm * inverse_f * partial, position)

    taken = [find(middle_ref[0].reshape(ROWS, 128), own), find(field[:, 8:16].reshape(ROWS, 128), own)]
    rows = taken + [spread(taken[0], 1)]
    rows += [spread(first, 16), first, spread(first, -16), spread(late, 16), late, spread(late, -16)]
    store_slots(out_ref, jnp.concatenate(rows + picks + [jnp.zeros((4, 128), f32)], axis=0))
    begin, end = faces_of(field.reshape(LAYERS * EXT, 128))
    begin_inverse, end_inverse = faces_of(inverse.reshape(LAYERS * EXT, 128))
    for k, (tile, cell, weight_there) in enumerate(found):
        begin = put_entry(begin, k, tile)
        begin = put_entry(begin, 4 + k, cell)
        begin_inverse = put_entry(begin_inverse, k, weight_there)
    put_faces(me, out_ref, 128, begin, end)
    put_faces(me, out_ref, 320, begin_inverse, end_inverse)


def put_entry(face, k, value):
    return jnp.where(iota(face.shape, 1) == EXT * k, value, face)


def get_entry(face, k):
    return face[:, EXT * k : EXT * k + 1]


def own_edges(seg_ref):
    own = seg_ref[10][0:1]
    return [[own[:, 8 * b + i : 8 * b + i + 1] for b in range(4)] for i in range(4)]


def edge_terms(code, edges, frac):
    starts, _, _, factors = edges
    return [factor * total(jnp.where(code == start, frac, 0.0)) for start, factor in zip(starts, factors)]


def arrive(code, targets, terms):
    gain = jnp.zeros(code.shape, f32)
    for target, term in zip(targets, terms):
        gain = gain + jnp.where(code == target, term, 0.0)
    return gain


def late_rows(edges, ends, terms):
    lane = iota((1, 128), 1)
    cells, values = [], []
    for there, (tile, cell, weight), term in zip(edges[2], ends, terms):
        at = (lane == tile.astype(i32)) & (there >= 0.0)
        cells.append(jnp.where(at, cell, 0.0))
        values.append(jnp.where(at, weight * term, 0.0))
    return jnp.concatenate(cells + values, axis=0)


def to_three(rows):
    return [spread(rows, 16), rows, spread(rows, -16)]


def scatter_late(late):
    return scatter([late[4:]], *cell_hot(as_row(late[:4].astype(i32) - 1)))[0]


def own_tile(field):
    return field[:, 8:16].reshape(ROWS, 128)


def start_of(edge, k, table):
    place = (iota((CAP, 128), 1) * CAP + iota((CAP, 128), 0)).astype(f32)
    return total(jnp.where(place == edge_in(edge, k, 1), table, 0.0))


def advance(cells_ref, field, halo, flow):
    tx, ty, tz, ty_first, inverse, res = (cells_ref[i] for i in range(6))
    return inverse * (res + stencil(tx, ty, tz, ty_first, field, halo) + flow)


def wide_halo(me, got_ref, start):
    return columns_of(*read_faces(me, got_ref, start, LAYERS * EXT)).reshape(LAYERS, EXT, 128)


def ends_of(ends_ref):
    held = ends_ref[0:1]
    return [[held[:, 3 * k + i : 3 * k + i + 1] for i in range(3)] for k in range(4)]


def send_wide(me, out_ref, code, edges, ends, seg_ref, cells_ref, index_ref, field, frac, resf):
    tnext, inverse_f, fm = seg_ref[0], seg_ref[1], seg_ref[3]
    terms = edge_terms(code, edges, frac)
    ahead = inverse_f * (resf + chain(tnext, frac) + arrive(code, edges[1], terms))
    part = advance(cells_ref, field, jnp.zeros((LAYERS, EXT, 128), f32), 0.0)
    position = jnp.concatenate([seg_ref[8], seg_ref[9]], axis=0).astype(i32)
    now = find(fm * frac, position)
    rows = [find(own_tile(field), index_ref[...])] + to_three(now) + to_three(find(fm * ahead, position))
    rows += to_three(late_rows(edges, ends, terms)) + [spread(now, shift) for shift in BESIDE]
    store_slots(out_ref, jnp.concatenate(rows + [jnp.zeros((24, 128), f32)], axis=0))
    begin, end = faces_of(field.reshape(LAYERS * EXT, 128))
    for b in range(4):
        end = put_entry(end, b, terms[b])
    put_faces(me, out_ref, 256, begin, end)
    put_faces(me, out_ref, 448, *faces_of(part.reshape(LAYERS * EXT, 128)))


def first_kernel(
    me_ref, got_ref, cells_ref, field_ref, index_ref, columns_ref, rows_ref, seg_ref, edge_ref,
    out_ref, new_field_ref, new_frac_ref, resf_ref, ends_ref, halo_inverse_ref, res_fracture_ref,
):
    me = me_ref[0]
    slots = load_slots(got_ref, 128)
    code = seg_code().astype(f32)
    tnext, inverse_f, partial, fm, mf, owner, rank = (seg_ref[i] for i in range(7))
    owner = owner.astype(i32)
    rank = rank.astype(i32)
    edge = edge_ref[0:1]
    edges = own_edges(seg_ref)
    starts, targets, nexts, factors = edges

    resf = partial - fm * look_up(slots[0:16], rank, owner)
    after = got_ref[jnp.minimum(me + 1, TILES - 1), :, :]
    for b in range(4):
        at = (code == starts[b]) & (nexts[b] >= 0.0)
        resf = resf - jnp.where(at, factors[b] * after[:, 120 + b : 121 + b], 0.0)
    frac = inverse_f * resf
    terms = edge_terms(code, edges, frac)
    before = [edge_in(edge, k, 4) - edge_in(edge, k, 3) * start_of(edge, k, slots[32:48]) for k in range(4)]
    gain = resf + chain(tnext, frac) + mf * look_up(slots[16:32], rank, owner)
    gain = gain + arrive(code, targets, terms) + arrive(code, [edge_in(edge, k, 0) for k in range(4)], before)
    frac = inverse_f * gain
    flow = []
    for side in range(3):
        sums = scatter([slots[48 + side * CAP : 64 + side * CAP]], columns_ref[side], rows_ref[side])
        flow.append(sums[0] + scatter_late(slots[96 + 8 * side : 104 + 8 * side]))
    flow = jnp.concatenate(flow, axis=1) - cells_ref[6]
    field = advance(cells_ref, field_ref[...], wide_halo(me, got_ref, 128), flow)
    new_field_ref[...] = field
    new_frac_ref[...] = frac
    resf_ref[...] = resf
    res_fracture_ref[...] = unfold(resf)
    halo_inverse_ref[...] = wide_halo(me, got_ref, 320)
    face, weights = after[:, 128:320], after[:, 320:512]
    ends = [(get_entry(face, k), get_entry(face, 4 + k), get_entry(weights, k)) for k in range(4)]
    lane = iota((8, 128), 1)
    held = jnp.zeros((8, 128), f32)
    for k in range(4):
        for i in range(3):
            held = jnp.where(lane == 3 * k + i, ends[k][i], held)
    ends_ref[...] = held

    send_wide(me, out_ref, code, edges, ends, seg_ref, cells_ref, index_ref, field, frac, resf)


def even_kernel(
    me_ref, got_ref, cells_ref, field_ref, index_ref, columns_ref, rows_ref, seg_ref, edge_ref,
    frac_ref, resf_ref, ends_ref, halo_inverse_ref, beside_ref,
    out_ref, third_ref, new_field_ref, new_frac_ref,
):
    me = me_ref[0]
    slots = load_slots(got_ref, 256)
    code = seg_code().astype(f32)
    tnext, inverse_f, _, fm, mf, owner, rank = (seg_ref[i] for i in range(7))
    edge = edge_ref[0:1]
    edges = own_edges(seg_ref)
    targets = edges[1]
    resf = resf_ref[...]
    frac = frac_ref[...]
    before = got_ref[jnp.maximum(me - 1, 0), :, 256:448]
    gain = resf + chain(tnext, frac) + mf * look_up(slots[0:16], rank.astype(i32), owner.astype(i32))
    gain = gain + arrive(code, targets, edge_terms(code, edges, frac))
    gain = gain + arrive(code, [edge_in(edge, k, 0) for k in range(4)], [get_entry(before, k) for k in range(4)])
    frac = inverse_f * gain
    terms = edge_terms(code, edges, frac)
    ahead = inverse_f * (resf + chain(tnext, frac) + arrive(code, targets, terms))
    new_frac_ref[...] = frac

    flow, later, beside = [], [], []
    lane = iota((ROWS, 128), 1)
    level = iota((ROWS, 128), 0)
    for side in range(3):
        start = 16 + side * CAP
        sums = scatter([slots[start : start + CAP], slots[start + 48 : start + 48 + CAP]], columns_ref[side], rows_ref[side])
        flow.append(sums[0])
        later.append(sums[1] + scatter_late(slots[112 + 8 * side : 120 + 8 * side]))
        column = jnp.zeros((ROWS, 128), f32)
        for i, at in enumerate((0, 127)):
            first = 48 * i + CAP * side
            held = jnp.zeros((ROWS, 128), f32)
            for r in range(first, first + CAP):
                held = held + jnp.where(level == beside_ref[r : r + 1], slots[136 + r : 137 + r], 0.0)
            column = jnp.where(lane == at, jnp.sum(held, axis=1, keepdims=True), column)
        beside.append(column.reshape(LAYERS, 8, 128))
    flow, later, beside = (jnp.concatenate(parts_x, axis=1) for parts_x in (flow, later, beside))
    second = field_ref[...]
    third = advance(cells_ref, second, wide_halo(me, got_ref, 256), flow)
    lane = iota((LAYERS, EXT, 128), 2)
    joint = jnp.where(lane == 0, cells_ref[3], jnp.where(lane == 127, cells_ref[1], 0.0))
    halo = wide_halo(me, got_ref, 448) + halo_inverse_ref[...] * (joint * second + beside)
    field = advance(cells_ref, third, halo, later + cells_ref[7] * second)
    third_ref[...] = third
    new_field_ref[...] = field

    position = jnp.concatenate([seg_ref[8], seg_ref[9]], axis=0).astype(i32)
    ends = ends_of(ends_ref)
    own_third = find(own_tile(third), index_ref[...])
    rows = [own_third, find(own_tile(field), index_ref[...]), spread(own_third, 1)] + to_three(find(fm * ahead, position))
    rows += to_three(late_rows(edges, ends, terms))
    store_slots(out_ref, jnp.concatenate(rows + [jnp.zeros((8, 128), f32)], axis=0))
    begin, end = faces_of(field.reshape(LAYERS * EXT, 128))
    for b, term in enumerate(terms + edge_terms(code, edges, ahead)):
        end = put_entry(end, b, term)
    put_faces(me, out_ref, 128, begin, end)
    lane = iota((1, 64), 1)
    two = jnp.zeros((1, 64), f32)
    for b in range(4):
        two = jnp.where(lane == b, terms[b], jnp.where(lane == 4 + b, edges[2][b], two))
    out_ref[jnp.where(me + 2 < TILES, me + 2, me), :, 320:384] = two


def odd_kernel(
    final, me_ref, got_ref, cells_ref, field_ref, index_ref, columns_ref, rows_ref, seg_ref, edge_ref,
    frac_ref, resf_ref, ends_ref, third_ref, *outs,
):
    me = me_ref[0]
    slots = load_slots(got_ref, 128)
    code = seg_code().astype(f32)
    tnext, inverse_f, _, _, mf, owner, rank = (seg_ref[i] for i in range(7))
    owner = owner.astype(i32)
    rank = rank.astype(i32)
    edge = edge_ref[0:1]
    edges = own_edges(seg_ref)
    targets = edges[1]
    resf = resf_ref[...]
    frac = frac_ref[...]
    before = got_ref[jnp.maximum(me - 1, 0), :, 128:320]
    two = jnp.where(me > 1, got_ref[jnp.maximum(me - 2, 0), :, 320:384], -1.0)
    heres = [edge_in(edge, k, 0) for k in range(4)]
    gain = resf + chain(tnext, frac) + mf * look_up(slots[0:16], rank, owner)
    gain = gain + arrive(code, targets, edge_terms(code, edges, frac))
    frac = inverse_f * (gain + arrive(code, heres, [get_entry(before, k) for k in range(4)]))
    terms = []
    for k in range(4):
        term = get_entry(before, 4 + k) + edge_in(edge, k, 6) * start_of(edge, k, slots[32:48])
        for j in range(4):
            meets = two[:, 4 + j : 5 + j] == edge_in(edge, k, 7)
            term = term + jnp.where(meets, edge_in(edge, k, 8) * two[:, j : j + 1], 0.0)
        terms.append(term)
    gain = resf + chain(tnext, frac) + mf * look_up(slots[16:32], rank, owner)
    gain = gain + arrive(code, targets, edge_terms(code, edges, frac))
    frac = inverse_f * (gain + arrive(code, heres, terms))

    flow = []
    for side in range(3):
        if final and side != 1:
            flow.append(jnp.zeros((LAYERS, 8, 128), f32))
            continue
        start = 48 + side * CAP
        sums = scatter([slots[start : start + CAP]], columns_ref[side], rows_ref[side])
        flow.append(sums[0] + scatter_late(slots[96 + 8 * side : 104 + 8 * side]))
    flow = jnp.concatenate(flow, axis=1) + cells_ref[7] * third_ref[...]
    field = advance(cells_ref, field_ref[...], wide_halo(me, got_ref, 128), flow)
    if final:
        adj_matrix_ref, adj_fracture_ref = outs
        adj_matrix_ref[...] = field[:, 8:16]
        adj_fracture_ref[...] = unfold(frac)
        return
    out_ref, new_field_ref, new_frac_ref = outs
    new_field_ref[...] = field
    new_frac_ref[...] = frac
    send_wide(me, out_ref, code, edges, ends_of(ends_ref), seg_ref, cells_ref, index_ref, field, frac, resf)


def call(kernel, name, scalars, arrays, outs, space=pltpu.VMEM, scratch=(), limit=20 * 1024 * 1024):
    spec = [pl.BlockSpec(memory_space=pltpu.SMEM)] * len(scalars)
    spec += [pl.BlockSpec(memory_space=space)] * len(arrays)
    return pl.pallas_call(
        kernel,
        name=name,
        out_shape=[jax.ShapeDtypeStruct(shape, kind) for shape, kind in outs],
        in_specs=spec,
        out_specs=[pl.BlockSpec(memory_space=pltpu.VMEM)] * len(outs),
        scratch_shapes=list(scratch),
        compiler_params=pltpu.CompilerParams(vmem_limit_bytes=limit),
    )(*scalars, *arrays)


def exchange(message):
    return lax.all_to_all(message, ALL, split_axis=0, concat_axis=0, tiled=True)


def swapped(block, first):
    pairs = [(i, i + 1) for i in range(first, lax.axis_size("gx") - 1, 2)]
    return lax.ppermute(block, "gx", pairs + [(j, i) for i, j in pairs])


def body(
    press_matrix, cond_matrix, accum_matrix, press_frac, accum_frac, trans_chain, couple_mf, couple_fm,
    conn_tile, conn_layer, conn_cell, inter_delta, inter_from, inter_to, inter_trans, well_tile, well_cell, well_rate,
):
    me = lax.axis_index(ALL).astype(i32).reshape(1)
    stacked = jnp.stack([press_matrix, cond_matrix, accum_matrix])
    inside = swapped(stacked, 0)
    across = swapped(stacked, 1)
    wide = (LAYERS, EXT, 128)
    tile = (LAYERS, 8, 128)
    seg = (8, 128)

    given = (conn_tile, conn_layer, conn_cell, press_frac, accum_frac, trans_chain, couple_mf, couple_fm, press_matrix, cond_matrix)
    message, segs = call(
        begin_kernel,
        "begin",
        (me, inter_delta, inter_from, inter_to, inter_trans, well_tile, well_cell, well_rate),
        given,
        [((TILES, 1, 512), f32), ((15, *seg), f32)],
        pl.ANY,
        [pltpu.VMEM(a.shape, a.dtype) for a in given] + [pltpu.SemaphoreType.DMA((len(given),))],
        64 * 1024 * 1024,
    )
    got = exchange(message)
    message, cells, field, index, columns, rows, edge, beside, res_matrix = call(
        cells_kernel,
        "cells",
        (me,),
        (got, stacked, inside, across, segs),
        [((TILES, 1, 512), f32), ((8, *wide), f32), (wide, f32), ((CAP, 128), i32), ((3, 128, SLOTS), bf16),
         ((3, ROWS, SLOTS), bf16), (seg, f32), ((96, 128), i32), (tile, f32)],
    )
    kept = (index, columns, rows, segs, edge)
    going = [(wide, f32), (seg, f32)]
    got = exchange(message)
    message, field, frac, resf, ends, halo_inverse, res_fracture = call(
        first_kernel,
        "first",
        (me,),
        (got, cells, field, *kept),
        [((TILES, 1, 640), f32), *going, (seg, f32), (seg, f32), (wide, f32), ((4, 256), f32)],
    )
    for final in (False, True):
        got = exchange(message)
        message, third, field, frac = call(
            even_kernel,
            "even",
            (me,),
            (got, cells, field, *kept, frac, resf, ends, halo_inverse, beside),
            [((TILES, 1, 384), f32), (wide, f32), *going],
        )
        got = exchange(message)

        def kernel(*refs, final=final):
            odd_kernel(final, *refs)

        outs = [(tile, f32), ((4, 256), f32)] if final else [((TILES, 1, 640), f32), *going]
        results = call(kernel, "odd", (me,), (got, cells, field, *kept, frac, resf, ends, third), outs)
        if not final:
            message, field, frac = results
    adj_matrix, adj_fracture = results
    return res_matrix, res_fracture, adj_matrix, adj_fracture


def solution(mesh):
    cells = P(None, "gx", YA)
    segs = P(ALL, None)
    blocks = P(ALL)
    in_specs = (cells,) * 3 + (segs,) * 8 + (blocks,) * 4 + (P(),) * 3
    return jax.shard_map(body, mesh=mesh, in_specs=in_specs, out_specs=(cells, segs, cells, segs), check_vma=False)
```

```python
import functools

import jax
import jax.numpy as jnp
from jax import lax
from jax.experimental import pallas as pl
from jax.experimental.pallas import tpu as pltpu
from jax.sharding import PartitionSpec as P

ITERS = 8
CAP = 16
TILES = 128
ROWS = 64
EXT = 24
LAYERS = 8
SLOTS = CAP * TILES
ALL = ("gx", "gy", "af")
YA = ("gy", "af")
BESIDE = (17, 1, -15, 15, -1, -17)
f32 = jnp.float32
bf16 = jnp.bfloat16
i32 = jnp.int32


def iota(shape, axis):
    return lax.broadcasted_iota(i32, shape, axis)


def parts(value):
    high = value.astype(bf16)
    return high, (value - high.astype(f32)).astype(bf16)


def dot_nn(a, b):
    return lax.dot_general(a, b, (((1,), (0,)), ((), ())), preferred_element_type=f32)


def dot_nt(a, b):
    return lax.dot_general(a, b, (((1,), (1,)), ((), ())), preferred_element_type=f32)


def dot_tn(a, b):
    return lax.dot_general(a, b, (((0,), (0,)), ((), ())), preferred_element_type=f32)


def as_row(rows):
    return jnp.concatenate([rows[i : i + 1] for i in range(rows.shape[0])], axis=1)


def as_rows(row):
    return jnp.concatenate([row[:, i : i + 128] for i in range(0, row.shape[1], 128)], axis=0)


def totals(values):
    rows = jnp.concatenate([jnp.sum(value, axis=0, keepdims=True) for value in values], axis=0)
    sums = jnp.sum(rows, axis=1, keepdims=True)
    return [sums[i : i + 1] for i in range(len(values))]


def fold(value):
    return jnp.concatenate([value[:, :128], value[:, 128:]], axis=0)


def unfold(value):
    return jnp.concatenate([value[:4], value[4:]], axis=1)


def seg_code():
    row = iota((8, 128), 0)
    return (row % 4) * 256 + (row // 4) * 128 + iota((8, 128), 1)


def chain(tnext, field):
    lane = iota((8, 128), 1)
    ahead = pltpu.roll(field, 127, 1)
    ahead = jnp.where(lane == 127, pltpu.roll(ahead, 4, 0), ahead)
    behind = pltpu.roll(tnext * field, 1, 1)
    behind = jnp.where(lane == 0, pltpu.roll(behind, 4, 0), behind)
    return tnext * ahead + behind


def owner_hot(owner_row):
    return (iota((TILES, 1024), 0) == owner_row).astype(bf16)


def rank_mask(rank_row):
    return iota((CAP, 1024), 0) == rank_row


def to_slots(values, hot, mask):
    halves = ([], [])
    for value in values:
        row = as_row(value)
        for half, part in zip(halves, parts(row)):
            half.append(jnp.where(mask, part.astype(f32), 0.0).astype(bf16))
    both = jnp.concatenate([jnp.concatenate(half, axis=0) for half in halves], axis=1)
    return dot_nt(both, jnp.concatenate([hot, hot], axis=1))


def look_up(table, row, lane):
    out = jnp.zeros(row.shape, f32)
    for r in range(table.shape[0]):
        picked = jnp.take_along_axis(jnp.broadcast_to(table[r : r + 1], row.shape), lane, axis=1, mode="promise_in_bounds")
        out = jnp.where(row == r, picked, out)
    return out


def find(table, index):
    return look_up(table, index >> 7, index & 127)


def swap_x(block):
    return jnp.swapaxes(block, 0, 1)


def cell_hot(index_row, low=0, high=ROWS):
    count = index_row.shape[1]
    columns = iota((128, count), 0) == (index_row & 127)
    rows = iota((high - low, count), 0) == (index_row >> 7) - low
    return columns.astype(bf16), rows.astype(bf16)


def scatter(tables, columns, rows):
    height = rows.shape[0]
    stacked = []
    for table in tables:
        for part in parts(table):
            row = as_row(part.astype(f32))
            tall = jnp.broadcast_to(row, (16, row.shape[1])).astype(bf16)
            stacked.append(rows * jnp.concatenate([tall] * (height // 16), axis=0))
    sums = dot_nt(jnp.concatenate(stacked, axis=0), columns)
    return [
        (sums[2 * i * height : (2 * i + 1) * height] + sums[(2 * i + 1) * height : (2 * i + 2) * height]).reshape(-1, 8, 128)
        for i in range(len(tables))
    ]


def side_rows(side, count):
    height = (count + 1) // 2 * 16
    return ((0, ROWS), (ROWS - height, ROWS), (0, height))[0 if side == 1 else 1 + side // 2]


def gather_wide(sums, count):
    left, middle, right = sums
    if count == 0:
        return middle
    return jnp.concatenate([left[left.shape[0] - count :], middle, right[:count]], axis=0)


def scatter_wide(tables, late, columns_ref, rows_ref, count):
    found = []
    for side in range(3):
        if side != 1 and count == 0:
            found.append([None] * len(tables))
            continue
        low, high = side_rows(side, count)
        sums = scatter([table[side] for table in tables], columns_ref[side], rows_ref[side, low:high])
        index = as_row(late[side][:4].astype(i32) - 1)
        sums[-1] = sums[-1] + scatter([late[side][4:]], *cell_hot(index, low, high))[0]
        found.append(sums)
    return [gather_wide([found[side][i] for side in range(3)], count) for i in range(len(tables))]


def faces_of(field):
    rows = iota((16, 128), 0)
    lanes = iota((16, 128), 1)
    pick = (((rows == 0) & (lanes == 0)) | ((rows == 1) & (lanes == 127))).astype(bf16)
    both = dot_nt(jnp.concatenate([pick, pick], axis=1), jnp.concatenate(parts(field), axis=1))
    return both[0:1], both[1:2]


def columns_of(left, right):
    width = left.shape[1]
    held = [part.astype(f32) for row in (left, right) for part in parts(row)]
    held = jnp.concatenate(held + [jnp.zeros((12, width), f32)], axis=0).astype(bf16)
    rows = iota((16, 128), 0)
    lanes = iota((16, 128), 1)
    place = (((rows < 2) & (lanes == 0)) | ((rows >= 2) & (rows < 4) & (lanes == 127))).astype(bf16)
    return dot_tn(held, place)


def up_y(v, halo):
    return jnp.where(iota(v.shape, 2) == 127, halo, pltpu.roll(v, 127, 2))


def down_y(v, first):
    return jnp.where(iota(v.shape, 2) == 0, first, pltpu.roll(v, 1, 2))


def stencil(tx_up, tx_down, ty, tz, ty_first, field, halo):
    middle = field[1:-1]
    out = tx_up * field[2:] + tx_down * field[:-2]
    out = out + ty * up_y(middle, halo) + down_y(ty * middle, ty_first * halo)
    return out + tz * pltpu.roll(middle, 7, 1) + pltpu.roll(tz * middle, 1, 1)


def harmonic(first, second):
    both = first + second
    return jnp.where(both > 0.0, 2.0 * first * second / jnp.where(both > 0.0, both, 1.0), 0.0)


def read_faces(me, got_ref, start, width, across=0):
    along = me & 15
    line = (me >> 4) + across // 16
    inside = (line >= 0) & (line < 8)
    before = got_ref[jnp.clip(me + across - 1, 0, TILES - 1), :, start : start + width]
    after = got_ref[jnp.clip(me + across + 1, 0, TILES - 1), :, start : start + width]
    return jnp.where(inside & (along > 0), before, 0.0), jnp.where(inside & (along < 15), after, 0.0)


def put_faces(me, out_ref, start, first, last, across=0):
    width = first.shape[1]
    for at, face in ((me + across - 1, first), (me + across + 1, last)):
        out_ref[jnp.where((at >= 0) & (at < TILES), at, me), :, start : start + width] = face


def edge_codes(delta_ref, to_ref, b):
    block = b + delta_ref[b]
    code = block * 256 + to_ref[b]
    return jnp.where(block < 4, code, -1), jnp.where(block >= 4, code - 1024, -1)


def spread(rows, shift):
    lane = iota(rows.shape, 1)
    inside = (lane >= shift) if shift > 0 else (lane < TILES + shift)
    return jnp.where(inside, pltpu.roll(rows, shift % TILES, 1), 0.0)


def store_slots(out_ref, rows):
    for i in range(0, rows.shape[0], 128):
        part = rows[i : i + 128].T
        out_ref[:, 0, i : i + part.shape[1]] = part


def load_slots(got_ref, count):
    return jnp.concatenate([got_ref[:, 0, i : i + 128].T for i in range(0, count, 128)], axis=0)


def begin_kernel(
    me_ref, delta_ref, from_ref, to_ref, trans_ref, well_tile_ref, well_cell_ref, well_rate_ref, *refs
):
    given, (out_ref, seg_ref), held, sems = refs[:10], refs[10:12], refs[12:22], refs[22]
    copies = [pltpu.make_async_copy(a, b, sems.at[i]) for i, (a, b) in enumerate(zip(given, held))]
    for copy in copies:
        copy.start()
    for copy in copies:
        copy.wait()
    tile_ref, layer_ref, cell_ref, press_frac_ref, accum_ref, chain_ref, mf_ref, fm_ref, press_ref, cond_ref = held
    me = me_ref[0]
    code = seg_code()
    owner = fold(tile_ref[...])
    owner_row = as_row(owner)
    hot = owner_hot(owner_row)
    before = (iota((128, 128), 0) < iota((128, 128), 1)).astype(bf16)
    base = jnp.zeros((TILES, 1), f32)
    ranks = []
    for c in range(8):
        part = hot[:, c * 128 : (c + 1) * 128]
        wide = part.astype(f32)
        count = dot_nn(part, before) + base
        ranks.append(jnp.sum(wide * count, axis=0, keepdims=True))
        base = base + jnp.sum(wide, axis=1, keepdims=True)
    rank_row = jnp.concatenate(ranks, axis=1).astype(i32)
    rank = as_rows(rank_row)
    mask = rank_mask(rank_row)

    press = fold(press_frac_ref[...])
    fm = fold(fm_ref[...])
    mf = fold(mf_ref[...])
    last = code % 256 == 255
    tnext = jnp.where(last, 0.0, fold(chain_ref[...]))
    tprev = pltpu.roll(tnext, 1, 1)
    tprev = jnp.where(iota((8, 128), 1) == 0, pltpu.roll(tprev, 4, 0), tprev)
    diag = fold(accum_ref[...]) + tnext + tprev + fm
    inverse = 1.0 / diag
    partial = diag * press - chain(tnext, press)
    heres = [edge_codes(delta_ref, to_ref, b)[0] for b in range(4)]
    for b, picked in enumerate(totals([jnp.where(code == here, press, 0.0) for here in heres])):
        at = code == b * 256 + from_ref[b]
        partial = partial - jnp.where(at, trans_ref[b] * picked, 0.0)
    cell = fold(cell_ref[...])
    where_cell = ((((cell >> 7) * 8 + fold(layer_ref[...])) << 7) + (cell & 127) + 1).astype(f32)
    position = (iota((8, 128), 0) * 128 + iota((8, 128), 1) + 1).astype(f32)
    slots = to_slots([where_cell, mf * press, fm * inverse * fm, fm * inverse * mf, position], hot, mask)
    inverse_index, slots = slots[64:80], slots[:64]
    place = (owner * CAP + rank).astype(f32)
    rows = []
    for b in range(4):
        _, there = edge_codes(delta_ref, to_ref, b)
        at = code == b * 256 + from_ref[b]
        gain = trans_ref[b] * inverse
        rows.append(jnp.where(iota((1, 128), 1) == 0, there.astype(f32), 0.0))
        for value in (place, where_cell, gain * fm, gain * partial, gain * trans_ref[b], gain * mf, code.astype(f32), gain):
            rows.append(jnp.sum(jnp.where(at, value, 0.0), axis=0, keepdims=True))
        rows.append(jnp.zeros((3, 128), f32))
    edges = [jnp.broadcast_to(jnp.sum(jnp.concatenate(rows, axis=0), axis=1, keepdims=True), (48, 128))]
    rows = [spread(slots, 16), slots, spread(slots, -16)] + edges
    rows += [spread(slots[:CAP], shift) for shift in BESIDE] + [jnp.zeros((48, 128), f32)]
    store_slots(out_ref, jnp.concatenate(rows, axis=0))
    first_face, last_face = faces_of(jnp.concatenate([swap_x(ref[...]).reshape(ROWS, 128) for ref in (press_ref, cond_ref)], axis=0))
    for across in (-16, 0, 16):
        put_faces(me, out_ref, 384, first_face, last_face, across)
    for i, value in enumerate((tnext, inverse, partial, fm, mf, owner.astype(f32), rank.astype(f32), press)):
        seg_ref[i] = value
    for i in range(2):
        seg_ref[8 + i] = inverse_index[8 * i : 8 * i + 8] - 1.0
    lane = iota((8, 128), 1)
    own = jnp.zeros((8, 128), f32)
    for b in range(4):
        here, there = edge_codes(delta_ref, to_ref, b)
        for i, value in enumerate((b * 256 + from_ref[b], here, there)):
            own = jnp.where(lane == 8 * b + i, value.astype(f32), own)
        own = jnp.where(lane == 8 * b + 3, trans_ref[b], own)
    seg_ref[10] = own
    plane_x = iota((EXT, 128), 0) + ((me >> 4) - 1) * 8
    plane_y = iota((EXT, 128), 1) + (me & 15) * 128
    source = jnp.zeros((EXT, 128), f32)
    for w in range(well_tile_ref.shape[0]):
        tile = well_tile_ref[w]
        cell = well_cell_ref[w]
        at = (plane_x == (tile >> 4) * 8 + (cell >> 7)) & (plane_y == (tile & 15) * 128 + (cell & 127))
        source = source + jnp.where(at, well_rate_ref[w], 0.0)
    for i in range(3):
        seg_ref[11 + i] = source[8 * i : 8 * i + 8]
    seg_ref[14] = where_cell


def edge_in(row, k, i):
    at = 64 + 12 * k + i
    return row[:, at : at + 1]


def cells_kernel(
    me_ref,
    got_ref, middle_ref, inside_ref, across_ref, seg_ref,
    out_ref, cells_ref, field_ref, index_ref, columns_ref, rows_ref, edge_ref, beside_ref, res_ref,
):
    me = me_ref[0]
    slots = load_slots(got_ref, 384)
    even = ((me >> 4) & 1) == 0
    press, cond, accum = (
        jnp.concatenate([swap_x(part) for part in (jnp.where(even, b, a), middle_ref[i], jnp.where(even, a, b))], axis=0)
        for i, a, b in ((i, inside_ref[i], across_ref[i]) for i in range(3))
    )
    sums = []
    for side in range(3):
        table = slots[side * 64 : side * 64 + 64]
        index = table[:CAP].astype(i32) - 1
        if side == 1:
            index_ref[...] = index
            own = index
        columns, rows = cell_hot(as_row(index))
        columns_ref[side] = columns
        rows_ref[side] = rows
        sums.append(scatter([table[16:32], table[32:48], table[48:64]], columns, rows))
    flow, weight, mirror = (jnp.concatenate([sums[side][i] for side in range(3)], axis=0) for i in range(3))
    beside = slots[240:336].astype(i32) - 1
    along = me & 15
    for i, (there, column) in enumerate(((along > 0, 127), (along < 15, 0))):
        part = beside[48 * i : 48 * i + 48]
        beside_ref[48 * i : 48 * i + 48] = jnp.where(there & (part >= 0) & ((part & 127) == column), part >> 7, -1)

    halos = [columns_of(*read_faces(me, got_ref, 384, 2 * ROWS, across)) for across in (-16, 0, 16)]
    press_halo = jnp.concatenate([halo[:ROWS].reshape(8, 8, 128) for halo in halos], axis=0)
    cond_halo = jnp.concatenate([halo[ROWS:].reshape(8, 8, 128) for halo in halos], axis=0)
    wide = (EXT, 8, 128)
    tx = harmonic(cond[:-1], cond[1:])
    ty = harmonic(cond, up_y(cond, cond_halo))
    tz = 0.5 * harmonic(cond, jnp.where(iota(wide, 1) == 7, 0.0, pltpu.roll(cond, 7, 1)))
    ty_first = jnp.where(iota(wide, 2) == 0, harmonic(cond, cond_halo), 0.0)
    diag = accum + ty + down_y(ty, ty_first) + tz + pltpu.roll(tz, 1, 1)
    diag = diag[1:-1] + tx[1:] + tx[:-1]
    inverse = jnp.where(diag > 0.0, 1.0 / jnp.where(diag > 0.0, diag, 1.0), 0.0)
    source = jnp.concatenate([seg_ref[11 + i] for i in range(3)], axis=0)

    res = diag * press[1:-1] - flow[1:-1] - source.reshape(EXT, 1, 128)[1:-1]
    res = res - stencil(tx[1:], tx[:-1], ty[1:-1], tz[1:-1], ty_first[1:-1], press, press_halo[1:-1])
    field = inverse * res
    cells_ref[0, : EXT - 1] = tx
    for i, value in ((1, ty), (2, tz), (3, ty_first), (6, weight * press), (7, mirror)):
        cells_ref[i] = value
    cells_ref[4, 1 : EXT - 1] = inverse
    cells_ref[5, 1 : EXT - 1] = res
    field_ref[...] = field
    res_ref[...] = swap_x(res[7:15])

    code = seg_code().astype(f32)
    _, inverse_f, partial, fm, _, owner, _, press_f = (seg_ref[i] for i in range(8))
    edge = jnp.where(me > 0, got_ref[before(me), :, 128:256], -1.0)
    lane = iota((1, 128), 1)
    cells, terms, picks, found = [], [], [], []
    ends = [code == edge_in(edge, k, 0) for k in range(4)]
    wanted = (press_f, owner, seg_ref[14], fm * inverse_f)
    sums = totals([jnp.where(at, value, 0.0) for at in ends for value in wanted])
    for k in range(4):
        picked = sums[4 * k]
        at = (lane == (edge_in(edge, k, 1).astype(i32) >> 4)) & (edge_in(edge, k, 0) >= 0.0)
        cells.append(jnp.where(at, edge_in(edge, k, 2), 0.0))
        terms.append(jnp.where(at, -edge_in(edge, k, 3) * picked, 0.0))
        picks.append(jnp.broadcast_to(picked, (1, 128)))
        found.append(sums[4 * k + 1 : 4 * k + 4])
    for k in range(4):
        edge = jnp.where(lane == 64 + 12 * k + 4, edge - edge_in(edge, k, 5) * sums[4 * k], edge)
    edge_ref[...] = jnp.broadcast_to(edge, (8, 128))
    late = jnp.concatenate(cells + terms, axis=0)
    position = jnp.concatenate([seg_ref[8], seg_ref[9]], axis=0).astype(i32)
    first = find(fm * inverse_f * partial, position)

    taken = [find(press[8:16].reshape(ROWS, 128), own), find(own_tile(field, 1), own)]
    rows = taken + [spread(taken[0], 1)]
    rows += [spread(first, 16), first, spread(first, -16), spread(late, 16), late, spread(late, -16)]
    store_slots(out_ref, jnp.concatenate(rows + picks + [jnp.zeros((4, 128), f32)], axis=0))
    put_faces(me, out_ref, FIRST, *faces_of(field[1:-1].reshape(-1, 128)))
    put_faces(me, out_ref, FIRST_INVERSE, *faces_of(inverse[3:19].reshape(-1, 128)))
    put_entries(out_ref, before(me), FIRST_ENDS, [end for ends in found for end in ends])


def put_entries(out_ref, at, start, entries):
    lane = iota((1, len(entries)), 1)
    row = jnp.zeros(lane.shape, f32)
    for i, entry in enumerate(entries):
        row = jnp.where(lane == i, entry, row)
    out_ref[at, :, start : start + len(entries)] = row


def get_entries(got_ref, at, start, count):
    row = got_ref[at, :, start : start + count]
    return [row[:, i : i + 1] for i in range(count)]


def before(me):
    return jnp.maximum(me - 1, 0)


def after(me):
    return jnp.minimum(me + 1, TILES - 1)


FIRST = 128
FIRST_ENDS = FIRST + 160
FIRST_INVERSE = FIRST_ENDS + 16
WIDE = 232
SLIM = 128
SLIM_TWO = 248


def wide_lanes(k):
    entries = WIDE + 8 * (22 - 2 * k)
    return entries, entries + 4


def own_edges(seg_ref):
    own = seg_ref[10][0:1]
    return [[own[:, 8 * b + i : 8 * b + i + 1] for b in range(4)] for i in range(4)]


def edge_terms(code, edges, frac):
    starts, _, _, factors = edges
    sums = totals([jnp.where(code == start, frac, 0.0) for start in starts])
    return [factor * picked for factor, picked in zip(factors, sums)]


def arrive(code, targets, terms):
    gain = jnp.zeros(code.shape, f32)
    for target, term in zip(targets, terms):
        gain = gain + jnp.where(code == target, term, 0.0)
    return gain


def late_rows(edges, ends, terms):
    lane = iota((1, 128), 1)
    cells, values = [], []
    for there, (tile, cell, weight), term in zip(edges[2], ends, terms):
        at = (lane == tile.astype(i32)) & (there >= 0.0)
        cells.append(jnp.where(at, cell, 0.0))
        values.append(jnp.where(at, weight * term, 0.0))
    return jnp.concatenate(cells + values, axis=0)


def to_three(rows):
    return [spread(rows, 16), rows, spread(rows, -16)]


def own_tile(field, k):
    return field[8 - k : 16 - k].reshape(ROWS, 128)


def starts_of(edge, table):
    place = (iota((CAP, 128), 1) * CAP + iota((CAP, 128), 0)).astype(f32)
    return totals([jnp.where(place == edge_in(edge, k, 1), table, 0.0) for k in range(4)])


def advance(cells_ref, k, field, halo, flow):
    low, high = k + 1, EXT - 1 - k
    ty, tz, ty_first, inverse, res = (cells_ref[i, low:high] for i in range(1, 6))
    tx_up, tx_down = cells_ref[0, low:high], cells_ref[0, low - 1 : high - 1]
    return inverse * (res + stencil(tx_up, tx_down, ty, tz, ty_first, field, halo) + flow)


def wide_halo(me, got_ref, start, count):
    return columns_of(*read_faces(me, got_ref, start, 8 * count)).reshape(count, 8, 128)


def ends_of(ends_ref):
    held = ends_ref[0:1]
    return [[held[:, 3 * k + i : 3 * k + i + 1] for i in range(3)] for k in range(4)]


def send_wide(me, out_ref, k, code, edges, ends, seg_ref, cells_ref, index_ref, field, frac, resf):
    tnext, inverse_f, fm = seg_ref[0], seg_ref[1], seg_ref[3]
    terms = edge_terms(code, edges, frac)
    ahead = inverse_f * (resf + chain(tnext, frac) + arrive(code, edges[1], terms))
    part = advance(cells_ref, k, field, jnp.zeros((22 - 2 * k, 8, 128), f32), 0.0)
    position = jnp.concatenate([seg_ref[8], seg_ref[9]], axis=0).astype(i32)
    now = find(fm * frac, position)
    rows = [find(own_tile(field, k), index_ref[...])] + to_three(now) + to_three(find(fm * ahead, position))
    rows += to_three(late_rows(edges, ends, terms)) + [spread(now, shift) for shift in BESIDE]
    store_slots(out_ref, jnp.concatenate(rows + [jnp.zeros((24, 128), f32)], axis=0))
    entries, further = wide_lanes(k)
    put_faces(me, out_ref, WIDE, *faces_of(field[1:-1].reshape(-1, 128)))
    put_faces(me, out_ref, further, *faces_of(part[1:-1].reshape(-1, 128)))
    put_entries(out_ref, jnp.where(me + 1 < TILES, me + 1, me), entries, terms)


def first_kernel(
    me_ref, got_ref, cells_ref, field_ref, index_ref, columns_ref, rows_ref, seg_ref, edge_ref,
    out_ref, new_field_ref, new_frac_ref, resf_ref, ends_ref, halo_inverse_ref, res_fracture_ref,
):
    me = me_ref[0]
    slots = load_slots(got_ref, 128)
    code = seg_code().astype(f32)
    tnext, inverse_f, partial, fm, mf, owner, rank = (seg_ref[i] for i in range(7))
    owner = owner.astype(i32)
    rank = rank.astype(i32)
    edge = edge_ref[0:1]
    edges = own_edges(seg_ref)
    starts, targets, nexts, factors = edges

    resf = partial - fm * look_up(slots[0:16], rank, owner)
    picks = get_entries(got_ref, after(me), 120, 4)
    for b in range(4):
        at = (code == starts[b]) & (nexts[b] >= 0.0)
        resf = resf - jnp.where(at, factors[b] * picks[b], 0.0)
    frac = inverse_f * resf
    terms = edge_terms(code, edges, frac)
    begun = starts_of(edge, slots[32:48])
    coming = [edge_in(edge, k, 4) - edge_in(edge, k, 3) * begun[k] for k in range(4)]
    gain = resf + chain(tnext, frac) + mf * look_up(slots[16:32], rank, owner)
    gain = gain + arrive(code, targets, terms) + arrive(code, [edge_in(edge, k, 0) for k in range(4)], coming)
    frac = inverse_f * gain
    late = [slots[96 + 8 * side : 104 + 8 * side] for side in range(3)]
    first = [slots[48 + side * CAP : 64 + side * CAP] for side in range(3)]
    (flow,) = scatter_wide([first], late, columns_ref, rows_ref, 6)
    field = advance(cells_ref, 1, field_ref[...], wide_halo(me, got_ref, FIRST, 20), flow - cells_ref[6, 2:22])
    new_field_ref[...] = field
    new_frac_ref[...] = frac
    resf_ref[...] = resf
    res_fracture_ref[...] = unfold(resf)
    halo_inverse_ref[...] = wide_halo(me, got_ref, FIRST_INVERSE, 16)
    ends = get_entries(got_ref, after(me), FIRST_ENDS, 12)
    ends = [ends[3 * k : 3 * k + 3] for k in range(4)]
    lane = iota((8, 128), 1)
    held = jnp.zeros((8, 128), f32)
    for k in range(4):
        for i in range(3):
            held = jnp.where(lane == 3 * k + i, ends[k][i], held)
    ends_ref[...] = held

    send_wide(me, out_ref, 2, code, edges, ends, seg_ref, cells_ref, index_ref, field, frac, resf)


def even_kernel(
    k, me_ref, got_ref, cells_ref, field_ref, index_ref, columns_ref, rows_ref, seg_ref, edge_ref,
    frac_ref, resf_ref, ends_ref, halo_inverse_ref, beside_ref,
    out_ref, third_ref, new_field_ref, new_frac_ref,
):
    me = me_ref[0]
    slots = load_slots(got_ref, 256)
    code = seg_code().astype(f32)
    tnext, inverse_f, _, fm, mf, owner, rank = (seg_ref[i] for i in range(7))
    edge = edge_ref[0:1]
    edges = own_edges(seg_ref)
    targets = edges[1]
    resf = resf_ref[...]
    frac = frac_ref[...]
    entries, further = wide_lanes(k)
    coming = get_entries(got_ref, before(me), entries, 4)
    gain = resf + chain(tnext, frac) + mf * look_up(slots[0:16], rank.astype(i32), owner.astype(i32))
    gain = gain + arrive(code, targets, edge_terms(code, edges, frac))
    gain = gain + arrive(code, [edge_in(edge, b, 0) for b in range(4)], coming)
    frac = inverse_f * gain
    terms = edge_terms(code, edges, frac)
    ahead = inverse_f * (resf + chain(tnext, frac) + arrive(code, targets, terms))
    new_frac_ref[...] = frac

    tables = [[slots[first + side * CAP : first + CAP + side * CAP] for side in range(3)] for first in (16, 64)]
    late = [slots[112 + 8 * side : 120 + 8 * side] for side in range(3)]
    flow, later = scatter_wide(tables, late, columns_ref, rows_ref, 7 - k)
    beside = []
    lane = iota((ROWS, 128), 1)
    level = iota((ROWS, 128), 0)
    for side in range(3):
        column = jnp.zeros((ROWS, 128), f32)
        for i, at in enumerate((0, 127)):
            first = 48 * i + CAP * side
            held = jnp.zeros((ROWS, 128), f32)
            for r in range(first, first + CAP):
                held = held + jnp.where(level == beside_ref[r : r + 1], slots[136 + r : 137 + r], 0.0)
            column = jnp.where(lane == at, jnp.sum(held, axis=1, keepdims=True), column)
        beside.append(column.reshape(8, 8, 128))
    beside = jnp.concatenate(beside, axis=0)[k + 2 : 22 - k]
    second = field_ref[...]
    third = advance(cells_ref, k, second, wide_halo(me, got_ref, WIDE, 22 - 2 * k), flow)
    inner = second[2:-2]
    lane = iota(inner.shape, 2)
    joint = jnp.where(lane == 0, cells_ref[3, k + 2 : 22 - k], jnp.where(lane == 127, cells_ref[1, k + 2 : 22 - k], 0.0))
    halo = wide_halo(me, got_ref, further, 20 - 2 * k) + halo_inverse_ref[k - 2 : 18 - k] * (joint * inner + beside)
    field = advance(cells_ref, k + 1, third, halo, later[1:-1] + cells_ref[7, k + 2 : 22 - k] * inner)
    third_ref[...] = third
    new_field_ref[...] = field

    position = jnp.concatenate([seg_ref[8], seg_ref[9]], axis=0).astype(i32)
    ends = ends_of(ends_ref)
    own_third = find(own_tile(third, k + 1), index_ref[...])
    rows = [own_third, find(own_tile(field, k + 2), index_ref[...]), spread(own_third, 1)] + to_three(find(fm * ahead, position))
    rows += to_three(late_rows(edges, ends, terms))
    store_slots(out_ref, jnp.concatenate(rows + [jnp.zeros((8, 128), f32)], axis=0))
    put_faces(me, out_ref, SLIM, *faces_of(field[1:-1].reshape(-1, 128)))
    to_next = jnp.where(me + 1 < TILES, me + 1, me)
    put_entries(out_ref, to_next, SLIM + 8 * (18 - 2 * k), terms + edge_terms(code, edges, ahead))
    put_entries(out_ref, jnp.where(me + 2 < TILES, me + 2, me), SLIM_TWO, terms + edges[2])


def odd_kernel(
    k, final, me_ref, got_ref, cells_ref, field_ref, index_ref, columns_ref, rows_ref, seg_ref, edge_ref,
    frac_ref, resf_ref, ends_ref, third_ref, *outs,
):
    me = me_ref[0]
    slots = load_slots(got_ref, 128)
    code = seg_code().astype(f32)
    tnext, inverse_f, _, _, mf, owner, rank = (seg_ref[i] for i in range(7))
    owner = owner.astype(i32)
    rank = rank.astype(i32)
    edge = edge_ref[0:1]
    edges = own_edges(seg_ref)
    targets = edges[1]
    resf = resf_ref[...]
    frac = frac_ref[...]
    coming = get_entries(got_ref, before(me), SLIM + 8 * (22 - 2 * k), 8)
    two = jnp.where(me > 1, got_ref[jnp.maximum(me - 2, 0), :, 128:256], -1.0)
    lane = iota((1, 128), 1)
    codes = jnp.where((lane >= SLIM_TWO - 128) & (lane < SLIM_TWO - 124), pltpu.roll(two, 124, 1), -2.0)
    meets = jnp.concatenate([jnp.where(codes == edge_in(edge, b, 7), two, 0.0) for b in range(4)], axis=0)
    meets = jnp.sum(meets, axis=1, keepdims=True)
    begun = starts_of(edge, slots[32:48])
    heres = [edge_in(edge, b, 0) for b in range(4)]
    gain = resf + chain(tnext, frac) + mf * look_up(slots[0:16], rank, owner)
    gain = gain + arrive(code, targets, edge_terms(code, edges, frac))
    frac = inverse_f * (gain + arrive(code, heres, coming[:4]))
    terms = [
        coming[4 + b] + edge_in(edge, b, 6) * begun[b] + edge_in(edge, b, 8) * meets[b : b + 1] for b in range(4)
    ]
    gain = resf + chain(tnext, frac) + mf * look_up(slots[16:32], rank, owner)
    gain = gain + arrive(code, targets, edge_terms(code, edges, frac))
    frac = inverse_f * (gain + arrive(code, heres, terms))

    late = [slots[96 + 8 * side : 104 + 8 * side] for side in range(3)]
    tables = [[slots[48 + side * CAP : 64 + side * CAP] for side in range(3)]]
    (flow,) = scatter_wide(tables, late, columns_ref, rows_ref, 7 - k)
    flow = flow + cells_ref[7, k + 1 : 23 - k] * third_ref[2:-2]
    field = advance(cells_ref, k, field_ref[...], wide_halo(me, got_ref, SLIM, 22 - 2 * k), flow)
    if final:
        adj_matrix_ref, adj_fracture_ref = outs
        adj_matrix_ref[...] = swap_x(field)
        adj_fracture_ref[...] = unfold(frac)
        return
    out_ref, new_field_ref, new_frac_ref = outs
    new_field_ref[...] = field
    new_frac_ref[...] = frac
    send_wide(me, out_ref, k + 1, code, edges, ends_of(ends_ref), seg_ref, cells_ref, index_ref, field, frac, resf)


def call(kernel, name, scalars, arrays, outs, space=pltpu.VMEM, scratch=(), limit=20 * 1024 * 1024):
    spec = [pl.BlockSpec(memory_space=pltpu.SMEM)] * len(scalars)
    spec += [pl.BlockSpec(memory_space=space)] * len(arrays)
    return pl.pallas_call(
        kernel,
        name=name,
        out_shape=[jax.ShapeDtypeStruct(shape, kind) for shape, kind in outs],
        in_specs=spec,
        out_specs=[pl.BlockSpec(memory_space=pltpu.VMEM)] * len(outs),
        scratch_shapes=list(scratch),
        compiler_params=pltpu.CompilerParams(vmem_limit_bytes=limit),
    )(*scalars, *arrays)


def exchange(message):
    return lax.all_to_all(message, ALL, split_axis=0, concat_axis=0, tiled=True)


def swapped(block, first):
    pairs = [(i, i + 1) for i in range(first, lax.axis_size("gx") - 1, 2)]
    return lax.ppermute(block, "gx", pairs + [(j, i) for i, j in pairs])


def body(
    press_matrix, cond_matrix, accum_matrix, press_frac, accum_frac, trans_chain, couple_mf, couple_fm,
    conn_tile, conn_layer, conn_cell, inter_delta, inter_from, inter_to, inter_trans, well_tile, well_cell, well_rate,
):
    me = lax.axis_index(ALL).astype(i32).reshape(1)
    stacked = jnp.stack([press_matrix, cond_matrix, accum_matrix])
    inside = swapped(stacked, 0)
    across = swapped(stacked, 1)
    wide = (EXT, 8, 128)
    tile = (LAYERS, 8, 128)
    seg = (8, 128)

    given = (conn_tile, conn_layer, conn_cell, press_frac, accum_frac, trans_chain, couple_mf, couple_fm, press_matrix, cond_matrix)
    message, segs = call(
        begin_kernel,
        "begin",
        (me, inter_delta, inter_from, inter_to, inter_trans, well_tile, well_cell, well_rate),
        given,
        [((TILES, 1, 512), f32), ((15, *seg), f32)],
        pl.ANY,
        [pltpu.VMEM(a.shape, a.dtype) for a in given] + [pltpu.SemaphoreType.DMA((len(given),))],
        64 * 1024 * 1024,
    )
    got = exchange(message)
    message, cells, field, index, columns, rows, edge, beside, res_matrix = call(
        cells_kernel,
        "cells",
        (me,),
        (got, stacked, inside, across, segs),
        [((TILES, 1, 512), f32), ((8, *wide), f32), ((22, 8, 128), f32), ((CAP, 128), i32), ((3, 128, SLOTS), bf16),
         ((3, ROWS, SLOTS), bf16), (seg, f32), ((96, 128), i32), (tile, f32)],
    )
    kept = (index, columns, rows, segs, edge)

    def after_sweeps(k):
        return ((EXT - 2 * k, 8, 128), f32)

    wide_message = ((TILES, 1, 512), f32)
    slim_message = ((TILES, 1, 256), f32)
    got = exchange(message)
    message, field, frac, resf, ends, halo_inverse, res_fracture = call(
        first_kernel,
        "first",
        (me,),
        (got, cells, field, *kept),
        [wide_message, after_sweeps(2), (seg, f32), (seg, f32), (seg, f32), ((16, 8, 128), f32), ((4, 256), f32)],
    )
    for k, final in ((2, False), (5, True)):
        got = exchange(message)
        message, third, field, frac = call(
            functools.partial(even_kernel, k),
            "even",
            (me,),
            (got, cells, field, *kept, frac, resf, ends, halo_inverse, beside),
            [slim_message, after_sweeps(k + 1), after_sweeps(k + 2), (seg, f32)],
        )
        got = exchange(message)
        outs = [(tile, f32), ((4, 256), f32)] if final else [wide_message, after_sweeps(k + 3), (seg, f32)]
        results = call(
            functools.partial(odd_kernel, k + 2, final),
            "odd",
            (me,),
            (got, cells, field, *kept, frac, resf, ends, third),
            outs,
        )
        if not final:
            message, field, frac = results
    adj_matrix, adj_fracture = results
    return res_matrix, res_fracture, adj_matrix, adj_fracture


def solution(mesh):
    cells = P(None, "gx", YA)
    segs = P(ALL, None)
    blocks = P(ALL)
    in_specs = (cells,) * 3 + (segs,) * 8 + (blocks,) * 4 + (P(),) * 3
    return jax.shard_map(body, mesh=mesh, in_specs=in_specs, out_specs=(cells, segs, cells, segs), check_vma=False)
```

```python
import functools

import jax
import jax.numpy as jnp
from jax import lax
from jax.experimental import pallas as pl
from jax.experimental.pallas import tpu as pltpu
from jax.sharding import PartitionSpec as P

ITERS = 8
CAP = 16
TILES = 128
ROWS = 64
EXT = 24
LAYERS = 8
SLOTS = CAP * TILES
ALL = ("gx", "gy", "af")
YA = ("gy", "af")
BESIDE = (17, 1, -15, 15, -1, -17)
f32 = jnp.float32
bf16 = jnp.bfloat16
i32 = jnp.int32


def iota(shape, axis):
    return lax.broadcasted_iota(i32, shape, axis)


def parts(value):
    high = value.astype(bf16)
    return high, (value - high.astype(f32)).astype(bf16)


def dot_nn(a, b):
    return lax.dot_general(a, b, (((1,), (0,)), ((), ())), preferred_element_type=f32)


def dot_nt(a, b):
    return lax.dot_general(a, b, (((1,), (1,)), ((), ())), preferred_element_type=f32)


def dot_tn(a, b):
    return lax.dot_general(a, b, (((0,), (0,)), ((), ())), preferred_element_type=f32)


def as_row(rows):
    return jnp.concatenate([rows[i : i + 1] for i in range(rows.shape[0])], axis=1)


def as_rows(row):
    return jnp.concatenate([row[:, i : i + 128] for i in range(0, row.shape[1], 128)], axis=0)


def totals(values):
    rows = jnp.concatenate([jnp.sum(value, axis=0, keepdims=True) for value in values], axis=0)
    sums = jnp.sum(rows, axis=1, keepdims=True)
    return [sums[i : i + 1] for i in range(len(values))]


def fold(value):
    return jnp.concatenate([value[:, :128], value[:, 128:]], axis=0)


def unfold(value):
    return jnp.concatenate([value[:4], value[4:]], axis=1)


def seg_code():
    row = iota((8, 128), 0)
    return (row % 4) * 256 + (row // 4) * 128 + iota((8, 128), 1)


def chain(tnext, field):
    lane = iota((8, 128), 1)
    ahead = pltpu.roll(field, 127, 1)
    ahead = jnp.where(lane == 127, pltpu.roll(ahead, 4, 0), ahead)
    behind = pltpu.roll(tnext * field, 1, 1)
    behind = jnp.where(lane == 0, pltpu.roll(behind, 4, 0), behind)
    return tnext * ahead + behind


def owner_hot(owner_row):
    return (iota((TILES, 1024), 0) == owner_row).astype(bf16)


def rank_mask(rank_row):
    return iota((CAP, 1024), 0) == rank_row


def to_slots(values, hot, mask):
    halves = ([], [])
    for value in values:
        row = as_row(value)
        for half, part in zip(halves, parts(row)):
            half.append(jnp.where(mask, part.astype(f32), 0.0).astype(bf16))
    both = jnp.concatenate([jnp.concatenate(half, axis=0) for half in halves], axis=1)
    return dot_nt(both, jnp.concatenate([hot, hot], axis=1))


def look_up(table, row, lane):
    out = jnp.zeros(row.shape, f32)
    for r in range(table.shape[0]):
        picked = jnp.take_along_axis(jnp.broadcast_to(table[r : r + 1], row.shape), lane, axis=1, mode="promise_in_bounds")
        out = jnp.where(row == r, picked, out)
    return out


def find(table, index):
    return look_up(table, index >> 7, index & 127)


def swap_x(block):
    return jnp.swapaxes(block, 0, 1)


def cell_hot(index_row, low=0, high=ROWS):
    count = index_row.shape[1]
    columns = iota((128, count), 0) == (index_row & 127)
    rows = iota((high - low, count), 0) == (index_row >> 7) - low
    return columns.astype(bf16), rows.astype(bf16)


def scatter(tables, columns, rows):
    height = rows.shape[0]
    stacked = []
    for table in tables:
        for part in parts(table):
            row = as_row(part.astype(f32))
            tall = jnp.broadcast_to(row, (16, row.shape[1])).astype(bf16)
            stacked.append(rows * jnp.concatenate([tall] * (height // 16), axis=0))
    sums = dot_nt(jnp.concatenate(stacked, axis=0), columns)
    return [
        (sums[2 * i * height : (2 * i + 1) * height] + sums[(2 * i + 1) * height : (2 * i + 2) * height]).reshape(-1, 8, 128)
        for i in range(len(tables))
    ]


def side_rows(side, count):
    height = (count + 1) // 2 * 16
    return ((0, ROWS), (ROWS - height, ROWS), (0, height))[0 if side == 1 else 1 + side // 2]


def gather_wide(sums, count):
    left, middle, right = sums
    if count == 0:
        return middle
    return jnp.concatenate([left[left.shape[0] - count :], middle, right[:count]], axis=0)


def scatter_wide(tables, late, columns_ref, rows_ref, count):
    fields = max(len(tables), 1)
    found = []
    for side in range(3):
        if side != 1 and count == 0:
            found.append([None] * fields)
            continue
        low, high = side_rows(side, count)
        index = as_row(late[side][:4].astype(i32) - 1)
        (sums,) = scatter([late[side][4:]], *cell_hot(index, low, high))
        if tables:
            *others, last = scatter([table[side] for table in tables], columns_ref[side], rows_ref[side, low:high])
            found.append([*others, last + sums])
        else:
            found.append([sums])
    return [gather_wide([found[side][i] for side in range(3)], count) for i in range(fields)]


def faces_of(field):
    turned = field.T
    return turned[0:1], turned[127:128]


def columns_of(left, right):
    width = left.shape[1]
    row = iota((128, width), 0)
    return jnp.where(row == 0, left, jnp.where(row == 127, right, 0.0)).T


def up_y(v, halo):
    return jnp.where(iota(v.shape, 2) == 127, halo, pltpu.roll(v, 127, 2))


def down_y(v, first):
    return jnp.where(iota(v.shape, 2) == 0, first, pltpu.roll(v, 1, 2))


def stencil(tx_up, tx_down, ty, tz, ty_first, field, halo):
    middle = field[1:-1]
    out = tx_up * field[2:] + tx_down * field[:-2]
    out = out + ty * up_y(middle, halo) + down_y(ty * middle, ty_first * halo)
    return out + tz * pltpu.roll(middle, 7, 1) + pltpu.roll(tz * middle, 1, 1)


def harmonic(first, second):
    both = first + second
    return jnp.where(both > 0.0, 2.0 * first * second / jnp.where(both > 0.0, both, 1.0), 0.0)


def read_faces(me, got_ref, start, width, across=0):
    along = me & 15
    line = (me >> 4) + across // 16
    inside = (line >= 0) & (line < 8)
    before = got_ref[jnp.clip(me + across - 1, 0, TILES - 1), :, start : start + width]
    after = got_ref[jnp.clip(me + across + 1, 0, TILES - 1), :, start : start + width]
    return jnp.where(inside & (along > 0), before, 0.0), jnp.where(inside & (along < 15), after, 0.0)


def put_faces(me, out_ref, start, first, last, across=0):
    width = first.shape[1]
    for at, face in ((me + across - 1, first), (me + across + 1, last)):
        out_ref[jnp.where((at >= 0) & (at < TILES), at, me), :, start : start + width] = face


def edge_codes(delta_ref, to_ref, b):
    block = b + delta_ref[b]
    code = block * 256 + to_ref[b]
    return jnp.where(block < 4, code, -1), jnp.where(block >= 4, code - 1024, -1)


def spread(rows, shift):
    lane = iota(rows.shape, 1)
    inside = (lane >= shift) if shift > 0 else (lane < TILES + shift)
    return jnp.where(inside, pltpu.roll(rows, shift % TILES, 1), 0.0)


def store_slots(out_ref, rows):
    for i in range(0, rows.shape[0], 128):
        part = rows[i : i + 128].T
        out_ref[:, 0, i : i + part.shape[1]] = part


def load_slots(got_ref, count):
    return jnp.concatenate([got_ref[:, 0, i : i + 128].T for i in range(0, count, 128)], axis=0)


def begin_kernel(me_ref, *refs):
    count = len(refs) // 2 - 2
    given, (out_ref, seg_ref, tile_out_ref), held, sems = refs[:count], refs[count : count + 3], refs[count + 3 : -1], refs[-1]
    copies = [pltpu.make_async_copy(a, b, sems.at[i]) for i, (a, b) in enumerate(zip(given, held))]
    passing = [pltpu.make_async_copy(held[8 + i], tile_out_ref.at[i], sems.at[count + i]) for i in range(3)]
    for copy in copies:
        copy.start()
    for copy in copies:
        copy.wait()
    for copy in passing:
        copy.start()
    tile_ref, layer_ref, cell_ref, press_frac_ref, accum_ref, chain_ref, mf_ref, fm_ref = held[:8]
    press_ref, cond_ref, accum_matrix_ref = held[8:11]
    delta_ref, from_ref, to_ref, trans_ref, well_tile_ref, well_cell_ref, well_rate_ref = held[11:]
    me = me_ref[0]
    code = seg_code()
    owner = fold(tile_ref[...])
    owner_row = as_row(owner)
    hot = owner_hot(owner_row)
    before = (iota((128, 128), 0) < iota((128, 128), 1)).astype(bf16)
    base = jnp.zeros((TILES, 1), f32)
    ranks = []
    for c in range(8):
        part = hot[:, c * 128 : (c + 1) * 128]
        wide = part.astype(f32)
        count = dot_nn(part, before) + base
        ranks.append(jnp.sum(wide * count, axis=0, keepdims=True))
        base = base + jnp.sum(wide, axis=1, keepdims=True)
    rank_row = jnp.concatenate(ranks, axis=1).astype(i32)
    rank = as_rows(rank_row)
    mask = rank_mask(rank_row)

    press = fold(press_frac_ref[...])
    fm = fold(fm_ref[...])
    mf = fold(mf_ref[...])
    last = code % 256 == 255
    tnext = jnp.where(last, 0.0, fold(chain_ref[...]))
    tprev = pltpu.roll(tnext, 1, 1)
    tprev = jnp.where(iota((8, 128), 1) == 0, pltpu.roll(tprev, 4, 0), tprev)
    diag = fold(accum_ref[...]) + tnext + tprev + fm
    inverse = 1.0 / diag
    partial = diag * press - chain(tnext, press)
    heres = [edge_codes(delta_ref, to_ref, b)[0] for b in range(4)]
    for b, picked in enumerate(totals([jnp.where(code == here, press, 0.0) for here in heres])):
        at = code == b * 256 + from_ref[b]
        partial = partial - jnp.where(at, trans_ref[b] * picked, 0.0)
    cell = fold(cell_ref[...])
    where_cell = ((((cell >> 7) * 8 + fold(layer_ref[...])) << 7) + (cell & 127) + 1).astype(f32)
    position = (iota((8, 128), 0) * 128 + iota((8, 128), 1) + 1).astype(f32)
    weight = fm * inverse
    slots = to_slots([where_cell, mf * press, weight * fm, weight * mf, weight * partial, position], hot, mask)
    inverse_index, slots = slots[80:96], slots[:80]
    place = (owner * CAP + rank).astype(f32)
    rows = []
    for b in range(4):
        _, there = edge_codes(delta_ref, to_ref, b)
        at = code == b * 256 + from_ref[b]
        gain = trans_ref[b] * inverse
        rows.append(jnp.where(iota((1, 128), 1) == 0, there.astype(f32), 0.0))
        for value in (place, where_cell, gain * fm, gain * partial, gain * trans_ref[b], gain * mf, code.astype(f32), gain):
            rows.append(jnp.sum(jnp.where(at, value, 0.0), axis=0, keepdims=True))
        rows.append(jnp.zeros((3, 128), f32))
    edges = [jnp.broadcast_to(jnp.sum(jnp.concatenate(rows, axis=0), axis=1, keepdims=True), (48, 128))]
    rows = edges + to_three(slots) + [spread(slots[:CAP], shift) for shift in BESIDE]
    store_slots(out_ref, jnp.concatenate(rows, axis=0))
    first_face, last_face = faces_of(jnp.concatenate([swap_x(ref[...]).reshape(ROWS, 128) for ref in (press_ref, cond_ref)], axis=0))
    for across in (-16, 0, 16):
        put_faces(me, out_ref, 384, first_face, last_face, across)
    for i, value in enumerate((tnext, inverse, partial, fm, mf, owner.astype(f32), rank.astype(f32), press)):
        seg_ref[i] = value
    for i in range(2):
        seg_ref[8 + i] = inverse_index[8 * i : 8 * i + 8] - 1.0
    lane = iota((8, 128), 1)
    own = jnp.zeros((8, 128), f32)
    for b in range(4):
        here, there = edge_codes(delta_ref, to_ref, b)
        for i, value in enumerate((b * 256 + from_ref[b], here, there)):
            own = jnp.where(lane == 8 * b + i, value.astype(f32), own)
        own = jnp.where(lane == 8 * b + 3, trans_ref[b], own)
    seg_ref[10] = own
    plane_x = iota((EXT, 128), 0) + ((me >> 4) - 1) * 8
    plane_y = iota((EXT, 128), 1) + (me & 15) * 128
    source = jnp.zeros((EXT, 128), f32)
    for w in range(well_tile_ref.shape[0]):
        tile = well_tile_ref[w]
        cell = well_cell_ref[w]
        at = (plane_x == (tile >> 4) * 8 + (cell >> 7)) & (plane_y == (tile & 15) * 128 + (cell & 127))
        source = source + jnp.where(at, well_rate_ref[w], 0.0)
    for i in range(3):
        seg_ref[11 + i] = source[8 * i : 8 * i + 8]
    seg_ref[14] = where_cell
    for i, ref in enumerate((press_ref, cond_ref, accum_matrix_ref)):
        seg_ref[15 + 8 * i : 23 + 8 * i] = swap_x(ref[...])
    for copy in passing:
        copy.wait()


def edge_in(row, k, i):
    at = 12 * k + i
    return row[:, at : at + 1]


def cells_kernel(
    me_ref,
    got_ref, inside_ref, across_ref, seg_ref,
    out_ref, cells_ref, field_ref, index_ref, columns_ref, rows_ref, edge_ref, beside_ref, res_ref,
):
    me = me_ref[0]
    slots = load_slots(got_ref, 384)
    even = ((me >> 4) & 1) == 0
    press, cond, accum = (
        jnp.concatenate(
            [swap_x(jnp.where(even, b, a)), seg_ref[15 + 8 * i : 23 + 8 * i], swap_x(jnp.where(even, a, b))], axis=0
        )
        for i, a, b in ((i, inside_ref[i], across_ref[i]) for i in range(3))
    )
    sums = []
    for side in range(3):
        table = slots[48 + side * 80 : 128 + side * 80]
        index = table[:CAP].astype(i32) - 1
        if side == 1:
            index_ref[...] = index
            own = index
        columns, rows = cell_hot(as_row(index))
        columns_ref[side] = columns
        rows_ref[side] = rows
        sums.append(scatter([table[i : i + CAP] for i in range(CAP, 5 * CAP, CAP)], columns, rows))
    flow, weight, mirror, first = (jnp.concatenate([sums[side][i] for side in range(3)], axis=0) for i in range(4))
    beside = slots[288:384].astype(i32) - 1
    along = me & 15
    for i, (there, column) in enumerate(((along > 0, 127), (along < 15, 0))):
        part = beside[48 * i : 48 * i + 48]
        beside_ref[48 * i : 48 * i + 48] = jnp.where(there & (part >= 0) & ((part & 127) == column), part >> 7, -1)

    halos = [columns_of(*read_faces(me, got_ref, 384, 2 * ROWS, across)) for across in (-16, 0, 16)]
    press_halo = jnp.concatenate([halo[:ROWS].reshape(8, 8, 128) for halo in halos], axis=0)
    cond_halo = jnp.concatenate([halo[ROWS:].reshape(8, 8, 128) for halo in halos], axis=0)
    wide = (EXT, 8, 128)
    tx = harmonic(cond[:-1], cond[1:])
    ty = harmonic(cond, up_y(cond, cond_halo))
    tz = 0.5 * harmonic(cond, jnp.where(iota(wide, 1) == 7, 0.0, pltpu.roll(cond, 7, 1)))
    ty_first = jnp.where(iota(wide, 2) == 0, harmonic(cond, cond_halo), 0.0)
    diag = accum + ty + down_y(ty, ty_first) + tz + pltpu.roll(tz, 1, 1)
    diag = diag[1:-1] + tx[1:] + tx[:-1]
    inverse = jnp.where(diag > 0.0, 1.0 / jnp.where(diag > 0.0, diag, 1.0), 0.0)
    source = jnp.concatenate([seg_ref[11 + i] for i in range(3)], axis=0)

    res = diag * press[1:-1] - flow[1:-1] - source.reshape(EXT, 1, 128)[1:-1]
    res = res - stencil(tx[1:], tx[:-1], ty[1:-1], tz[1:-1], ty_first[1:-1], press, press_halo[1:-1])
    field = inverse * res
    cells_ref[0, : EXT - 1] = tx
    for i, value in ((1, ty), (2, tz), (3, ty_first), (6, first - weight * press), (7, mirror)):
        cells_ref[i] = value
    cells_ref[4, 1 : EXT - 1] = inverse
    cells_ref[5, 1 : EXT - 1] = res
    field_ref[...] = field
    res_ref[...] = swap_x(res[7:15])

    code = seg_code().astype(f32)
    _, inverse_f, partial, fm, _, owner, _, press_f = (seg_ref[i] for i in range(8))
    edge = jnp.where(me > 0, got_ref[before(me), :, 0:128], -1.0)
    lane = iota((1, 128), 1)
    cells, terms, picks, found = [], [], [], []
    ends = [code == edge_in(edge, k, 0) for k in range(4)]
    wanted = (press_f, owner, seg_ref[14], fm * inverse_f)
    sums = totals([jnp.where(at, value, 0.0) for at in ends for value in wanted])
    for k in range(4):
        picked = sums[4 * k]
        at = (lane == (edge_in(edge, k, 1).astype(i32) >> 4)) & (edge_in(edge, k, 0) >= 0.0)
        cells.append(jnp.where(at, edge_in(edge, k, 2), 0.0))
        terms.append(jnp.where(at, -edge_in(edge, k, 3) * picked, 0.0))
        picks.append(jnp.broadcast_to(picked, (1, 128)))
        found.append(sums[4 * k + 1 : 4 * k + 4])
    for k in range(4):
        edge = jnp.where(lane == 12 * k + 4, edge - edge_in(edge, k, 5) * sums[4 * k], edge)
    edge_ref[...] = jnp.broadcast_to(edge, (8, 128))
    late = jnp.concatenate(cells + terms, axis=0)

    taken = [find(press[8:16].reshape(ROWS, 128), own), find(own_tile(field, 1), own)]
    rows = taken + [spread(taken[0], 1)]
    store_slots(out_ref, jnp.concatenate(rows + to_three(late) + picks + [jnp.zeros((52, 128), f32)], axis=0))
    put_faces(me, out_ref, FIRST, *faces_of(field[1:-1].reshape(-1, 128)))
    put_faces(me, out_ref, FIRST_INVERSE, *faces_of(inverse[3:19].reshape(-1, 128)))
    put_entries(out_ref, before(me), FIRST_ENDS, [end for ends in found for end in ends])


def put_entries(out_ref, at, start, entries):
    lane = iota((1, len(entries)), 1)
    row = jnp.zeros(lane.shape, f32)
    for i, entry in enumerate(entries):
        row = jnp.where(lane == i, entry, row)
    out_ref[at, :, start : start + len(entries)] = row


def get_entries(got_ref, at, start, count):
    row = got_ref[at, :, start : start + count]
    return [row[:, i : i + 1] for i in range(count)]


def before(me):
    return jnp.maximum(me - 1, 0)


def after(me):
    return jnp.minimum(me + 1, TILES - 1)


FIRST = 76
FIRST_ENDS = FIRST + 160
FIRST_INVERSE = FIRST_ENDS + 12
WIDE = 232
SLIM = 128
SLIM_TWO = 248


def wide_lanes(k):
    entries = WIDE + 8 * (22 - 2 * k)
    return entries, entries + 4


def own_edges(seg_ref):
    own = seg_ref[10][0:1]
    return [[own[:, 8 * b + i : 8 * b + i + 1] for b in range(4)] for i in range(4)]


def edge_terms(code, edges, frac):
    starts, _, _, factors = edges
    sums = totals([jnp.where(code == start, frac, 0.0) for start in starts])
    return [factor * picked for factor, picked in zip(factors, sums)]


def arrive(code, targets, terms):
    gain = jnp.zeros(code.shape, f32)
    for target, term in zip(targets, terms):
        gain = gain + jnp.where(code == target, term, 0.0)
    return gain


def late_rows(edges, ends, terms):
    lane = iota((1, 128), 1)
    cells, values = [], []
    for there, (tile, cell, weight), term in zip(edges[2], ends, terms):
        at = (lane == tile.astype(i32)) & (there >= 0.0)
        cells.append(jnp.where(at, cell, 0.0))
        values.append(jnp.where(at, weight * term, 0.0))
    return jnp.concatenate(cells + values, axis=0)


def to_three(rows):
    return [spread(rows, 16), rows, spread(rows, -16)]


def own_tile(field, k):
    return field[8 - k : 16 - k].reshape(ROWS, 128)


def starts_of(edge, table):
    place = (iota((CAP, 128), 1) * CAP + iota((CAP, 128), 0)).astype(f32)
    return totals([jnp.where(place == edge_in(edge, k, 1), table, 0.0) for k in range(4)])


def advance(cells_ref, k, field, halo, flow):
    low, high = k + 1, EXT - 1 - k
    ty, tz, ty_first, inverse, res = (cells_ref[i, low:high] for i in range(1, 6))
    tx_up, tx_down = cells_ref[0, low:high], cells_ref[0, low - 1 : high - 1]
    return inverse * (res + stencil(tx_up, tx_down, ty, tz, ty_first, field, halo) + flow)


def wide_halo(me, got_ref, start, count):
    return columns_of(*read_faces(me, got_ref, start, 8 * count)).reshape(count, 8, 128)


def ends_of(ends_ref):
    held = ends_ref[0:1]
    return [[held[:, 3 * k + i : 3 * k + i + 1] for i in range(3)] for k in range(4)]


def send_wide(me, out_ref, k, code, edges, ends, seg_ref, cells_ref, index_ref, field, frac, resf):
    tnext, inverse_f, fm = seg_ref[0], seg_ref[1], seg_ref[3]
    terms = edge_terms(code, edges, frac)
    ahead = inverse_f * (resf + chain(tnext, frac) + arrive(code, edges[1], terms))
    part = advance(cells_ref, k, field, jnp.zeros((22 - 2 * k, 8, 128), f32), 0.0)
    position = jnp.concatenate([seg_ref[8], seg_ref[9]], axis=0).astype(i32)
    now = find(fm * frac, position)
    rows = [find(own_tile(field, k), index_ref[...])] + to_three(now) + to_three(find(fm * ahead, position))
    rows += to_three(late_rows(edges, ends, terms)) + [spread(now, shift) for shift in BESIDE]
    store_slots(out_ref, jnp.concatenate(rows + [jnp.zeros((24, 128), f32)], axis=0))
    entries, further = wide_lanes(k)
    put_faces(me, out_ref, WIDE, *faces_of(field[1:-1].reshape(-1, 128)))
    put_faces(me, out_ref, further, *faces_of(part[1:-1].reshape(-1, 128)))
    put_entries(out_ref, jnp.where(me + 1 < TILES, me + 1, me), entries, terms)


def first_kernel(
    me_ref, got_ref, cells_ref, field_ref, index_ref, columns_ref, rows_ref, seg_ref, edge_ref,
    out_ref, new_field_ref, new_frac_ref, resf_ref, ends_ref, halo_inverse_ref, res_fracture_ref,
):
    me = me_ref[0]
    slots = load_slots(got_ref, 128)
    code = seg_code().astype(f32)
    tnext, inverse_f, partial, fm, mf, owner, rank = (seg_ref[i] for i in range(7))
    owner = owner.astype(i32)
    rank = rank.astype(i32)
    edge = edge_ref[0:1]
    edges = own_edges(seg_ref)
    starts, targets, nexts, factors = edges

    resf = partial - fm * look_up(slots[0:16], rank, owner)
    picks = get_entries(got_ref, after(me), 72, 4)
    for b in range(4):
        at = (code == starts[b]) & (nexts[b] >= 0.0)
        resf = resf - jnp.where(at, factors[b] * picks[b], 0.0)
    frac = inverse_f * resf
    terms = edge_terms(code, edges, frac)
    begun = starts_of(edge, slots[32:48])
    coming = [edge_in(edge, k, 4) - edge_in(edge, k, 3) * begun[k] for k in range(4)]
    gain = resf + chain(tnext, frac) + mf * look_up(slots[16:32], rank, owner)
    gain = gain + arrive(code, targets, terms) + arrive(code, [edge_in(edge, k, 0) for k in range(4)], coming)
    frac = inverse_f * gain
    late = [slots[48 + 8 * side : 56 + 8 * side] for side in range(3)]
    (flow,) = scatter_wide([], late, columns_ref, rows_ref, 6)
    field = advance(cells_ref, 1, field_ref[...], wide_halo(me, got_ref, FIRST, 20), flow + cells_ref[6, 2:22])
    new_field_ref[...] = field
    new_frac_ref[...] = frac
    resf_ref[...] = resf
    res_fracture_ref[...] = unfold(resf)
    halo_inverse_ref[...] = wide_halo(me, got_ref, FIRST_INVERSE, 16)
    ends = get_entries(got_ref, after(me), FIRST_ENDS, 12)
    ends = [ends[3 * k : 3 * k + 3] for k in range(4)]
    lane = iota((8, 128), 1)
    held = jnp.zeros((8, 128), f32)
    for k in range(4):
        for i in range(3):
            held = jnp.where(lane == 3 * k + i, ends[k][i], held)
    ends_ref[...] = held

    send_wide(me, out_ref, 2, code, edges, ends, seg_ref, cells_ref, index_ref, field, frac, resf)


def even_kernel(
    k, me_ref, got_ref, cells_ref, field_ref, index_ref, columns_ref, rows_ref, seg_ref, edge_ref,
    frac_ref, resf_ref, ends_ref, halo_inverse_ref, beside_ref,
    out_ref, third_ref, new_field_ref, new_frac_ref,
):
    me = me_ref[0]
    slots = load_slots(got_ref, 256)
    code = seg_code().astype(f32)
    tnext, inverse_f, _, fm, mf, owner, rank = (seg_ref[i] for i in range(7))
    edge = edge_ref[0:1]
    edges = own_edges(seg_ref)
    targets = edges[1]
    resf = resf_ref[...]
    frac = frac_ref[...]
    entries, further = wide_lanes(k)
    coming = get_entries(got_ref, before(me), entries, 4)
    gain = resf + chain(tnext, frac) + mf * look_up(slots[0:16], rank.astype(i32), owner.astype(i32))
    gain = gain + arrive(code, targets, edge_terms(code, edges, frac))
    gain = gain + arrive(code, [edge_in(edge, b, 0) for b in range(4)], coming)
    frac = inverse_f * gain
    terms = edge_terms(code, edges, frac)
    ahead = inverse_f * (resf + chain(tnext, frac) + arrive(code, targets, terms))
    new_frac_ref[...] = frac

    tables = [[slots[first + side * CAP : first + CAP + side * CAP] for side in range(3)] for first in (16, 64)]
    late = [slots[112 + 8 * side : 120 + 8 * side] for side in range(3)]
    flow, later = scatter_wide(tables, late, columns_ref, rows_ref, 7 - k)
    beside = []
    for side in range(3):
        height = ROWS if side == 1 else 8 * (6 - k)
        level = iota((height, 128), 0) + (ROWS - height if side == 0 else 0)
        lane = iota((height, 128), 1)
        column = jnp.zeros((height, 128), f32)
        for i, at in enumerate((0, 127)):
            first = 48 * i + CAP * side
            held = jnp.zeros((height, 128), f32)
            for r in range(first, first + CAP):
                held = held + jnp.where(level == beside_ref[r : r + 1], slots[136 + r : 137 + r], 0.0)
            column = jnp.where(lane == at, jnp.sum(held, axis=1, keepdims=True), column)
        beside.append(column.reshape(-1, 8, 128))
    beside = jnp.concatenate(beside, axis=0)
    second = field_ref[...]
    third = advance(cells_ref, k, second, wide_halo(me, got_ref, WIDE, 22 - 2 * k), flow)
    inner = second[2:-2]
    lane = iota(inner.shape, 2)
    joint = jnp.where(lane == 0, cells_ref[3, k + 2 : 22 - k], jnp.where(lane == 127, cells_ref[1, k + 2 : 22 - k], 0.0))
    halo = wide_halo(me, got_ref, further, 20 - 2 * k) + halo_inverse_ref[k - 2 : 18 - k] * (joint * inner + beside)
    field = advance(cells_ref, k + 1, third, halo, later[1:-1] + cells_ref[7, k + 2 : 22 - k] * inner)
    third_ref[...] = third
    new_field_ref[...] = field

    position = jnp.concatenate([seg_ref[8], seg_ref[9]], axis=0).astype(i32)
    ends = ends_of(ends_ref)
    own_third = find(own_tile(third, k + 1), index_ref[...])
    rows = [own_third, find(own_tile(field, k + 2), index_ref[...]), spread(own_third, 1)] + to_three(find(fm * ahead, position))
    rows += to_three(late_rows(edges, ends, terms))
    store_slots(out_ref, jnp.concatenate(rows + [jnp.zeros((8, 128), f32)], axis=0))
    put_faces(me, out_ref, SLIM, *faces_of(field[1:-1].reshape(-1, 128)))
    to_next = jnp.where(me + 1 < TILES, me + 1, me)
    put_entries(out_ref, to_next, SLIM + 8 * (18 - 2 * k), terms + edge_terms(code, edges, ahead))
    put_entries(out_ref, jnp.where(me + 2 < TILES, me + 2, me), SLIM_TWO, terms + edges[2])


def odd_kernel(
    k, final, me_ref, got_ref, cells_ref, field_ref, index_ref, columns_ref, rows_ref, seg_ref, edge_ref,
    frac_ref, resf_ref, ends_ref, third_ref, *outs,
):
    me = me_ref[0]
    slots = load_slots(got_ref, 128)
    code = seg_code().astype(f32)
    tnext, inverse_f, _, _, mf, owner, rank = (seg_ref[i] for i in range(7))
    owner = owner.astype(i32)
    rank = rank.astype(i32)
    edge = edge_ref[0:1]
    edges = own_edges(seg_ref)
    targets = edges[1]
    resf = resf_ref[...]
    frac = frac_ref[...]
    coming = get_entries(got_ref, before(me), SLIM + 8 * (22 - 2 * k), 8)
    two = jnp.where(me > 1, got_ref[jnp.maximum(me - 2, 0), :, 128:256], -1.0)
    lane = iota((1, 128), 1)
    codes = jnp.where((lane >= SLIM_TWO - 128) & (lane < SLIM_TWO - 124), pltpu.roll(two, 124, 1), -2.0)
    meets = jnp.concatenate([jnp.where(codes == edge_in(edge, b, 7), two, 0.0) for b in range(4)], axis=0)
    meets = jnp.sum(meets, axis=1, keepdims=True)
    begun = starts_of(edge, slots[32:48])
    heres = [edge_in(edge, b, 0) for b in range(4)]
    gain = resf + chain(tnext, frac) + mf * look_up(slots[0:16], rank, owner)
    gain = gain + arrive(code, targets, edge_terms(code, edges, frac))
    frac = inverse_f * (gain + arrive(code, heres, coming[:4]))
    terms = [
        coming[4 + b] + edge_in(edge, b, 6) * begun[b] + edge_in(edge, b, 8) * meets[b : b + 1] for b in range(4)
    ]
    gain = resf + chain(tnext, frac) + mf * look_up(slots[16:32], rank, owner)
    gain = gain + arrive(code, targets, edge_terms(code, edges, frac))
    frac = inverse_f * (gain + arrive(code, heres, terms))

    late = [slots[96 + 8 * side : 104 + 8 * side] for side in range(3)]
    tables = [[slots[48 + side * CAP : 64 + side * CAP] for side in range(3)]]
    (flow,) = scatter_wide(tables, late, columns_ref, rows_ref, 7 - k)
    flow = flow + cells_ref[7, k + 1 : 23 - k] * third_ref[2:-2]
    field = advance(cells_ref, k, field_ref[...], wide_halo(me, got_ref, SLIM, 22 - 2 * k), flow)
    if final:
        adj_matrix_ref, adj_fracture_ref = outs
        adj_matrix_ref[...] = swap_x(field)
        adj_fracture_ref[...] = unfold(frac)
        return
    out_ref, new_field_ref, new_frac_ref = outs
    new_field_ref[...] = field
    new_frac_ref[...] = frac
    send_wide(me, out_ref, k + 1, code, edges, ends_of(ends_ref), seg_ref, cells_ref, index_ref, field, frac, resf)


def call(kernel, name, scalars, arrays, outs, space=pltpu.VMEM, scratch=(), limit=20 * 1024 * 1024, out_spaces=None):
    spec = [pl.BlockSpec(memory_space=pltpu.SMEM)] * len(scalars)
    spec += [pl.BlockSpec(memory_space=space)] * len(arrays)
    return pl.pallas_call(
        kernel,
        name=name,
        out_shape=[jax.ShapeDtypeStruct(shape, kind) for shape, kind in outs],
        in_specs=spec,
        out_specs=[pl.BlockSpec(memory_space=out) for out in out_spaces or [pltpu.VMEM] * len(outs)],
        scratch_shapes=list(scratch),
        compiler_params=pltpu.CompilerParams(vmem_limit_bytes=limit),
    )(*scalars, *arrays)


def exchange(message):
    return lax.all_to_all(message, ALL, split_axis=0, concat_axis=0, tiled=True)


def swapped(block, first):
    pairs = [(i, i + 1) for i in range(first, lax.axis_size("gx") - 1, 2)]
    return lax.ppermute(block, "gx", pairs + [(j, i) for i, j in pairs])


def body(
    press_matrix, cond_matrix, accum_matrix, press_frac, accum_frac, trans_chain, couple_mf, couple_fm,
    conn_tile, conn_layer, conn_cell, inter_delta, inter_from, inter_to, inter_trans, well_tile, well_cell, well_rate,
):
    me = lax.axis_index(ALL).astype(i32).reshape(1)
    wide = (EXT, 8, 128)
    tile = (LAYERS, 8, 128)
    seg = (8, 128)

    given = (
        conn_tile, conn_layer, conn_cell, press_frac, accum_frac, trans_chain, couple_mf, couple_fm,
        press_matrix, cond_matrix, accum_matrix,
        inter_delta, inter_from, inter_to, inter_trans, well_tile, well_cell, well_rate,
    )
    message, segs, stacked = call(
        begin_kernel,
        "begin",
        (me,),
        given,
        [((TILES, 1, 512), f32), ((39, *seg), f32), ((3, *tile), f32)],
        pl.ANY,
        [(pltpu.VMEM if a.ndim > 1 else pltpu.SMEM)(a.shape, a.dtype) for a in given] + [pltpu.SemaphoreType.DMA((len(given) + 3,))],
        64 * 1024 * 1024,
        [pltpu.VMEM, pltpu.VMEM, pl.ANY],
    )
    inside = swapped(stacked, 0)
    across = swapped(stacked, 1)
    got = exchange(message)
    message, cells, field, index, columns, rows, edge, beside, res_matrix = call(
        cells_kernel,
        "cells",
        (me,),
        (got, inside, across, segs),
        [((TILES, 1, 384), f32), ((8, *wide), f32), ((22, 8, 128), f32), ((CAP, 128), i32), ((3, 128, SLOTS), bf16),
         ((3, ROWS, SLOTS), bf16), (seg, f32), ((96, 128), i32), (tile, f32)],
    )
    kept = (index, columns, rows, segs, edge)

    def after_sweeps(k):
        return ((EXT - 2 * k, 8, 128), f32)

    wide_message = ((TILES, 1, 512), f32)
    slim_message = ((TILES, 1, 256), f32)
    got = exchange(message)
    message, field, frac, resf, ends, halo_inverse, res_fracture = call(
        first_kernel,
        "first",
        (me,),
        (got, cells, field, *kept),
        [wide_message, after_sweeps(2), (seg, f32), (seg, f32), (seg, f32), ((16, 8, 128), f32), ((4, 256), f32)],
    )
    for k, final in ((2, False), (5, True)):
        got = exchange(message)
        message, third, field, frac = call(
            functools.partial(even_kernel, k),
            "even",
            (me,),
            (got, cells, field, *kept, frac, resf, ends, halo_inverse, beside),
            [slim_message, after_sweeps(k + 1), after_sweeps(k + 2), (seg, f32)],
        )
        got = exchange(message)
        outs = [(tile, f32), ((4, 256), f32)] if final else [wide_message, after_sweeps(k + 3), (seg, f32)]
        results = call(
            functools.partial(odd_kernel, k + 2, final),
            "odd",
            (me,),
            (got, cells, field, *kept, frac, resf, ends, third),
            outs,
        )
        if not final:
            message, field, frac = results
    adj_matrix, adj_fracture = results
    return res_matrix, res_fracture, adj_matrix, adj_fracture


def solution(mesh):
    cells = P(None, "gx", YA)
    segs = P(ALL, None)
    blocks = P(ALL)
    in_specs = (cells,) * 3 + (segs,) * 8 + (blocks,) * 4 + (P(),) * 3
    return jax.shard_map(body, mesh=mesh, in_specs=in_specs, out_specs=(cells, segs, cells, segs), check_vma=False)
```

```python
import functools

import jax
import jax.numpy as jnp
from jax import lax
from jax.experimental import pallas as pl
from jax.experimental.pallas import tpu as pltpu
from jax.sharding import PartitionSpec as P

ITERS = 8
CAP = 16
TILES = 128
ROWS = 64
EXT = 24
LAYERS = 8
SLOTS = CAP * TILES
ALL = ("gx", "gy", "af")
YA = ("gy", "af")
BESIDE = (17, 1, -15, 15, -1, -17)
f32 = jnp.float32
bf16 = jnp.bfloat16
i32 = jnp.int32


def iota(shape, axis):
    return lax.broadcasted_iota(i32, shape, axis)


def parts(value):
    high = value.astype(bf16)
    return high, (value - high.astype(f32)).astype(bf16)


def dot_nn(a, b):
    return lax.dot_general(a, b, (((1,), (0,)), ((), ())), preferred_element_type=f32)


def dot_nt(a, b):
    return lax.dot_general(a, b, (((1,), (1,)), ((), ())), preferred_element_type=f32)


def dot_tn(a, b):
    return lax.dot_general(a, b, (((0,), (0,)), ((), ())), preferred_element_type=f32)


def as_row(rows):
    return jnp.concatenate([rows[i : i + 1] for i in range(rows.shape[0])], axis=1)


def as_rows(row):
    return jnp.concatenate([row[:, i : i + 128] for i in range(0, row.shape[1], 128)], axis=0)


def totals(values):
    rows = jnp.concatenate([jnp.sum(value, axis=0, keepdims=True) for value in values], axis=0)
    sums = jnp.sum(rows, axis=1, keepdims=True)
    return [sums[i : i + 1] for i in range(len(values))]


def fold(value):
    return jnp.concatenate([value[:, :128], value[:, 128:]], axis=0)


def unfold(value):
    return jnp.concatenate([value[:4], value[4:]], axis=1)


def seg_code():
    row = iota((8, 128), 0)
    return (row % 4) * 256 + (row // 4) * 128 + iota((8, 128), 1)


def chain(tnext, field):
    lane = iota((8, 128), 1)
    ahead = pltpu.roll(field, 127, 1)
    ahead = jnp.where(lane == 127, pltpu.roll(ahead, 4, 0), ahead)
    behind = pltpu.roll(tnext * field, 1, 1)
    behind = jnp.where(lane == 0, pltpu.roll(behind, 4, 0), behind)
    return tnext * ahead + behind


def owner_hot(owner_row):
    return (iota((TILES, 1024), 0) == owner_row).astype(bf16)


def rank_mask(rank_row):
    return iota((CAP, 1024), 0) == rank_row


def to_slots(values, hot, mask):
    halves = ([], [])
    for value in values:
        row = as_row(value)
        for half, part in zip(halves, parts(row)):
            half.append(jnp.where(mask, part.astype(f32), 0.0).astype(bf16))
    both = jnp.concatenate([jnp.concatenate(half, axis=0) for half in halves], axis=1)
    return dot_nt(both, jnp.concatenate([hot, hot], axis=1))


def look_up(table, row, lane):
    out = jnp.zeros(row.shape, f32)
    for r in range(table.shape[0]):
        picked = jnp.take_along_axis(jnp.broadcast_to(table[r : r + 1], row.shape), lane, axis=1, mode="promise_in_bounds")
        out = jnp.where(row == r, picked, out)
    return out


def find(table, index):
    return look_up(table, index >> 7, index & 127)


def swap_x(block):
    return jnp.swapaxes(block, 0, 1)


def cell_hot(index_row, low=0, high=ROWS):
    count = index_row.shape[1]
    columns = iota((128, count), 0) == (index_row & 127)
    rows = iota((high - low, count), 0) == (index_row >> 7) - low
    return columns.astype(bf16), rows.astype(bf16)


def scatter(tables, columns, rows):
    height = rows.shape[0]
    stacked = []
    for table in tables:
        for part in parts(table):
            row = as_row(part.astype(f32))
            tall = jnp.broadcast_to(row, (16, row.shape[1])).astype(bf16)
            stacked.append(rows * jnp.concatenate([tall] * (height // 16), axis=0))
    sums = dot_nt(jnp.concatenate(stacked, axis=0), columns)
    return [
        (sums[2 * i * height : (2 * i + 1) * height] + sums[(2 * i + 1) * height : (2 * i + 2) * height]).reshape(-1, 8, 128)
        for i in range(len(tables))
    ]


def side_rows(side, count):
    height = (count + 1) // 2 * 16
    return ((0, ROWS), (ROWS - height, ROWS), (0, height))[0 if side == 1 else 1 + side // 2]


def gather_wide(sums, count):
    left, middle, right = sums
    if count == 0:
        return middle
    return jnp.concatenate([left[left.shape[0] - count :], middle, right[:count]], axis=0)


def scatter_wide(tables, late, columns_ref, rows_ref, count):
    fields = max(len(tables), 1)
    found = []
    for side in range(3):
        if side != 1 and count == 0:
            found.append([None] * fields)
            continue
        low, high = side_rows(side, count)
        index = as_row(late[side][:4].astype(i32) - 1)
        (sums,) = scatter([late[side][4:]], *cell_hot(index, low, high))
        if tables:
            *others, last = scatter([table[side] for table in tables], columns_ref[side], rows_ref[side, low:high])
            found.append([*others, last + sums])
        else:
            found.append([sums])
    return [gather_wide([found[side][i] for side in range(3)], count) for i in range(fields)]


def faces_of(field):
    turned = field.T
    return turned[0:1], turned[127:128]


def columns_of(left, right):
    width = left.shape[1]
    row = iota((128, width), 0)
    return jnp.where(row == 0, left, jnp.where(row == 127, right, 0.0)).T


def up_y(v, halo):
    return jnp.where(iota(v.shape, 2) == 127, halo, pltpu.roll(v, 127, 2))


def down_y(v, first):
    return jnp.where(iota(v.shape, 2) == 0, first, pltpu.roll(v, 1, 2))


def stencil(tx_up, tx_down, ty, tz, ty_first, field, halo):
    middle = field[1:-1]
    out = tx_up * field[2:] + tx_down * field[:-2]
    out = out + ty * up_y(middle, halo) + down_y(ty * middle, ty_first * halo)
    return out + tz * pltpu.roll(middle, 7, 1) + pltpu.roll(tz * middle, 1, 1)


def harmonic(first, second):
    both = first + second
    return jnp.where(both > 0.0, 2.0 * first * second / jnp.where(both > 0.0, both, 1.0), 0.0)


def read_faces(me, got_ref, start, width, across=0):
    along = me & 15
    line = (me >> 4) + across // 16
    inside = (line >= 0) & (line < 8)
    before = got_ref[jnp.clip(me + across - 1, 0, TILES - 1), :, start : start + width]
    after = got_ref[jnp.clip(me + across + 1, 0, TILES - 1), :, start : start + width]
    return jnp.where(inside & (along > 0), before, 0.0), jnp.where(inside & (along < 15), after, 0.0)


def put_faces(me, out_ref, start, first, last, across=0):
    width = first.shape[1]
    for at, face in ((me + across - 1, first), (me + across + 1, last)):
        out_ref[jnp.where((at >= 0) & (at < TILES), at, me), :, start : start + width] = face


def edge_codes(delta_ref, to_ref, b):
    block = b + delta_ref[b]
    code = block * 256 + to_ref[b]
    return jnp.where(block < 4, code, -1), jnp.where(block >= 4, code - 1024, -1)


def spread(rows, shift):
    lane = iota(rows.shape, 1)
    inside = (lane >= shift) if shift > 0 else (lane < TILES + shift)
    return jnp.where(inside, pltpu.roll(rows, shift % TILES, 1), 0.0)


def store_slots(out_ref, rows):
    for i in range(0, rows.shape[0], 128):
        part = rows[i : i + 128].T
        out_ref[:, 0, i : i + part.shape[1]] = part


def load_slots(got_ref, count):
    return jnp.concatenate([got_ref[:, 0, i : i + 128].T for i in range(0, count, 128)], axis=0)


def begin_kernel(me_ref, *refs):
    count = len(refs) // 2 - 2
    given, (out_ref, seg_ref, tile_out_ref), held, sems = refs[:count], refs[count : count + 3], refs[count + 3 : -1], refs[-1]
    copies = [pltpu.make_async_copy(a, b, sems.at[i]) for i, (a, b) in enumerate(zip(given, held))]
    passing = [pltpu.make_async_copy(held[8 + i], tile_out_ref.at[i], sems.at[count + i]) for i in range(3)]
    for copy in copies:
        copy.start()
    for copy in copies:
        copy.wait()
    for copy in passing:
        copy.start()
    tile_ref, layer_ref, cell_ref, press_frac_ref, accum_ref, chain_ref, mf_ref, fm_ref = held[:8]
    press_ref, cond_ref, accum_matrix_ref = held[8:11]
    delta_ref, from_ref, to_ref, trans_ref, well_tile_ref, well_cell_ref, well_rate_ref = held[11:]
    me = me_ref[0]
    code = seg_code()
    owner = fold(tile_ref[...])
    owner_row = as_row(owner)
    hot = owner_hot(owner_row)
    before = (iota((128, 128), 0) < iota((128, 128), 1)).astype(bf16)
    base = jnp.zeros((TILES, 1), f32)
    ranks = []
    for c in range(8):
        part = hot[:, c * 128 : (c + 1) * 128]
        wide = part.astype(f32)
        count = dot_nn(part, before) + base
        ranks.append(jnp.sum(wide * count, axis=0, keepdims=True))
        base = base + jnp.sum(wide, axis=1, keepdims=True)
    rank_row = jnp.concatenate(ranks, axis=1).astype(i32)
    rank = as_rows(rank_row)
    mask = rank_mask(rank_row)

    press = fold(press_frac_ref[...])
    fm = fold(fm_ref[...])
    mf = fold(mf_ref[...])
    last = code % 256 == 255
    tnext = jnp.where(last, 0.0, fold(chain_ref[...]))
    tprev = pltpu.roll(tnext, 1, 1)
    tprev = jnp.where(iota((8, 128), 1) == 0, pltpu.roll(tprev, 4, 0), tprev)
    diag = fold(accum_ref[...]) + tnext + tprev + fm
    inverse = 1.0 / diag
    partial = diag * press - chain(tnext, press)
    heres = [edge_codes(delta_ref, to_ref, b)[0] for b in range(4)]
    for b, picked in enumerate(totals([jnp.where(code == here, press, 0.0) for here in heres])):
        at = code == b * 256 + from_ref[b]
        partial = partial - jnp.where(at, trans_ref[b] * picked, 0.0)
    cell = fold(cell_ref[...])
    where_cell = ((((cell >> 7) * 8 + fold(layer_ref[...])) << 7) + (cell & 127) + 1).astype(f32)
    position = (iota((8, 128), 0) * 128 + iota((8, 128), 1) + 1).astype(f32)
    weight = fm * inverse
    slots = to_slots([where_cell, mf * press, weight * fm, weight * mf, weight * partial, position], hot, mask)
    inverse_index, slots = slots[80:96], slots[:80]
    place = (owner * CAP + rank).astype(f32)
    rows = []
    for b in range(4):
        _, there = edge_codes(delta_ref, to_ref, b)
        at = code == b * 256 + from_ref[b]
        gain = trans_ref[b] * inverse
        rows.append(jnp.where(iota((1, 128), 1) == 0, there.astype(f32), 0.0))
        for value in (place, where_cell, gain * fm, gain * partial, gain * trans_ref[b], gain * mf, code.astype(f32), gain):
            rows.append(jnp.sum(jnp.where(at, value, 0.0), axis=0, keepdims=True))
        rows.append(jnp.zeros((3, 128), f32))
    edges = [jnp.broadcast_to(jnp.sum(jnp.concatenate(rows, axis=0), axis=1, keepdims=True), (48, 128))]
    rows = edges + to_three(slots) + [spread(slots[:CAP], shift) for shift in BESIDE]
    store_slots(out_ref, jnp.concatenate(rows, axis=0))
    first_face, last_face = faces_of(jnp.concatenate([swap_x(ref[...]).reshape(ROWS, 128) for ref in (press_ref, cond_ref)], axis=0))
    for across in (-16, 0, 16):
        put_faces(me, out_ref, 384, first_face, last_face, across)
    for i, value in enumerate((tnext, inverse, partial, fm, mf, owner.astype(f32), rank.astype(f32), press)):
        seg_ref[i] = value
    for i in range(2):
        seg_ref[8 + i] = inverse_index[8 * i : 8 * i + 8] - 1.0
    lane = iota((8, 128), 1)
    own = jnp.zeros((8, 128), f32)
    for b in range(4):
        here, there = edge_codes(delta_ref, to_ref, b)
        for i, value in enumerate((b * 256 + from_ref[b], here, there)):
            own = jnp.where(lane == 8 * b + i, value.astype(f32), own)
        own = jnp.where(lane == 8 * b + 3, trans_ref[b], own)
    seg_ref[10] = own
    plane_x = iota((EXT, 128), 0) + ((me >> 4) - 1) * 8
    plane_y = iota((EXT, 128), 1) + (me & 15) * 128
    source = jnp.zeros((EXT, 128), f32)
    for w in range(well_tile_ref.shape[0]):
        tile = well_tile_ref[w]
        cell = well_cell_ref[w]
        at = (plane_x == (tile >> 4) * 8 + (cell >> 7)) & (plane_y == (tile & 15) * 128 + (cell & 127))
        source = source + jnp.where(at, well_rate_ref[w], 0.0)
    for i in range(3):
        seg_ref[11 + i] = source[8 * i : 8 * i + 8]
    seg_ref[14] = where_cell
    for i, ref in enumerate((press_ref, cond_ref, accum_matrix_ref)):
        seg_ref[15 + 8 * i : 23 + 8 * i] = swap_x(ref[...])
    for copy in passing:
        copy.wait()


def edge_in(row, k, i):
    at = 12 * k + i
    return row[:, at : at + 1]


def cells_kernel(
    me_ref,
    got_ref, inside_ref, across_ref, seg_ref,
    out_ref, cells_ref, field_ref, index_ref, columns_ref, rows_ref, edge_ref, beside_ref, res_ref,
):
    me = me_ref[0]
    slots = load_slots(got_ref, 384)
    even = ((me >> 4) & 1) == 0
    press, cond, accum = (
        jnp.concatenate(
            [swap_x(jnp.where(even, b, a)), seg_ref[15 + 8 * i : 23 + 8 * i], swap_x(jnp.where(even, a, b))], axis=0
        )
        for i, a, b in ((i, inside_ref[i], across_ref[i]) for i in range(3))
    )
    sums = []
    for side in range(3):
        table = slots[48 + side * 80 : 128 + side * 80]
        index = table[:CAP].astype(i32) - 1
        if side == 1:
            index_ref[...] = index
            own = index
        columns, rows = cell_hot(as_row(index))
        columns_ref[side] = columns
        rows_ref[side] = rows
        sums.append(scatter([table[i : i + CAP] for i in range(CAP, 5 * CAP, CAP)], columns, rows))
    flow, weight, mirror, first = (jnp.concatenate([sums[side][i] for side in range(3)], axis=0) for i in range(4))
    beside = slots[288:384].astype(i32) - 1
    along = me & 15
    for i, (there, column) in enumerate(((along > 0, 127), (along < 15, 0))):
        part = beside[48 * i : 48 * i + 48]
        beside_ref[48 * i : 48 * i + 48] = jnp.where(there & (part >= 0) & ((part & 127) == column), part >> 7, -1)

    halos = [columns_of(*read_faces(me, got_ref, 384, 2 * ROWS, across)) for across in (-16, 0, 16)]
    press_halo = jnp.concatenate([halo[:ROWS].reshape(8, 8, 128) for halo in halos], axis=0)
    cond_halo = jnp.concatenate([halo[ROWS:].reshape(8, 8, 128) for halo in halos], axis=0)
    wide = (EXT, 8, 128)
    tx = harmonic(cond[:-1], cond[1:])
    ty = harmonic(cond, up_y(cond, cond_halo))
    tz = 0.5 * harmonic(cond, jnp.where(iota(wide, 1) == 7, 0.0, pltpu.roll(cond, 7, 1)))
    ty_first = jnp.where(iota(wide, 2) == 0, harmonic(cond, cond_halo), 0.0)
    diag = accum + ty + down_y(ty, ty_first) + tz + pltpu.roll(tz, 1, 1)
    diag = diag[1:-1] + tx[1:] + tx[:-1]
    inverse = jnp.where(diag > 0.0, 1.0 / jnp.where(diag > 0.0, diag, 1.0), 0.0)
    source = jnp.concatenate([seg_ref[11 + i] for i in range(3)], axis=0)

    res = diag * press[1:-1] - flow[1:-1] - source.reshape(EXT, 1, 128)[1:-1]
    res = res - stencil(tx[1:], tx[:-1], ty[1:-1], tz[1:-1], ty_first[1:-1], press, press_halo[1:-1])
    field = inverse * res
    cells_ref[0, : EXT - 1] = tx
    for i, value in ((1, ty), (2, tz), (3, ty_first), (6, first - weight * press), (7, mirror)):
        cells_ref[i] = value
    cells_ref[4, 1 : EXT - 1] = inverse
    cells_ref[5, 1 : EXT - 1] = res
    field_ref[...] = field
    res_ref[...] = swap_x(res[7:15])

    code = seg_code().astype(f32)
    _, inverse_f, partial, fm, _, owner, _, press_f = (seg_ref[i] for i in range(8))
    edge = jnp.where(me > 0, got_ref[before(me), :, 0:128], -1.0)
    lane = iota((1, 128), 1)
    cells, terms, picks, found = [], [], [], []
    ends = [code == edge_in(edge, k, 0) for k in range(4)]
    wanted = (press_f, owner, seg_ref[14], fm * inverse_f)
    sums = totals([jnp.where(at, value, 0.0) for at in ends for value in wanted])
    for k in range(4):
        picked = sums[4 * k]
        at = (lane == (edge_in(edge, k, 1).astype(i32) >> 4)) & (edge_in(edge, k, 0) >= 0.0)
        cells.append(jnp.where(at, edge_in(edge, k, 2), 0.0))
        terms.append(jnp.where(at, -edge_in(edge, k, 3) * picked, 0.0))
        picks.append(jnp.broadcast_to(picked, (1, 128)))
        found.append(sums[4 * k + 1 : 4 * k + 4])
    for k in range(4):
        edge = jnp.where(lane == 12 * k + 4, edge - edge_in(edge, k, 5) * sums[4 * k], edge)
    edge_ref[...] = jnp.broadcast_to(edge, (8, 128))
    late = jnp.concatenate(cells + terms, axis=0)

    taken = [find(press[8:16].reshape(ROWS, 128), own), find(own_tile(field, 1), own)]
    rows = taken + [spread(taken[0], 1)]
    store_slots(out_ref, jnp.concatenate(rows + to_three(late) + picks + [jnp.zeros((52, 128), f32)], axis=0))
    put_faces(me, out_ref, FIRST, *faces_of(field[1:-1].reshape(-1, 128)))
    put_faces(me, out_ref, FIRST_INVERSE, *faces_of(inverse[3:19].reshape(-1, 128)))
    put_entries(out_ref, before(me), FIRST_ENDS, [end for ends in found for end in ends])


def put_entries(out_ref, at, start, entries):
    lane = iota((1, len(entries)), 1)
    row = jnp.zeros(lane.shape, f32)
    for i, entry in enumerate(entries):
        row = jnp.where(lane == i, entry, row)
    out_ref[at, :, start : start + len(entries)] = row


def get_entries(got_ref, at, start, count):
    row = got_ref[at, :, start : start + count]
    return [row[:, i : i + 1] for i in range(count)]


def before(me):
    return jnp.maximum(me - 1, 0)


def after(me):
    return jnp.minimum(me + 1, TILES - 1)


FIRST = 76
FIRST_ENDS = FIRST + 160
FIRST_INVERSE = FIRST_ENDS + 12
WIDE = 232
SLIM = 128
SLIM_TWO = 248


def wide_lanes(k):
    entries = WIDE + 8 * (22 - 2 * k)
    return entries, entries + 4


def own_edges(seg_ref):
    own = seg_ref[10][0:1]
    return [[own[:, 8 * b + i : 8 * b + i + 1] for b in range(4)] for i in range(4)]


def edge_terms(code, edges, frac):
    starts, _, _, factors = edges
    sums = totals([jnp.where(code == start, frac, 0.0) for start in starts])
    return [factor * picked for factor, picked in zip(factors, sums)]


def arrive(code, targets, terms):
    gain = jnp.zeros(code.shape, f32)
    for target, term in zip(targets, terms):
        gain = gain + jnp.where(code == target, term, 0.0)
    return gain


def late_rows(edges, ends, terms):
    lane = iota((1, 128), 1)
    cells, values = [], []
    for there, (tile, cell, weight), term in zip(edges[2], ends, terms):
        at = (lane == tile.astype(i32)) & (there >= 0.0)
        cells.append(jnp.where(at, cell, 0.0))
        values.append(jnp.where(at, weight * term, 0.0))
    return jnp.concatenate(cells + values, axis=0)


def to_three(rows):
    return [spread(rows, 16), rows, spread(rows, -16)]


def own_tile(field, k):
    return field[8 - k : 16 - k].reshape(ROWS, 128)


def starts_of(edge, table):
    place = (iota((CAP, 128), 1) * CAP + iota((CAP, 128), 0)).astype(f32)
    return totals([jnp.where(place == edge_in(edge, k, 1), table, 0.0) for k in range(4)])


def advance(cells_ref, k, field, halo, flow):
    low, high = k + 1, EXT - 1 - k
    ty, tz, ty_first, inverse, res = (cells_ref[i, low:high] for i in range(1, 6))
    tx_up, tx_down = cells_ref[0, low:high], cells_ref[0, low - 1 : high - 1]
    return inverse * (res + stencil(tx_up, tx_down, ty, tz, ty_first, field, halo) + flow)


def wide_halo(me, got_ref, start, count):
    return columns_of(*read_faces(me, got_ref, start, 8 * count)).reshape(count, 8, 128)


def ends_of(ends_ref):
    held = ends_ref[0:1]
    return [[held[:, 3 * k + i : 3 * k + i + 1] for i in range(3)] for k in range(4)]


def send_wide(me, out_ref, k, code, edges, ends, seg_ref, cells_ref, index_ref, field, frac, resf):
    tnext, inverse_f, fm = seg_ref[0], seg_ref[1], seg_ref[3]
    terms = edge_terms(code, edges, frac)
    ahead = inverse_f * (resf + chain(tnext, frac) + arrive(code, edges[1], terms))
    part = advance(cells_ref, k, field, jnp.zeros((22 - 2 * k, 8, 128), f32), 0.0)
    position = jnp.concatenate([seg_ref[8], seg_ref[9]], axis=0).astype(i32)
    now = find(fm * frac, position)
    rows = [find(own_tile(field, k), index_ref[...])] + to_three(now) + to_three(find(fm * ahead, position))
    rows += to_three(late_rows(edges, ends, terms)) + [spread(now, shift) for shift in BESIDE]
    store_slots(out_ref, jnp.concatenate(rows + [jnp.zeros((24, 128), f32)], axis=0))
    entries, further = wide_lanes(k)
    put_faces(me, out_ref, WIDE, *faces_of(field[1:-1].reshape(-1, 128)))
    put_faces(me, out_ref, further, *faces_of(part[1:-1].reshape(-1, 128)))
    put_entries(out_ref, jnp.where(me + 1 < TILES, me + 1, me), entries, terms)


def first_kernel(
    me_ref, got_ref, cells_ref, field_ref, index_ref, columns_ref, rows_ref, seg_ref, edge_ref,
    out_ref, new_field_ref, new_frac_ref, resf_ref, ends_ref, halo_inverse_ref, res_fracture_ref,
):
    me = me_ref[0]
    slots = load_slots(got_ref, 128)
    code = seg_code().astype(f32)
    tnext, inverse_f, partial, fm, mf, owner, rank = (seg_ref[i] for i in range(7))
    owner = owner.astype(i32)
    rank = rank.astype(i32)
    edge = edge_ref[0:1]
    edges = own_edges(seg_ref)
    starts, targets, nexts, factors = edges

    resf = partial - fm * look_up(slots[0:16], rank, owner)
    picks = get_entries(got_ref, after(me), 72, 4)
    for b in range(4):
        at = (code == starts[b]) & (nexts[b] >= 0.0)
        resf = resf - jnp.where(at, factors[b] * picks[b], 0.0)
    frac = inverse_f * resf
    terms = edge_terms(code, edges, frac)
    begun = starts_of(edge, slots[32:48])
    coming = [edge_in(edge, k, 4) - edge_in(edge, k, 3) * begun[k] for k in range(4)]
    gain = resf + chain(tnext, frac) + mf * look_up(slots[16:32], rank, owner)
    gain = gain + arrive(code, targets, terms) + arrive(code, [edge_in(edge, k, 0) for k in range(4)], coming)
    frac = inverse_f * gain
    late = [slots[48 + 8 * side : 56 + 8 * side] for side in range(3)]
    (flow,) = scatter_wide([], late, columns_ref, rows_ref, 6)
    field = advance(cells_ref, 1, field_ref[...], wide_halo(me, got_ref, FIRST, 20), flow + cells_ref[6, 2:22])
    new_field_ref[...] = field
    new_frac_ref[...] = frac
    resf_ref[...] = resf
    res_fracture_ref[...] = unfold(resf)
    halo_inverse_ref[...] = wide_halo(me, got_ref, FIRST_INVERSE, 16)
    ends = get_entries(got_ref, after(me), FIRST_ENDS, 12)
    ends = [ends[3 * k : 3 * k + 3] for k in range(4)]
    lane = iota((8, 128), 1)
    held = jnp.zeros((8, 128), f32)
    for k in range(4):
        for i in range(3):
            held = jnp.where(lane == 3 * k + i, ends[k][i], held)
    ends_ref[...] = held

    send_wide(me, out_ref, 2, code, edges, ends, seg_ref, cells_ref, index_ref, field, frac, resf)


def even_kernel(
    k, me_ref, got_ref, cells_ref, field_ref, index_ref, columns_ref, rows_ref, seg_ref, edge_ref,
    frac_ref, resf_ref, ends_ref, halo_inverse_ref, beside_ref,
    out_ref, third_ref, new_field_ref, new_frac_ref,
):
    me = me_ref[0]
    slots = load_slots(got_ref, 256)
    code = seg_code().astype(f32)
    tnext, inverse_f, _, fm, mf, owner, rank = (seg_ref[i] for i in range(7))
    edge = edge_ref[0:1]
    edges = own_edges(seg_ref)
    targets = edges[1]
    resf = resf_ref[...]
    frac = frac_ref[...]
    entries, further = wide_lanes(k)
    coming = get_entries(got_ref, before(me), entries, 4)
    gain = resf + chain(tnext, frac) + mf * look_up(slots[0:16], rank.astype(i32), owner.astype(i32))
    gain = gain + arrive(code, targets, edge_terms(code, edges, frac))
    gain = gain + arrive(code, [edge_in(edge, b, 0) for b in range(4)], coming)
    frac = inverse_f * gain
    terms = edge_terms(code, edges, frac)
    ahead = inverse_f * (resf + chain(tnext, frac) + arrive(code, targets, terms))
    new_frac_ref[...] = frac

    tables = [[slots[first + side * CAP : first + CAP + side * CAP] for side in range(3)] for first in (16, 64)]
    late = [slots[112 + 8 * side : 120 + 8 * side] for side in range(3)]
    flow, later = scatter_wide(tables, late, columns_ref, rows_ref, 7 - k)
    beside = []
    for side in range(3):
        height = ROWS if side == 1 else 8 * (6 - k)
        level = iota((height, 128), 0) + (ROWS - height if side == 0 else 0)
        lane = iota((height, 128), 1)
        column = jnp.zeros((height, 128), f32)
        for i, at in enumerate((0, 127)):
            first = 48 * i + CAP * side
            held = jnp.zeros((height, 128), f32)
            for r in range(first, first + CAP):
                held = held + jnp.where(level == beside_ref[r : r + 1], slots[136 + r : 137 + r], 0.0)
            column = jnp.where(lane == at, jnp.sum(held, axis=1, keepdims=True), column)
        beside.append(column.reshape(-1, 8, 128))
    beside = jnp.concatenate(beside, axis=0)
    second = field_ref[...]
    third = advance(cells_ref, k, second, wide_halo(me, got_ref, WIDE, 22 - 2 * k), flow)
    inner = second[2:-2]
    lane = iota(inner.shape, 2)
    joint = jnp.where(lane == 0, cells_ref[3, k + 2 : 22 - k], jnp.where(lane == 127, cells_ref[1, k + 2 : 22 - k], 0.0))
    halo = wide_halo(me, got_ref, further, 20 - 2 * k) + halo_inverse_ref[k - 2 : 18 - k] * (joint * inner + beside)
    field = advance(cells_ref, k + 1, third, halo, later[1:-1] + cells_ref[7, k + 2 : 22 - k] * inner)
    third_ref[...] = third
    new_field_ref[...] = field

    position = jnp.concatenate([seg_ref[8], seg_ref[9]], axis=0).astype(i32)
    ends = ends_of(ends_ref)
    own_third = find(own_tile(third, k + 1), index_ref[...])
    rows = [own_third, find(own_tile(field, k + 2), index_ref[...]), spread(own_third, 1)] + to_three(find(fm * ahead, position))
    rows += to_three(late_rows(edges, ends, terms))
    store_slots(out_ref, jnp.concatenate(rows + [jnp.zeros((8, 128), f32)], axis=0))
    put_faces(me, out_ref, SLIM, *faces_of(field[1:-1].reshape(-1, 128)))
    to_next = jnp.where(me + 1 < TILES, me + 1, me)
    put_entries(out_ref, to_next, SLIM + 8 * (18 - 2 * k), terms + edge_terms(code, edges, ahead))
    put_entries(out_ref, jnp.where(me + 2 < TILES, me + 2, me), SLIM_TWO, terms + edges[2])


def odd_kernel(
    k, final, me_ref, got_ref, cells_ref, field_ref, index_ref, columns_ref, rows_ref, seg_ref, edge_ref,
    frac_ref, resf_ref, ends_ref, third_ref, *outs,
):
    me = me_ref[0]
    slots = load_slots(got_ref, 128)
    code = seg_code().astype(f32)
    tnext, inverse_f, _, _, mf, owner, rank = (seg_ref[i] for i in range(7))
    owner = owner.astype(i32)
    rank = rank.astype(i32)
    edge = edge_ref[0:1]
    edges = own_edges(seg_ref)
    targets = edges[1]
    resf = resf_ref[...]
    frac = frac_ref[...]
    coming = get_entries(got_ref, before(me), SLIM + 8 * (22 - 2 * k), 8)
    two = jnp.where(me > 1, got_ref[jnp.maximum(me - 2, 0), :, 128:256], -1.0)
    lane = iota((1, 128), 1)
    codes = jnp.where((lane >= SLIM_TWO - 128) & (lane < SLIM_TWO - 124), pltpu.roll(two, 124, 1), -2.0)
    meets = jnp.concatenate([jnp.where(codes == edge_in(edge, b, 7), two, 0.0) for b in range(4)], axis=0)
    meets = jnp.sum(meets, axis=1, keepdims=True)
    begun = starts_of(edge, slots[32:48])
    heres = [edge_in(edge, b, 0) for b in range(4)]
    gain = resf + chain(tnext, frac) + mf * look_up(slots[0:16], rank, owner)
    gain = gain + arrive(code, targets, edge_terms(code, edges, frac))
    frac = inverse_f * (gain + arrive(code, heres, coming[:4]))
    terms = [
        coming[4 + b] + edge_in(edge, b, 6) * begun[b] + edge_in(edge, b, 8) * meets[b : b + 1] for b in range(4)
    ]
    gain = resf + chain(tnext, frac) + mf * look_up(slots[16:32], rank, owner)
    gain = gain + arrive(code, targets, edge_terms(code, edges, frac))
    frac = inverse_f * (gain + arrive(code, heres, terms))

    late = [slots[96 + 8 * side : 104 + 8 * side] for side in range(3)]
    tables = [[slots[48 + side * CAP : 64 + side * CAP] for side in range(3)]]
    (flow,) = scatter_wide(tables, late, columns_ref, rows_ref, 7 - k)
    flow = flow + cells_ref[7, k + 1 : 23 - k] * third_ref[2:-2]
    field = advance(cells_ref, k, field_ref[...], wide_halo(me, got_ref, SLIM, 22 - 2 * k), flow)
    if final:
        adj_matrix_ref, adj_fracture_ref = outs
        adj_matrix_ref[...] = swap_x(field)
        adj_fracture_ref[...] = unfold(frac)
        return
    out_ref, new_field_ref, new_frac_ref = outs
    new_field_ref[...] = field
    new_frac_ref[...] = frac
    send_wide(me, out_ref, k + 1, code, edges, ends_of(ends_ref), seg_ref, cells_ref, index_ref, field, frac, resf)


def hold_kernel(given_ref, out_ref):
    out_ref[...] = given_ref[...]


def call(kernel, name, scalars, arrays, outs, space=pltpu.VMEM, scratch=(), limit=20 * 1024 * 1024, out_spaces=None):
    spec = [pl.BlockSpec(memory_space=pltpu.SMEM)] * len(scalars)
    spec += [pl.BlockSpec(memory_space=space)] * len(arrays)
    return pl.pallas_call(
        kernel,
        name=name,
        out_shape=[jax.ShapeDtypeStruct(shape, kind) for shape, kind in outs],
        in_specs=spec,
        out_specs=[pl.BlockSpec(memory_space=out) for out in out_spaces or [pltpu.VMEM] * len(outs)],
        scratch_shapes=list(scratch),
        compiler_params=pltpu.CompilerParams(vmem_limit_bytes=limit),
    )(*scalars, *arrays)


def exchange(message):
    return lax.all_to_all(message, ALL, split_axis=0, concat_axis=0, tiled=True)


def swapped(block, first):
    pairs = [(i, i + 1) for i in range(first, lax.axis_size("gx") - 1, 2)]
    return lax.ppermute(block, "gx", pairs + [(j, i) for i, j in pairs])


def body(
    press_matrix, cond_matrix, accum_matrix, press_frac, accum_frac, trans_chain, couple_mf, couple_fm,
    conn_tile, conn_layer, conn_cell, inter_delta, inter_from, inter_to, inter_trans, well_tile, well_cell, well_rate,
):
    me = lax.axis_index(ALL).astype(i32).reshape(1)
    wide = (EXT, 8, 128)
    tile = (LAYERS, 8, 128)
    seg = (8, 128)

    given = (
        conn_tile, conn_layer, conn_cell, press_frac, accum_frac, trans_chain, couple_mf, couple_fm,
        press_matrix, cond_matrix, accum_matrix,
        inter_delta, inter_from, inter_to, inter_trans, well_tile, well_cell, well_rate,
    )
    message, segs, stacked = call(
        begin_kernel,
        "begin",
        (me,),
        given,
        [((TILES, 1, 512), f32), ((39, *seg), f32), ((3, *tile), f32)],
        pl.ANY,
        [(pltpu.VMEM if a.ndim > 1 else pltpu.SMEM)(a.shape, a.dtype) for a in given] + [pltpu.SemaphoreType.DMA((len(given) + 3,))],
        64 * 1024 * 1024,
        [pltpu.VMEM, pltpu.VMEM, pl.ANY],
    )
    inside = swapped(stacked, 0)
    across = swapped(stacked, 1)
    (segs,) = call(hold_kernel, "hold", (), (segs,), [(segs.shape, f32)])
    got = exchange(message)
    message, cells, field, index, columns, rows, edge, beside, res_matrix = call(
        cells_kernel,
        "cells",
        (me,),
        (got, inside, across, segs),
        [((TILES, 1, 384), f32), ((8, *wide), f32), ((22, 8, 128), f32), ((CAP, 128), i32), ((3, 128, SLOTS), bf16),
         ((3, ROWS, SLOTS), bf16), (seg, f32), ((96, 128), i32), (tile, f32)],
    )
    kept = (index, columns, rows, segs, edge)

    def after_sweeps(k):
        return ((EXT - 2 * k, 8, 128), f32)

    wide_message = ((TILES, 1, 512), f32)
    slim_message = ((TILES, 1, 256), f32)
    got = exchange(message)
    message, field, frac, resf, ends, halo_inverse, res_fracture = call(
        first_kernel,
        "first",
        (me,),
        (got, cells, field, *kept),
        [wide_message, after_sweeps(2), (seg, f32), (seg, f32), (seg, f32), ((16, 8, 128), f32), ((4, 256), f32)],
    )
    for k, final in ((2, False), (5, True)):
        got = exchange(message)
        message, third, field, frac = call(
            functools.partial(even_kernel, k),
            "even",
            (me,),
            (got, cells, field, *kept, frac, resf, ends, halo_inverse, beside),
            [slim_message, after_sweeps(k + 1), after_sweeps(k + 2), (seg, f32)],
        )
        got = exchange(message)
        outs = [(tile, f32), ((4, 256), f32)] if final else [wide_message, after_sweeps(k + 3), (seg, f32)]
        results = call(
            functools.partial(odd_kernel, k + 2, final),
            "odd",
            (me,),
            (got, cells, field, *kept, frac, resf, ends, third),
            outs,
        )
        if not final:
            message, field, frac = results
    adj_matrix, adj_fracture = results
    return res_matrix, res_fracture, adj_matrix, adj_fracture


def solution(mesh):
    cells = P(None, "gx", YA)
    segs = P(ALL, None)
    blocks = P(ALL)
    in_specs = (cells,) * 3 + (segs,) * 8 + (blocks,) * 4 + (P(),) * 3
    return jax.shard_map(body, mesh=mesh, in_specs=in_specs, out_specs=(cells, segs, cells, segs), check_vma=False)
```

```python
import functools

import jax
import jax.numpy as jnp
from jax import lax
from jax.experimental import pallas as pl
from jax.experimental.pallas import tpu as pltpu
from jax.sharding import PartitionSpec as P

ITERS = 8
CAP = 16
TILES = 128
ROWS = 64
EXT = 24
LAYERS = 8
SLOTS = CAP * TILES
ALL = ("gx", "gy", "af")
YA = ("gy", "af")
BESIDE = (17, 1, -15, 15, -1, -17)
f32 = jnp.float32
bf16 = jnp.bfloat16
i32 = jnp.int32


def iota(shape, axis):
    return lax.broadcasted_iota(i32, shape, axis)


def parts(value):
    high = value.astype(bf16)
    return high, (value - high.astype(f32)).astype(bf16)


def dot_nn(a, b):
    return lax.dot_general(a, b, (((1,), (0,)), ((), ())), preferred_element_type=f32)


def dot_nt(a, b):
    return lax.dot_general(a, b, (((1,), (1,)), ((), ())), preferred_element_type=f32)


def dot_tn(a, b):
    return lax.dot_general(a, b, (((0,), (0,)), ((), ())), preferred_element_type=f32)


def as_row(rows):
    return jnp.concatenate([rows[i : i + 1] for i in range(rows.shape[0])], axis=1)


def as_rows(row):
    return jnp.concatenate([row[:, i : i + 128] for i in range(0, row.shape[1], 128)], axis=0)


def totals(values):
    rows = jnp.concatenate([jnp.sum(value, axis=0, keepdims=True) for value in values], axis=0)
    sums = jnp.sum(rows, axis=1, keepdims=True)
    return [sums[i : i + 1] for i in range(len(values))]


def fold(value):
    return jnp.concatenate([value[:, :128], value[:, 128:]], axis=0)


def unfold(value):
    return jnp.concatenate([value[:4], value[4:]], axis=1)


def seg_code():
    row = iota((8, 128), 0)
    return (row % 4) * 256 + (row // 4) * 128 + iota((8, 128), 1)


def chain(tnext, field):
    lane = iota((8, 128), 1)
    ahead = pltpu.roll(field, 127, 1)
    ahead = jnp.where(lane == 127, pltpu.roll(ahead, 4, 0), ahead)
    behind = pltpu.roll(tnext * field, 1, 1)
    behind = jnp.where(lane == 0, pltpu.roll(behind, 4, 0), behind)
    return tnext * ahead + behind


def owner_hot(owner_row):
    return (iota((TILES, 1024), 0) == owner_row).astype(bf16)


def rank_mask(rank_row):
    return iota((CAP, 1024), 0) == rank_row


def to_slots(values, hot, mask):
    halves = ([], [])
    for value in values:
        row = as_row(value)
        for half, part in zip(halves, parts(row)):
            half.append(jnp.where(mask, part.astype(f32), 0.0).astype(bf16))
    both = jnp.concatenate([jnp.concatenate(half, axis=0) for half in halves], axis=1)
    return dot_nt(both, jnp.concatenate([hot, hot], axis=1))


def look_up(table, row, lane):
    out = jnp.zeros(row.shape, f32)
    for r in range(table.shape[0]):
        picked = jnp.take_along_axis(jnp.broadcast_to(table[r : r + 1], row.shape), lane, axis=1, mode="promise_in_bounds")
        out = jnp.where(row == r, picked, out)
    return out


def find(table, index):
    return look_up(table, index >> 7, index & 127)


def swap_x(block):
    return jnp.swapaxes(block, 0, 1)


def cell_hot(index_row, low=0, high=ROWS):
    count = index_row.shape[1]
    columns = iota((128, count), 0) == (index_row & 127)
    rows = iota((high - low, count), 0) == (index_row >> 7) - low
    return columns.astype(bf16), rows.astype(bf16)


def scatter(tables, columns, rows):
    height = rows.shape[0]
    stacked = []
    for table in tables:
        for part in parts(table):
            row = as_row(part.astype(f32))
            tall = jnp.broadcast_to(row, (16, row.shape[1])).astype(bf16)
            stacked.append(rows * jnp.concatenate([tall] * (height // 16), axis=0))
    sums = dot_nt(jnp.concatenate(stacked, axis=0), columns)
    return [
        (sums[2 * i * height : (2 * i + 1) * height] + sums[(2 * i + 1) * height : (2 * i + 2) * height]).reshape(-1, 8, 128)
        for i in range(len(tables))
    ]


def side_rows(side, count):
    height = (count + 1) // 2 * 16
    return ((0, ROWS), (ROWS - height, ROWS), (0, height))[0 if side == 1 else 1 + side // 2]


def gather_wide(sums, count):
    left, middle, right = sums
    if count == 0:
        return middle
    return jnp.concatenate([left[left.shape[0] - count :], middle, right[:count]], axis=0)


def scatter_wide(tables, late, columns_ref, rows_ref, count):
    fields = max(len(tables), 1)
    found = []
    for side in range(3):
        if side != 1 and count == 0:
            found.append([None] * fields)
            continue
        low, high = side_rows(side, count)
        index = as_row(late[side][:4].astype(i32) - 1)
        (sums,) = scatter([late[side][4:]], *cell_hot(index, low, high))
        if tables:
            *others, last = scatter([table[side] for table in tables], columns_ref[side], rows_ref[side, low:high])
            found.append([*others, last + sums])
        else:
            found.append([sums])
    return [gather_wide([found[side][i] for side in range(3)], count) for i in range(fields)]


def faces_of(field):
    if field.shape[0] >= 128:
        turned = field.T
        return turned[0:1], turned[127:128]
    rows = iota((16, 128), 0)
    lanes = iota((16, 128), 1)
    pick = (((rows == 0) & (lanes == 0)) | ((rows == 1) & (lanes == 127))).astype(bf16)
    both = dot_nt(jnp.concatenate([pick, pick], axis=1), jnp.concatenate(parts(field), axis=1))
    return both[0:1], both[1:2]


def columns_of(left, right):
    width = left.shape[1]
    row = iota((128, width), 0)
    return jnp.where(row == 0, left, jnp.where(row == 127, right, 0.0)).T


def up_y(v, halo):
    return jnp.where(iota(v.shape, 2) == 127, halo, pltpu.roll(v, 127, 2))


def down_y(v, first):
    return jnp.where(iota(v.shape, 2) == 0, first, pltpu.roll(v, 1, 2))


def stencil(tx_up, tx_down, ty, tz, ty_first, field, halo):
    middle = field[1:-1]
    out = tx_up * field[2:] + tx_down * field[:-2]
    out = out + ty * up_y(middle, halo) + down_y(ty * middle, ty_first * halo)
    return out + tz * pltpu.roll(middle, 7, 1) + pltpu.roll(tz * middle, 1, 1)


def harmonic(first, second):
    both = first + second
    return jnp.where(both > 0.0, 2.0 * first * second / jnp.where(both > 0.0, both, 1.0), 0.0)


def read_faces(me, got_ref, start, width, across=0):
    along = me & 15
    line = (me >> 4) + across // 16
    inside = (line >= 0) & (line < 8)
    before = got_ref[jnp.clip(me + across - 1, 0, TILES - 1), :, start : start + width]
    after = got_ref[jnp.clip(me + across + 1, 0, TILES - 1), :, start : start + width]
    return jnp.where(inside & (along > 0), before, 0.0), jnp.where(inside & (along < 15), after, 0.0)


def put_faces(me, out_ref, start, first, last, across=0):
    width = first.shape[1]
    for at, face in ((me + across - 1, first), (me + across + 1, last)):
        out_ref[jnp.where((at >= 0) & (at < TILES), at, me), :, start : start + width] = face


def edge_codes(delta_ref, to_ref, b):
    block = b + delta_ref[b]
    code = block * 256 + to_ref[b]
    return jnp.where(block < 4, code, -1), jnp.where(block >= 4, code - 1024, -1)


def spread(rows, shift):
    lane = iota(rows.shape, 1)
    inside = (lane >= shift) if shift > 0 else (lane < TILES + shift)
    return jnp.where(inside, pltpu.roll(rows, shift % TILES, 1), 0.0)


def store_slots(out_ref, rows):
    for i in range(0, rows.shape[0], 128):
        part = rows[i : i + 128].T
        out_ref[:, 0, i : i + part.shape[1]] = part


def load_slots(got_ref, count):
    return jnp.concatenate([got_ref[:, 0, i : i + 128].T for i in range(0, count, 128)], axis=0)


def begin_kernel(me_ref, *refs):
    count = len(refs) // 2 - 2
    given, (out_ref, seg_ref, tile_out_ref), held, sems = refs[:count], refs[count : count + 3], refs[count + 3 : -1], refs[-1]
    copies = [pltpu.make_async_copy(a, b, sems.at[i]) for i, (a, b) in enumerate(zip(given, held))]
    passing = [pltpu.make_async_copy(held[8 + i], tile_out_ref.at[i], sems.at[count + i]) for i in range(3)]
    for copy in copies:
        copy.start()
    for copy in copies:
        copy.wait()
    for copy in passing:
        copy.start()
    tile_ref, layer_ref, cell_ref, press_frac_ref, accum_ref, chain_ref, mf_ref, fm_ref = held[:8]
    press_ref, cond_ref, accum_matrix_ref = held[8:11]
    delta_ref, from_ref, to_ref, trans_ref, well_tile_ref, well_cell_ref, well_rate_ref = held[11:]
    me = me_ref[0]
    code = seg_code()
    owner = fold(tile_ref[...])
    owner_row = as_row(owner)
    hot = owner_hot(owner_row)
    before = (iota((128, 128), 0) < iota((128, 128), 1)).astype(bf16)
    base = jnp.zeros((TILES, 1), f32)
    ranks = []
    for c in range(8):
        part = hot[:, c * 128 : (c + 1) * 128]
        wide = part.astype(f32)
        count = dot_nn(part, before) + base
        ranks.append(jnp.sum(wide * count, axis=0, keepdims=True))
        base = base + jnp.sum(wide, axis=1, keepdims=True)
    rank_row = jnp.concatenate(ranks, axis=1).astype(i32)
    rank = as_rows(rank_row)
    mask = rank_mask(rank_row)

    press = fold(press_frac_ref[...])
    fm = fold(fm_ref[...])
    mf = fold(mf_ref[...])
    last = code % 256 == 255
    tnext = jnp.where(last, 0.0, fold(chain_ref[...]))
    tprev = pltpu.roll(tnext, 1, 1)
    tprev = jnp.where(iota((8, 128), 1) == 0, pltpu.roll(tprev, 4, 0), tprev)
    diag = fold(accum_ref[...]) + tnext + tprev + fm
    inverse = 1.0 / diag
    partial = diag * press - chain(tnext, press)
    heres = [edge_codes(delta_ref, to_ref, b)[0] for b in range(4)]
    for b, picked in enumerate(totals([jnp.where(code == here, press, 0.0) for here in heres])):
        at = code == b * 256 + from_ref[b]
        partial = partial - jnp.where(at, trans_ref[b] * picked, 0.0)
    cell = fold(cell_ref[...])
    where_cell = ((((cell >> 7) * 8 + fold(layer_ref[...])) << 7) + (cell & 127) + 1).astype(f32)
    position = (iota((8, 128), 0) * 128 + iota((8, 128), 1) + 1).astype(f32)
    weight = fm * inverse
    slots = to_slots([where_cell, mf * press, weight * fm, weight * mf, weight * partial, position], hot, mask)
    inverse_index, slots = slots[80:96], slots[:80]
    place = (owner * CAP + rank).astype(f32)
    rows = []
    for b in range(4):
        _, there = edge_codes(delta_ref, to_ref, b)
        at = code == b * 256 + from_ref[b]
        gain = trans_ref[b] * inverse
        rows.append(jnp.where(iota((1, 128), 1) == 0, there.astype(f32), 0.0))
        for value in (place, where_cell, gain * fm, gain * partial, gain * trans_ref[b], gain * mf, code.astype(f32), gain):
            rows.append(jnp.sum(jnp.where(at, value, 0.0), axis=0, keepdims=True))
        rows.append(jnp.zeros((3, 128), f32))
    edges = [jnp.broadcast_to(jnp.sum(jnp.concatenate(rows, axis=0), axis=1, keepdims=True), (48, 128))]
    rows = edges + to_three(slots) + [spread(slots[:CAP], shift) for shift in BESIDE]
    store_slots(out_ref, jnp.concatenate(rows, axis=0))
    first_face, last_face = faces_of(jnp.concatenate([swap_x(ref[...]).reshape(ROWS, 128) for ref in (press_ref, cond_ref)], axis=0))
    for across in (-16, 0, 16):
        put_faces(me, out_ref, 384, first_face, last_face, across)
    for i, value in enumerate((tnext, inverse, partial, fm, mf, owner.astype(f32), rank.astype(f32), press)):
        seg_ref[i] = value
    for i in range(2):
        seg_ref[8 + i] = inverse_index[8 * i : 8 * i + 8] - 1.0
    lane = iota((8, 128), 1)
    own = jnp.zeros((8, 128), f32)
    for b in range(4):
        here, there = edge_codes(delta_ref, to_ref, b)
        for i, value in enumerate((b * 256 + from_ref[b], here, there)):
            own = jnp.where(lane == 8 * b + i, value.astype(f32), own)
        own = jnp.where(lane == 8 * b + 3, trans_ref[b], own)
    seg_ref[10] = own
    plane_x = iota((EXT, 128), 0) + ((me >> 4) - 1) * 8
    plane_y = iota((EXT, 128), 1) + (me & 15) * 128
    source = jnp.zeros((EXT, 128), f32)
    for w in range(well_tile_ref.shape[0]):
        tile = well_tile_ref[w]
        cell = well_cell_ref[w]
        at = (plane_x == (tile >> 4) * 8 + (cell >> 7)) & (plane_y == (tile & 15) * 128 + (cell & 127))
        source = source + jnp.where(at, well_rate_ref[w], 0.0)
    for i in range(3):
        seg_ref[11 + i] = source[8 * i : 8 * i + 8]
    seg_ref[14] = where_cell
    for i, ref in enumerate((press_ref, cond_ref, accum_matrix_ref)):
        seg_ref[15 + 8 * i : 23 + 8 * i] = swap_x(ref[...])
    for copy in passing:
        copy.wait()


def edge_in(row, k, i):
    at = 12 * k + i
    return row[:, at : at + 1]


def cells_kernel(
    me_ref,
    got_ref, inside_ref, across_ref, seg_ref,
    out_ref, cells_ref, field_ref, index_ref, columns_ref, rows_ref, edge_ref, beside_ref, res_ref,
):
    me = me_ref[0]
    slots = load_slots(got_ref, 384)
    even = ((me >> 4) & 1) == 0
    press, cond, accum = (
        jnp.concatenate(
            [swap_x(jnp.where(even, b, a)), seg_ref[15 + 8 * i : 23 + 8 * i], swap_x(jnp.where(even, a, b))], axis=0
        )
        for i, a, b in ((i, inside_ref[i], across_ref[i]) for i in range(3))
    )
    sums = []
    for side in range(3):
        table = slots[48 + side * 80 : 128 + side * 80]
        index = table[:CAP].astype(i32) - 1
        if side == 1:
            index_ref[...] = index
            own = index
        columns, rows = cell_hot(as_row(index))
        columns_ref[side] = columns
        rows_ref[side] = rows
        sums.append(scatter([table[i : i + CAP] for i in range(CAP, 5 * CAP, CAP)], columns, rows))
    flow, weight, mirror, first = (jnp.concatenate([sums[side][i] for side in range(3)], axis=0) for i in range(4))
    beside = slots[288:384].astype(i32) - 1
    along = me & 15
    for i, (there, column) in enumerate(((along > 0, 127), (along < 15, 0))):
        part = beside[48 * i : 48 * i + 48]
        beside_ref[48 * i : 48 * i + 48] = jnp.where(there & (part >= 0) & ((part & 127) == column), part >> 7, -1)

    halos = [columns_of(*read_faces(me, got_ref, 384, 2 * ROWS, across)) for across in (-16, 0, 16)]
    press_halo = jnp.concatenate([halo[:ROWS].reshape(8, 8, 128) for halo in halos], axis=0)
    cond_halo = jnp.concatenate([halo[ROWS:].reshape(8, 8, 128) for halo in halos], axis=0)
    wide = (EXT, 8, 128)
    tx = harmonic(cond[:-1], cond[1:])
    ty = harmonic(cond, up_y(cond, cond_halo))
    tz = 0.5 * harmonic(cond, jnp.where(iota(wide, 1) == 7, 0.0, pltpu.roll(cond, 7, 1)))
    ty_first = jnp.where(iota(wide, 2) == 0, harmonic(cond, cond_halo), 0.0)
    diag = accum + ty + down_y(ty, ty_first) + tz + pltpu.roll(tz, 1, 1)
    diag = diag[1:-1] + tx[1:] + tx[:-1]
    inverse = jnp.where(diag > 0.0, 1.0 / jnp.where(diag > 0.0, diag, 1.0), 0.0)
    source = jnp.concatenate([seg_ref[11 + i] for i in range(3)], axis=0)

    res = diag * press[1:-1] - flow[1:-1] - source.reshape(EXT, 1, 128)[1:-1]
    res = res - stencil(tx[1:], tx[:-1], ty[1:-1], tz[1:-1], ty_first[1:-1], press, press_halo[1:-1])
    field = inverse * res
    cells_ref[0, : EXT - 1] = tx
    for i, value in ((1, ty), (2, tz), (3, ty_first), (6, first - weight * press), (7, mirror)):
        cells_ref[i] = value
    cells_ref[4, 1 : EXT - 1] = inverse
    cells_ref[5, 1 : EXT - 1] = res
    field_ref[...] = field
    res_ref[...] = swap_x(res[7:15])

    code = seg_code().astype(f32)
    _, inverse_f, partial, fm, _, owner, _, press_f = (seg_ref[i] for i in range(8))
    edge = jnp.where(me > 0, got_ref[before(me), :, 0:128], -1.0)
    lane = iota((1, 128), 1)
    cells, terms, picks, found = [], [], [], []
    ends = [code == edge_in(edge, k, 0) for k in range(4)]
    wanted = (press_f, owner, seg_ref[14], fm * inverse_f)
    sums = totals([jnp.where(at, value, 0.0) for at in ends for value in wanted])
    for k in range(4):
        picked = sums[4 * k]
        at = (lane == (edge_in(edge, k, 1).astype(i32) >> 4)) & (edge_in(edge, k, 0) >= 0.0)
        cells.append(jnp.where(at, edge_in(edge, k, 2), 0.0))
        terms.append(jnp.where(at, -edge_in(edge, k, 3) * picked, 0.0))
        picks.append(jnp.broadcast_to(picked, (1, 128)))
        found.append(sums[4 * k + 1 : 4 * k + 4])
    for k in range(4):
        edge = jnp.where(lane == 12 * k + 4, edge - edge_in(edge, k, 5) * sums[4 * k], edge)
    edge_ref[...] = jnp.broadcast_to(edge, (8, 128))
    late = jnp.concatenate(cells + terms, axis=0)

    taken = [find(press[8:16].reshape(ROWS, 128), own), find(own_tile(field, 1), own)]
    rows = taken + [spread(taken[0], 1)]
    store_slots(out_ref, jnp.concatenate(rows + to_three(late) + picks + [jnp.zeros((52, 128), f32)], axis=0))
    put_faces(me, out_ref, FIRST, *faces_of(field[1:-1].reshape(-1, 128)))
    put_faces(me, out_ref, FIRST_INVERSE, *faces_of(inverse[3:19].reshape(-1, 128)))
    put_entries(out_ref, before(me), FIRST_ENDS, [end for ends in found for end in ends])


def put_entries(out_ref, at, start, entries):
    lane = iota((1, len(entries)), 1)
    row = jnp.zeros(lane.shape, f32)
    for i, entry in enumerate(entries):
        row = jnp.where(lane == i, entry, row)
    out_ref[at, :, start : start + len(entries)] = row


def get_entries(got_ref, at, start, count):
    row = got_ref[at, :, start : start + count]
    return [row[:, i : i + 1] for i in range(count)]


def before(me):
    return jnp.maximum(me - 1, 0)


def after(me):
    return jnp.minimum(me + 1, TILES - 1)


FIRST = 76
FIRST_ENDS = FIRST + 160
FIRST_INVERSE = FIRST_ENDS + 12
WIDE = 232
SLIM = 128
SLIM_TWO = 248


def wide_lanes(k):
    entries = WIDE + 8 * (22 - 2 * k)
    return entries, entries + 4


def own_edges(seg_ref):
    own = seg_ref[10][0:1]
    return [[own[:, 8 * b + i : 8 * b + i + 1] for b in range(4)] for i in range(4)]


def edge_terms(code, edges, frac):
    starts, _, _, factors = edges
    sums = totals([jnp.where(code == start, frac, 0.0) for start in starts])
    return [factor * picked for factor, picked in zip(factors, sums)]


def arrive(code, targets, terms):
    gain = jnp.zeros(code.shape, f32)
    for target, term in zip(targets, terms):
        gain = gain + jnp.where(code == target, term, 0.0)
    return gain


def late_rows(edges, ends, terms):
    lane = iota((1, 128), 1)
    cells, values = [], []
    for there, (tile, cell, weight), term in zip(edges[2], ends, terms):
        at = (lane == tile.astype(i32)) & (there >= 0.0)
        cells.append(jnp.where(at, cell, 0.0))
        values.append(jnp.where(at, weight * term, 0.0))
    return jnp.concatenate(cells + values, axis=0)


def to_three(rows):
    return [spread(rows, 16), rows, spread(rows, -16)]


def own_tile(field, k):
    return field[8 - k : 16 - k].reshape(ROWS, 128)


def starts_of(edge, table):
    place = (iota((CAP, 128), 1) * CAP + iota((CAP, 128), 0)).astype(f32)
    return totals([jnp.where(place == edge_in(edge, k, 1), table, 0.0) for k in range(4)])


def advance(cells_ref, k, field, halo, flow):
    low, high = k + 1, EXT - 1 - k
    ty, tz, ty_first, inverse, res = (cells_ref[i, low:high] for i in range(1, 6))
    tx_up, tx_down = cells_ref[0, low:high], cells_ref[0, low - 1 : high - 1]
    return inverse * (res + stencil(tx_up, tx_down, ty, tz, ty_first, field, halo) + flow)


def wide_halo(me, got_ref, start, count):
    return columns_of(*read_faces(me, got_ref, start, 8 * count)).reshape(count, 8, 128)


def ends_of(ends_ref):
    held = ends_ref[0:1]
    return [[held[:, 3 * k + i : 3 * k + i + 1] for i in range(3)] for k in range(4)]


def send_wide(me, out_ref, k, code, edges, ends, seg_ref, cells_ref, index_ref, field, frac, resf):
    tnext, inverse_f, fm = seg_ref[0], seg_ref[1], seg_ref[3]
    terms = edge_terms(code, edges, frac)
    ahead = inverse_f * (resf + chain(tnext, frac) + arrive(code, edges[1], terms))
    part = advance(cells_ref, k, field, jnp.zeros((22 - 2 * k, 8, 128), f32), 0.0)
    position = jnp.concatenate([seg_ref[8], seg_ref[9]], axis=0).astype(i32)
    now = find(fm * frac, position)
    rows = [find(own_tile(field, k), index_ref[...])] + to_three(now) + to_three(find(fm * ahead, position))
    rows += to_three(late_rows(edges, ends, terms)) + [spread(now, shift) for shift in BESIDE]
    store_slots(out_ref, jnp.concatenate(rows + [jnp.zeros((24, 128), f32)], axis=0))
    entries, further = wide_lanes(k)
    put_faces(me, out_ref, WIDE, *faces_of(field[1:-1].reshape(-1, 128)))
    put_faces(me, out_ref, further, *faces_of(part[1:-1].reshape(-1, 128)))
    put_entries(out_ref, jnp.where(me + 1 < TILES, me + 1, me), entries, terms)


def first_kernel(
    me_ref, got_ref, cells_ref, field_ref, index_ref, columns_ref, rows_ref, seg_ref, edge_ref,
    out_ref, new_field_ref, new_frac_ref, resf_ref, ends_ref, halo_inverse_ref, res_fracture_ref,
):
    me = me_ref[0]
    slots = load_slots(got_ref, 128)
    code = seg_code().astype(f32)
    tnext, inverse_f, partial, fm, mf, owner, rank = (seg_ref[i] for i in range(7))
    owner = owner.astype(i32)
    rank = rank.astype(i32)
    edge = edge_ref[0:1]
    edges = own_edges(seg_ref)
    starts, targets, nexts, factors = edges

    resf = partial - fm * look_up(slots[0:16], rank, owner)
    picks = get_entries(got_ref, after(me), 72, 4)
    for b in range(4):
        at = (code == starts[b]) & (nexts[b] >= 0.0)
        resf = resf - jnp.where(at, factors[b] * picks[b], 0.0)
    frac = inverse_f * resf
    terms = edge_terms(code, edges, frac)
    begun = starts_of(edge, slots[32:48])
    coming = [edge_in(edge, k, 4) - edge_in(edge, k, 3) * begun[k] for k in range(4)]
    gain = resf + chain(tnext, frac) + mf * look_up(slots[16:32], rank, owner)
    gain = gain + arrive(code, targets, terms) + arrive(code, [edge_in(edge, k, 0) for k in range(4)], coming)
    frac = inverse_f * gain
    late = [slots[48 + 8 * side : 56 + 8 * side] for side in range(3)]
    (flow,) = scatter_wide([], late, columns_ref, rows_ref, 6)
    field = advance(cells_ref, 1, field_ref[...], wide_halo(me, got_ref, FIRST, 20), flow + cells_ref[6, 2:22])
    new_field_ref[...] = field
    new_frac_ref[...] = frac
    resf_ref[...] = resf
    res_fracture_ref[...] = unfold(resf)
    halo_inverse_ref[...] = wide_halo(me, got_ref, FIRST_INVERSE, 16)
    ends = get_entries(got_ref, after(me), FIRST_ENDS, 12)
    ends = [ends[3 * k : 3 * k + 3] for k in range(4)]
    lane = iota((8, 128), 1)
    held = jnp.zeros((8, 128), f32)
    for k in range(4):
        for i in range(3):
            held = jnp.where(lane == 3 * k + i, ends[k][i], held)
    ends_ref[...] = held

    send_wide(me, out_ref, 2, code, edges, ends, seg_ref, cells_ref, index_ref, field, frac, resf)


def even_kernel(
    k, me_ref, got_ref, cells_ref, field_ref, index_ref, columns_ref, rows_ref, seg_ref, edge_ref,
    frac_ref, resf_ref, ends_ref, halo_inverse_ref, beside_ref,
    out_ref, third_ref, new_field_ref, new_frac_ref,
):
    me = me_ref[0]
    slots = load_slots(got_ref, 256)
    code = seg_code().astype(f32)
    tnext, inverse_f, _, fm, mf, owner, rank = (seg_ref[i] for i in range(7))
    edge = edge_ref[0:1]
    edges = own_edges(seg_ref)
    targets = edges[1]
    resf = resf_ref[...]
    frac = frac_ref[...]
    entries, further = wide_lanes(k)
    coming = get_entries(got_ref, before(me), entries, 4)
    gain = resf + chain(tnext, frac) + mf * look_up(slots[0:16], rank.astype(i32), owner.astype(i32))
    gain = gain + arrive(code, targets, edge_terms(code, edges, frac))
    gain = gain + arrive(code, [edge_in(edge, b, 0) for b in range(4)], coming)
    frac = inverse_f * gain
    terms = edge_terms(code, edges, frac)
    ahead = inverse_f * (resf + chain(tnext, frac) + arrive(code, targets, terms))
    new_frac_ref[...] = frac

    tables = [[slots[first + side * CAP : first + CAP + side * CAP] for side in range(3)] for first in (16, 64)]
    late = [slots[112 + 8 * side : 120 + 8 * side] for side in range(3)]
    flow, later = scatter_wide(tables, late, columns_ref, rows_ref, 7 - k)
    beside = []
    for side in range(3):
        height = ROWS if side == 1 else 8 * (6 - k)
        level = iota((height, 128), 0) + (ROWS - height if side == 0 else 0)
        lane = iota((height, 128), 1)
        column = jnp.zeros((height, 128), f32)
        for i, at in enumerate((0, 127)):
            first = 48 * i + CAP * side
            held = jnp.zeros((height, 128), f32)
            for r in range(first, first + CAP):
                held = held + jnp.where(level == beside_ref[r : r + 1], slots[136 + r : 137 + r], 0.0)
            column = jnp.where(lane == at, jnp.sum(held, axis=1, keepdims=True), column)
        beside.append(column.reshape(-1, 8, 128))
    beside = jnp.concatenate(beside, axis=0)
    second = field_ref[...]
    third = advance(cells_ref, k, second, wide_halo(me, got_ref, WIDE, 22 - 2 * k), flow)
    inner = second[2:-2]
    lane = iota(inner.shape, 2)
    joint = jnp.where(lane == 0, cells_ref[3, k + 2 : 22 - k], jnp.where(lane == 127, cells_ref[1, k + 2 : 22 - k], 0.0))
    halo = wide_halo(me, got_ref, further, 20 - 2 * k) + halo_inverse_ref[k - 2 : 18 - k] * (joint * inner + beside)
    field = advance(cells_ref, k + 1, third, halo, later[1:-1] + cells_ref[7, k + 2 : 22 - k] * inner)
    third_ref[...] = third
    new_field_ref[...] = field

    position = jnp.concatenate([seg_ref[8], seg_ref[9]], axis=0).astype(i32)
    ends = ends_of(ends_ref)
    own_third = find(own_tile(third, k + 1), index_ref[...])
    rows = [own_third, find(own_tile(field, k + 2), index_ref[...]), spread(own_third, 1)] + to_three(find(fm * ahead, position))
    rows += to_three(late_rows(edges, ends, terms))
    store_slots(out_ref, jnp.concatenate(rows + [jnp.zeros((8, 128), f32)], axis=0))
    put_faces(me, out_ref, SLIM, *faces_of(field[1:-1].reshape(-1, 128)))
    to_next = jnp.where(me + 1 < TILES, me + 1, me)
    put_entries(out_ref, to_next, SLIM + 8 * (18 - 2 * k), terms + edge_terms(code, edges, ahead))
    put_entries(out_ref, jnp.where(me + 2 < TILES, me + 2, me), SLIM_TWO, terms + edges[2])


def odd_kernel(
    k, final, me_ref, got_ref, cells_ref, field_ref, index_ref, columns_ref, rows_ref, seg_ref, edge_ref,
    frac_ref, resf_ref, ends_ref, third_ref, *outs,
):
    me = me_ref[0]
    slots = load_slots(got_ref, 128)
    code = seg_code().astype(f32)
    tnext, inverse_f, _, _, mf, owner, rank = (seg_ref[i] for i in range(7))
    owner = owner.astype(i32)
    rank = rank.astype(i32)
    edge = edge_ref[0:1]
    edges = own_edges(seg_ref)
    targets = edges[1]
    resf = resf_ref[...]
    frac = frac_ref[...]
    coming = get_entries(got_ref, before(me), SLIM + 8 * (22 - 2 * k), 8)
    two = jnp.where(me > 1, got_ref[jnp.maximum(me - 2, 0), :, 128:256], -1.0)
    lane = iota((1, 128), 1)
    codes = jnp.where((lane >= SLIM_TWO - 128) & (lane < SLIM_TWO - 124), pltpu.roll(two, 124, 1), -2.0)
    meets = jnp.concatenate([jnp.where(codes == edge_in(edge, b, 7), two, 0.0) for b in range(4)], axis=0)
    meets = jnp.sum(meets, axis=1, keepdims=True)
    begun = starts_of(edge, slots[32:48])
    heres = [edge_in(edge, b, 0) for b in range(4)]
    gain = resf + chain(tnext, frac) + mf * look_up(slots[0:16], rank, owner)
    gain = gain + arrive(code, targets, edge_terms(code, edges, frac))
    frac = inverse_f * (gain + arrive(code, heres, coming[:4]))
    terms = [
        coming[4 + b] + edge_in(edge, b, 6) * begun[b] + edge_in(edge, b, 8) * meets[b : b + 1] for b in range(4)
    ]
    gain = resf + chain(tnext, frac) + mf * look_up(slots[16:32], rank, owner)
    gain = gain + arrive(code, targets, edge_terms(code, edges, frac))
    frac = inverse_f * (gain + arrive(code, heres, terms))

    late = [slots[96 + 8 * side : 104 + 8 * side] for side in range(3)]
    tables = [[slots[48 + side * CAP : 64 + side * CAP] for side in range(3)]]
    (flow,) = scatter_wide(tables, late, columns_ref, rows_ref, 7 - k)
    flow = flow + cells_ref[7, k + 1 : 23 - k] * third_ref[2:-2]
    field = advance(cells_ref, k, field_ref[...], wide_halo(me, got_ref, SLIM, 22 - 2 * k), flow)
    if final:
        adj_matrix_ref, adj_fracture_ref = outs
        adj_matrix_ref[...] = swap_x(field)
        adj_fracture_ref[...] = unfold(frac)
        return
    out_ref, new_field_ref, new_frac_ref = outs
    new_field_ref[...] = field
    new_frac_ref[...] = frac
    send_wide(me, out_ref, k + 1, code, edges, ends_of(ends_ref), seg_ref, cells_ref, index_ref, field, frac, resf)


def hold_kernel(given_ref, out_ref):
    out_ref[...] = given_ref[...]


def call(kernel, name, scalars, arrays, outs, space=pltpu.VMEM, scratch=(), limit=20 * 1024 * 1024, out_spaces=None):
    spec = [pl.BlockSpec(memory_space=pltpu.SMEM)] * len(scalars)
    spec += [pl.BlockSpec(memory_space=space)] * len(arrays)
    return pl.pallas_call(
        kernel,
        name=name,
        out_shape=[jax.ShapeDtypeStruct(shape, kind) for shape, kind in outs],
        in_specs=spec,
        out_specs=[pl.BlockSpec(memory_space=out) for out in out_spaces or [pltpu.VMEM] * len(outs)],
        scratch_shapes=list(scratch),
        compiler_params=pltpu.CompilerParams(vmem_limit_bytes=limit),
    )(*scalars, *arrays)


def exchange(message):
    return lax.all_to_all(message, ALL, split_axis=0, concat_axis=0, tiled=True)


def swapped(block, first):
    pairs = [(i, i + 1) for i in range(first, lax.axis_size("gx") - 1, 2)]
    return lax.ppermute(block, "gx", pairs + [(j, i) for i, j in pairs])


def body(
    press_matrix, cond_matrix, accum_matrix, press_frac, accum_frac, trans_chain, couple_mf, couple_fm,
    conn_tile, conn_layer, conn_cell, inter_delta, inter_from, inter_to, inter_trans, well_tile, well_cell, well_rate,
):
    me = lax.axis_index(ALL).astype(i32).reshape(1)
    wide = (EXT, 8, 128)
    tile = (LAYERS, 8, 128)
    seg = (8, 128)

    given = (
        conn_tile, conn_layer, conn_cell, press_frac, accum_frac, trans_chain, couple_mf, couple_fm,
        press_matrix, cond_matrix, accum_matrix,
        inter_delta, inter_from, inter_to, inter_trans, well_tile, well_cell, well_rate,
    )
    message, segs, stacked = call(
        begin_kernel,
        "begin",
        (me,),
        given,
        [((TILES, 1, 512), f32), ((39, *seg), f32), ((3, *tile), f32)],
        pl.ANY,
        [(pltpu.VMEM if a.ndim > 1 else pltpu.SMEM)(a.shape, a.dtype) for a in given] + [pltpu.SemaphoreType.DMA((len(given) + 3,))],
        64 * 1024 * 1024,
        [pltpu.VMEM, pltpu.VMEM, pl.ANY],
    )
    inside = swapped(stacked, 0)
    across = swapped(stacked, 1)
    (segs,) = call(hold_kernel, "hold", (), (segs,), [(segs.shape, f32)])
    got = exchange(message)
    message, cells, field, index, columns, rows, edge, beside, res_matrix = call(
        cells_kernel,
        "cells",
        (me,),
        (got, inside, across, segs),
        [((TILES, 1, 384), f32), ((8, *wide), f32), ((22, 8, 128), f32), ((CAP, 128), i32), ((3, 128, SLOTS), bf16),
         ((3, ROWS, SLOTS), bf16), (seg, f32), ((96, 128), i32), (tile, f32)],
    )
    kept = (index, columns, rows, segs, edge)

    def after_sweeps(k):
        return ((EXT - 2 * k, 8, 128), f32)

    wide_message = ((TILES, 1, 512), f32)
    slim_message = ((TILES, 1, 256), f32)
    got = exchange(message)
    message, field, frac, resf, ends, halo_inverse, res_fracture = call(
        first_kernel,
        "first",
        (me,),
        (got, cells, field, *kept),
        [wide_message, after_sweeps(2), (seg, f32), (seg, f32), (seg, f32), ((16, 8, 128), f32), ((4, 256), f32)],
    )
    for k, final in ((2, False), (5, True)):
        got = exchange(message)
        message, third, field, frac = call(
            functools.partial(even_kernel, k),
            "even",
            (me,),
            (got, cells, field, *kept, frac, resf, ends, halo_inverse, beside),
            [slim_message, after_sweeps(k + 1), after_sweeps(k + 2), (seg, f32)],
        )
        got = exchange(message)
        outs = [(tile, f32), ((4, 256), f32)] if final else [wide_message, after_sweeps(k + 3), (seg, f32)]
        results = call(
            functools.partial(odd_kernel, k + 2, final),
            "odd",
            (me,),
            (got, cells, field, *kept, frac, resf, ends, third),
            outs,
        )
        if not final:
            message, field, frac = results
    adj_matrix, adj_fracture = results
    return res_matrix, res_fracture, adj_matrix, adj_fracture


def solution(mesh):
    cells = P(None, "gx", YA)
    segs = P(ALL, None)
    blocks = P(ALL)
    in_specs = (cells,) * 3 + (segs,) * 8 + (blocks,) * 4 + (P(),) * 3
    return jax.shard_map(body, mesh=mesh, in_specs=in_specs, out_specs=(cells, segs, cells, segs), check_vma=False)
```

```python
import functools

import jax
import jax.numpy as jnp
from jax import lax
from jax.experimental import pallas as pl
from jax.experimental.pallas import tpu as pltpu
from jax.sharding import PartitionSpec as P

ITERS = 8
CAP = 16
TILES = 128
ROWS = 64
EXT = 24
LAYERS = 8
SLOTS = CAP * TILES
ALL = ("gx", "gy", "af")
YA = ("gy", "af")
BESIDE = (17, 1, -15, 15, -1, -17)
f32 = jnp.float32
bf16 = jnp.bfloat16
i32 = jnp.int32


def iota(shape, axis):
    return lax.broadcasted_iota(i32, shape, axis)


def parts(value):
    high = value.astype(bf16)
    return high, (value - high.astype(f32)).astype(bf16)


def dot_nn(a, b):
    return lax.dot_general(a, b, (((1,), (0,)), ((), ())), preferred_element_type=f32)


def dot_nt(a, b):
    return lax.dot_general(a, b, (((1,), (1,)), ((), ())), preferred_element_type=f32)


def dot_tn(a, b):
    return lax.dot_general(a, b, (((0,), (0,)), ((), ())), preferred_element_type=f32)


def as_row(rows):
    return jnp.concatenate([rows[i : i + 1] for i in range(rows.shape[0])], axis=1)


def as_rows(row):
    return jnp.concatenate([row[:, i : i + 128] for i in range(0, row.shape[1], 128)], axis=0)


def totals(values):
    rows = jnp.concatenate([jnp.sum(value, axis=0, keepdims=True) for value in values], axis=0)
    sums = jnp.sum(rows, axis=1, keepdims=True)
    return [sums[i : i + 1] for i in range(len(values))]


def fold(value):
    return jnp.concatenate([value[:, :128], value[:, 128:]], axis=0)


def unfold(value):
    return jnp.concatenate([value[:4], value[4:]], axis=1)


def seg_code():
    row = iota((8, 128), 0)
    return (row % 4) * 256 + (row // 4) * 128 + iota((8, 128), 1)


def chain(tnext, field):
    lane = iota((8, 128), 1)
    ahead = pltpu.roll(field, 127, 1)
    ahead = jnp.where(lane == 127, pltpu.roll(ahead, 4, 0), ahead)
    behind = pltpu.roll(tnext * field, 1, 1)
    behind = jnp.where(lane == 0, pltpu.roll(behind, 4, 0), behind)
    return tnext * ahead + behind


def owner_hot(owner_row):
    return (iota((TILES, 1024), 0) == owner_row).astype(bf16)


def rank_mask(rank_row):
    return iota((CAP, 1024), 0) == rank_row


def to_slots(values, hot, mask):
    halves = ([], [])
    for value in values:
        row = as_row(value)
        for half, part in zip(halves, parts(row)):
            half.append(jnp.where(mask, part.astype(f32), 0.0).astype(bf16))
    both = jnp.concatenate([jnp.concatenate(half, axis=0) for half in halves], axis=1)
    return dot_nt(both, jnp.concatenate([hot, hot], axis=1))


def look_up(table, row, lane):
    out = jnp.zeros(row.shape, f32)
    for r in range(table.shape[0]):
        picked = jnp.take_along_axis(jnp.broadcast_to(table[r : r + 1], row.shape), lane, axis=1, mode="promise_in_bounds")
        out = jnp.where(row == r, picked, out)
    return out


def find(table, index):
    return look_up(table, index >> 7, index & 127)


def swap_x(block):
    return jnp.swapaxes(block, 0, 1)


def cell_hot(index_row, low=0, high=ROWS):
    count = index_row.shape[1]
    columns = iota((128, count), 0) == (index_row & 127)
    rows = iota((high - low, count), 0) == (index_row >> 7) - low
    return columns.astype(bf16), rows.astype(bf16)


def scatter(tables, columns, rows):
    height = rows.shape[0]
    stacked = []
    for table in tables:
        for part in parts(table):
            row = as_row(part.astype(f32))
            tall = jnp.broadcast_to(row, (16, row.shape[1])).astype(bf16)
            stacked.append(rows * jnp.concatenate([tall] * (height // 16), axis=0))
    sums = dot_nt(jnp.concatenate(stacked, axis=0), columns)
    return [
        (sums[2 * i * height : (2 * i + 1) * height] + sums[(2 * i + 1) * height : (2 * i + 2) * height]).reshape(-1, 8, 128)
        for i in range(len(tables))
    ]


def side_rows(side, count):
    height = (count + 1) // 2 * 16
    return ((0, ROWS), (ROWS - height, ROWS), (0, height))[0 if side == 1 else 1 + side // 2]


def gather_wide(sums, count):
    left, middle, right = sums
    if count == 0:
        return middle
    return jnp.concatenate([left[left.shape[0] - count :], middle, right[:count]], axis=0)


def scatter_wide(tables, late, columns_ref, rows_ref, count):
    fields = max(len(tables), 1)
    found = []
    for side in range(3):
        if side != 1 and count == 0:
            found.append([None] * fields)
            continue
        low, high = side_rows(side, count)
        index = as_row(late[side][:4].astype(i32) - 1)
        (sums,) = scatter([late[side][4:]], *cell_hot(index, low, high))
        if tables:
            *others, last = scatter([table[side] for table in tables], columns_ref[side], rows_ref[side, low:high])
            found.append([*others, last + sums])
        else:
            found.append([sums])
    return [gather_wide([found[side][i] for side in range(3)], count) for i in range(fields)]


def faces_of(field):
    if field.shape[0] >= 128:
        turned = field.T
        return turned[0:1], turned[127:128]
    rows = iota((16, 128), 0)
    lanes = iota((16, 128), 1)
    pick = (((rows == 0) & (lanes == 0)) | ((rows == 1) & (lanes == 127))).astype(bf16)
    both = dot_nt(jnp.concatenate([pick, pick], axis=1), jnp.concatenate(parts(field), axis=1))
    return both[0:1], both[1:2]


def columns_of(left, right):
    width = left.shape[1]
    row = iota((128, width), 0)
    return jnp.where(row == 0, left, jnp.where(row == 127, right, 0.0)).T


def up_y(v, halo):
    return jnp.where(iota(v.shape, 2) == 127, halo, pltpu.roll(v, 127, 2))


def down_y(v, first):
    return jnp.where(iota(v.shape, 2) == 0, first, pltpu.roll(v, 1, 2))


def stencil(tx_up, tx_down, ty, tz, ty_first, field, halo):
    middle = field[1:-1]
    out = tx_up * field[2:] + tx_down * field[:-2]
    out = out + ty * up_y(middle, halo) + down_y(ty * middle, ty_first * halo)
    return out + tz * pltpu.roll(middle, 7, 1) + pltpu.roll(tz * middle, 1, 1)


def harmonic(first, second):
    both = first + second
    return jnp.where(both > 0.0, 2.0 * first * second / jnp.where(both > 0.0, both, 1.0), 0.0)


def read_faces(me, got_ref, start, width, across=0):
    along = me & 15
    line = (me >> 4) + across // 16
    inside = (line >= 0) & (line < 8)
    before = got_ref[jnp.clip(me + across - 1, 0, TILES - 1), :, start : start + width]
    after = got_ref[jnp.clip(me + across + 1, 0, TILES - 1), :, start : start + width]
    return jnp.where(inside & (along > 0), before, 0.0), jnp.where(inside & (along < 15), after, 0.0)


def put_faces(me, out_ref, start, first, last, across=0):
    width = first.shape[1]
    for at, face in ((me + across - 1, first), (me + across + 1, last)):
        out_ref[jnp.where((at >= 0) & (at < TILES), at, me), :, start : start + width] = face


def edge_codes(delta_ref, to_ref, b):
    block = b + delta_ref[b]
    code = block * 256 + to_ref[b]
    return jnp.where(block < 4, code, -1), jnp.where(block >= 4, code - 1024, -1)


def spread(rows, shift):
    lane = iota(rows.shape, 1)
    inside = (lane >= shift) if shift > 0 else (lane < TILES + shift)
    return jnp.where(inside, pltpu.roll(rows, shift % TILES, 1), 0.0)


def store_slots(out_ref, rows):
    for i in range(0, rows.shape[0], 128):
        part = rows[i : i + 128].T
        out_ref[:, 0, i : i + part.shape[1]] = part


def load_slots(got_ref, count):
    return jnp.concatenate([got_ref[:, 0, i : i + 128].T for i in range(0, count, 128)], axis=0)


def begin_kernel(me_ref, *refs):
    count = len(refs) // 2 - 2
    given, (out_ref, seg_ref, tile_out_ref), held, sems = refs[:count], refs[count : count + 3], refs[count + 3 : -1], refs[-1]
    copies = [pltpu.make_async_copy(a, b, sems.at[i]) for i, (a, b) in enumerate(zip(given, held))]
    passing = [pltpu.make_async_copy(held[8 + i], tile_out_ref.at[i], sems.at[count + i]) for i in range(3)]
    for copy in copies:
        copy.start()
    for copy in copies:
        copy.wait()
    for copy in passing:
        copy.start()
    tile_ref, layer_ref, cell_ref, press_frac_ref, accum_ref, chain_ref, mf_ref, fm_ref = held[:8]
    press_ref, cond_ref, accum_matrix_ref = held[8:11]
    delta_ref, from_ref, to_ref, trans_ref, well_tile_ref, well_cell_ref, well_rate_ref = held[11:]
    me = me_ref[0]
    code = seg_code()
    owner = fold(tile_ref[...])
    owner_row = as_row(owner)
    hot = owner_hot(owner_row)
    before = (iota((128, 128), 0) < iota((128, 128), 1)).astype(bf16)
    base = jnp.zeros((TILES, 1), f32)
    ranks = []
    for c in range(8):
        part = hot[:, c * 128 : (c + 1) * 128]
        wide = part.astype(f32)
        count = dot_nn(part, before) + base
        ranks.append(jnp.sum(wide * count, axis=0, keepdims=True))
        base = base + jnp.sum(wide, axis=1, keepdims=True)
    rank_row = jnp.concatenate(ranks, axis=1).astype(i32)
    rank = as_rows(rank_row)
    mask = rank_mask(rank_row)

    press = fold(press_frac_ref[...])
    fm = fold(fm_ref[...])
    mf = fold(mf_ref[...])
    last = code % 256 == 255
    tnext = jnp.where(last, 0.0, fold(chain_ref[...]))
    tprev = pltpu.roll(tnext, 1, 1)
    tprev = jnp.where(iota((8, 128), 1) == 0, pltpu.roll(tprev, 4, 0), tprev)
    diag = fold(accum_ref[...]) + tnext + tprev + fm
    inverse = 1.0 / diag
    partial = diag * press - chain(tnext, press)
    heres = [edge_codes(delta_ref, to_ref, b)[0] for b in range(4)]
    for b, picked in enumerate(totals([jnp.where(code == here, press, 0.0) for here in heres])):
        at = code == b * 256 + from_ref[b]
        partial = partial - jnp.where(at, trans_ref[b] * picked, 0.0)
    cell = fold(cell_ref[...])
    where_cell = ((((cell >> 7) * 8 + fold(layer_ref[...])) << 7) + (cell & 127) + 1).astype(f32)
    position = (iota((8, 128), 0) * 128 + iota((8, 128), 1) + 1).astype(f32)
    weight = fm * inverse
    slots = to_slots([where_cell, mf * press, weight * fm, weight * mf, weight * partial, position], hot, mask)
    inverse_index, slots = slots[80:96], slots[:80]
    place = (owner * CAP + rank).astype(f32)
    rows = []
    for b in range(4):
        _, there = edge_codes(delta_ref, to_ref, b)
        at = code == b * 256 + from_ref[b]
        gain = trans_ref[b] * inverse
        rows.append(jnp.where(iota((1, 128), 1) == 0, there.astype(f32), 0.0))
        for value in (place, where_cell, gain * fm, gain * partial, gain * trans_ref[b], gain * mf, code.astype(f32), gain):
            rows.append(jnp.sum(jnp.where(at, value, 0.0), axis=0, keepdims=True))
        rows.append(jnp.zeros((3, 128), f32))
    edges = [jnp.broadcast_to(jnp.sum(jnp.concatenate(rows, axis=0), axis=1, keepdims=True), (48, 128))]
    rows = edges + to_three(slots) + [spread(slots[:CAP], shift) for shift in BESIDE]
    store_slots(out_ref, jnp.concatenate(rows, axis=0))
    first_face, last_face = faces_of(jnp.concatenate([swap_x(ref[...]).reshape(ROWS, 128) for ref in (press_ref, cond_ref)], axis=0))
    for across in (-16, 0, 16):
        put_faces(me, out_ref, 384, first_face, last_face, across)
    for i, value in enumerate((tnext, inverse, partial, fm, mf, owner.astype(f32), rank.astype(f32), press)):
        seg_ref[i] = value
    for i in range(2):
        seg_ref[8 + i] = inverse_index[8 * i : 8 * i + 8] - 1.0
    lane = iota((8, 128), 1)
    own = jnp.zeros((8, 128), f32)
    for b in range(4):
        here, there = edge_codes(delta_ref, to_ref, b)
        for i, value in enumerate((b * 256 + from_ref[b], here, there)):
            own = jnp.where(lane == 8 * b + i, value.astype(f32), own)
        own = jnp.where(lane == 8 * b + 3, trans_ref[b], own)
    seg_ref[10] = own
    plane_x = iota((EXT, 128), 0) + ((me >> 4) - 1) * 8
    plane_y = iota((EXT, 128), 1) + (me & 15) * 128
    source = jnp.zeros((EXT, 128), f32)
    for w in range(well_tile_ref.shape[0]):
        tile = well_tile_ref[w]
        cell = well_cell_ref[w]
        at = (plane_x == (tile >> 4) * 8 + (cell >> 7)) & (plane_y == (tile & 15) * 128 + (cell & 127))
        source = source + jnp.where(at, well_rate_ref[w], 0.0)
    for i in range(3):
        seg_ref[11 + i] = source[8 * i : 8 * i + 8]
    seg_ref[14] = where_cell
    for i, ref in enumerate((press_ref, cond_ref, accum_matrix_ref)):
        seg_ref[15 + 8 * i : 23 + 8 * i] = ref[...]
    for copy in passing:
        copy.wait()


def edge_in(row, k, i):
    at = 12 * k + i
    return row[:, at : at + 1]


def cells_kernel(
    me_ref,
    got_ref, inside_ref, across_ref, seg_ref,
    out_ref, cells_ref, field_ref, index_ref, columns_ref, rows_ref, edge_ref, beside_ref, res_ref,
):
    me = me_ref[0]
    slots = load_slots(got_ref, 384)
    even = ((me >> 4) & 1) == 0
    press, cond, accum = (
        jnp.concatenate(
            [swap_x(jnp.where(even, b, a)), seg_ref[15 + 8 * i : 23 + 8 * i], swap_x(jnp.where(even, a, b))], axis=0
        )
        for i, a, b in ((i, inside_ref[i], across_ref[i]) for i in range(3))
    )
    sums = []
    for side in range(3):
        table = slots[48 + side * 80 : 128 + side * 80]
        index = table[:CAP].astype(i32) - 1
        if side == 1:
            index_ref[...] = index
            own = index
        columns, rows = cell_hot(as_row(index))
        columns_ref[side] = columns
        rows_ref[side] = rows
        sums.append(scatter([table[i : i + CAP] for i in range(CAP, 5 * CAP, CAP)], columns, rows))
    flow, weight, mirror, first = (jnp.concatenate([sums[side][i] for side in range(3)], axis=0) for i in range(4))
    beside = slots[288:384].astype(i32) - 1
    along = me & 15
    for i, (there, column) in enumerate(((along > 0, 127), (along < 15, 0))):
        part = beside[48 * i : 48 * i + 48]
        beside_ref[48 * i : 48 * i + 48] = jnp.where(there & (part >= 0) & ((part & 127) == column), part >> 7, -1)

    halos = [columns_of(*read_faces(me, got_ref, 384, 2 * ROWS, across)) for across in (-16, 0, 16)]
    press_halo = jnp.concatenate([halo[:ROWS].reshape(8, 8, 128) for halo in halos], axis=0)
    cond_halo = jnp.concatenate([halo[ROWS:].reshape(8, 8, 128) for halo in halos], axis=0)
    wide = (EXT, 8, 128)
    tx = harmonic(cond[:-1], cond[1:])
    ty = harmonic(cond, up_y(cond, cond_halo))
    tz = 0.5 * harmonic(cond, jnp.where(iota(wide, 1) == 7, 0.0, pltpu.roll(cond, 7, 1)))
    ty_first = jnp.where(iota(wide, 2) == 0, harmonic(cond, cond_halo), 0.0)
    diag = accum + ty + down_y(ty, ty_first) + tz + pltpu.roll(tz, 1, 1)
    diag = diag[1:-1] + tx[1:] + tx[:-1]
    inverse = jnp.where(diag > 0.0, 1.0 / jnp.where(diag > 0.0, diag, 1.0), 0.0)
    source = jnp.concatenate([seg_ref[11 + i] for i in range(3)], axis=0)

    res = diag * press[1:-1] - flow[1:-1] - source.reshape(EXT, 1, 128)[1:-1]
    res = res - stencil(tx[1:], tx[:-1], ty[1:-1], tz[1:-1], ty_first[1:-1], press, press_halo[1:-1])
    field = inverse * res
    cells_ref[0, : EXT - 1] = tx
    for i, value in ((1, ty), (2, tz), (3, ty_first), (6, first - weight * press), (7, mirror)):
        cells_ref[i] = value
    cells_ref[4, 1 : EXT - 1] = inverse
    cells_ref[5, 1 : EXT - 1] = res
    field_ref[...] = field
    res_ref[...] = swap_x(res[7:15])

    code = seg_code().astype(f32)
    _, inverse_f, partial, fm, _, owner, _, press_f = (seg_ref[i] for i in range(8))
    edge = jnp.where(me > 0, got_ref[before(me), :, 0:128], -1.0)
    lane = iota((1, 128), 1)
    cells, terms, picks, found = [], [], [], []
    ends = [code == edge_in(edge, k, 0) for k in range(4)]
    wanted = (press_f, owner, seg_ref[14], fm * inverse_f)
    sums = totals([jnp.where(at, value, 0.0) for at in ends for value in wanted])
    for k in range(4):
        picked = sums[4 * k]
        at = (lane == (edge_in(edge, k, 1).astype(i32) >> 4)) & (edge_in(edge, k, 0) >= 0.0)
        cells.append(jnp.where(at, edge_in(edge, k, 2), 0.0))
        terms.append(jnp.where(at, -edge_in(edge, k, 3) * picked, 0.0))
        picks.append(jnp.broadcast_to(picked, (1, 128)))
        found.append(sums[4 * k + 1 : 4 * k + 4])
    for k in range(4):
        edge = jnp.where(lane == 12 * k + 4, edge - edge_in(edge, k, 5) * sums[4 * k], edge)
    edge_ref[...] = jnp.broadcast_to(edge, (8, 128))
    late = jnp.concatenate(cells + terms, axis=0)

    taken = [find(press[8:16].reshape(ROWS, 128), own), find(own_tile(field, 1), own)]
    rows = taken + [spread(taken[0], 1)]
    store_slots(out_ref, jnp.concatenate(rows + to_three(late) + picks + [jnp.zeros((52, 128), f32)], axis=0))
    put_faces(me, out_ref, FIRST, *faces_of(field[1:-1].reshape(-1, 128)))
    put_faces(me, out_ref, FIRST_INVERSE, *faces_of(inverse[3:19].reshape(-1, 128)))
    put_entries(out_ref, before(me), FIRST_ENDS, [end for ends in found for end in ends])


def put_entries(out_ref, at, start, entries):
    lane = iota((1, len(entries)), 1)
    row = jnp.zeros(lane.shape, f32)
    for i, entry in enumerate(entries):
        row = jnp.where(lane == i, entry, row)
    out_ref[at, :, start : start + len(entries)] = row


def get_entries(got_ref, at, start, count):
    row = got_ref[at, :, start : start + count]
    return [row[:, i : i + 1] for i in range(count)]


def before(me):
    return jnp.maximum(me - 1, 0)


def after(me):
    return jnp.minimum(me + 1, TILES - 1)


FIRST = 76
FIRST_ENDS = FIRST + 160
FIRST_INVERSE = FIRST_ENDS + 12
WIDE = 232
SLIM = 128
SLIM_TWO = 248


def wide_lanes(k):
    entries = WIDE + 8 * (22 - 2 * k)
    return entries, entries + 4


def own_edges(seg_ref):
    own = seg_ref[10][0:1]
    return [[own[:, 8 * b + i : 8 * b + i + 1] for b in range(4)] for i in range(4)]


def edge_terms(code, edges, frac):
    starts, _, _, factors = edges
    sums = totals([jnp.where(code == start, frac, 0.0) for start in starts])
    return [factor * picked for factor, picked in zip(factors, sums)]


def arrive(code, targets, terms):
    gain = jnp.zeros(code.shape, f32)
    for target, term in zip(targets, terms):
        gain = gain + jnp.where(code == target, term, 0.0)
    return gain


def late_rows(edges, ends, terms):
    lane = iota((1, 128), 1)
    cells, values = [], []
    for there, (tile, cell, weight), term in zip(edges[2], ends, terms):
        at = (lane == tile.astype(i32)) & (there >= 0.0)
        cells.append(jnp.where(at, cell, 0.0))
        values.append(jnp.where(at, weight * term, 0.0))
    return jnp.concatenate(cells + values, axis=0)


def to_three(rows):
    return [spread(rows, 16), rows, spread(rows, -16)]


def own_tile(field, k):
    return field[8 - k : 16 - k].reshape(ROWS, 128)


def starts_of(edge, table):
    place = (iota((CAP, 128), 1) * CAP + iota((CAP, 128), 0)).astype(f32)
    return totals([jnp.where(place == edge_in(edge, k, 1), table, 0.0) for k in range(4)])


def advance(cells_ref, k, field, halo, flow):
    low, high = k + 1, EXT - 1 - k
    ty, tz, ty_first, inverse, res = (cells_ref[i, low:high] for i in range(1, 6))
    tx_up, tx_down = cells_ref[0, low:high], cells_ref[0, low - 1 : high - 1]
    return inverse * (res + stencil(tx_up, tx_down, ty, tz, ty_first, field, halo) + flow)


def wide_halo(me, got_ref, start, count):
    return columns_of(*read_faces(me, got_ref, start, 8 * count)).reshape(count, 8, 128)


def ends_of(ends_ref):
    held = ends_ref[0:1]
    return [[held[:, 3 * k + i : 3 * k + i + 1] for i in range(3)] for k in range(4)]


def send_wide(me, out_ref, k, code, edges, ends, seg_ref, cells_ref, index_ref, field, frac, resf):
    tnext, inverse_f, fm = seg_ref[0], seg_ref[1], seg_ref[3]
    terms = edge_terms(code, edges, frac)
    ahead = inverse_f * (resf + chain(tnext, frac) + arrive(code, edges[1], terms))
    part = advance(cells_ref, k, field, jnp.zeros((22 - 2 * k, 8, 128), f32), 0.0)
    position = jnp.concatenate([seg_ref[8], seg_ref[9]], axis=0).astype(i32)
    now = find(fm * frac, position)
    rows = [find(own_tile(field, k), index_ref[...])] + to_three(now) + to_three(find(fm * ahead, position))
    rows += to_three(late_rows(edges, ends, terms)) + [spread(now, shift) for shift in BESIDE]
    store_slots(out_ref, jnp.concatenate(rows + [jnp.zeros((24, 128), f32)], axis=0))
    entries, further = wide_lanes(k)
    put_faces(me, out_ref, WIDE, *faces_of(field[1:-1].reshape(-1, 128)))
    put_faces(me, out_ref, further, *faces_of(part[1:-1].reshape(-1, 128)))
    put_entries(out_ref, jnp.where(me + 1 < TILES, me + 1, me), entries, terms)


def first_kernel(
    me_ref, got_ref, cells_ref, field_ref, index_ref, columns_ref, rows_ref, seg_ref, edge_ref,
    out_ref, new_field_ref, new_frac_ref, resf_ref, ends_ref, halo_inverse_ref, res_fracture_ref,
):
    me = me_ref[0]
    slots = load_slots(got_ref, 128)
    code = seg_code().astype(f32)
    tnext, inverse_f, partial, fm, mf, owner, rank = (seg_ref[i] for i in range(7))
    owner = owner.astype(i32)
    rank = rank.astype(i32)
    edge = edge_ref[0:1]
    edges = own_edges(seg_ref)
    starts, targets, nexts, factors = edges

    resf = partial - fm * look_up(slots[0:16], rank, owner)
    picks = get_entries(got_ref, after(me), 72, 4)
    for b in range(4):
        at = (code == starts[b]) & (nexts[b] >= 0.0)
        resf = resf - jnp.where(at, factors[b] * picks[b], 0.0)
    frac = inverse_f * resf
    terms = edge_terms(code, edges, frac)
    begun = starts_of(edge, slots[32:48])
    coming = [edge_in(edge, k, 4) - edge_in(edge, k, 3) * begun[k] for k in range(4)]
    gain = resf + chain(tnext, frac) + mf * look_up(slots[16:32], rank, owner)
    gain = gain + arrive(code, targets, terms) + arrive(code, [edge_in(edge, k, 0) for k in range(4)], coming)
    frac = inverse_f * gain
    late = [slots[48 + 8 * side : 56 + 8 * side] for side in range(3)]
    (flow,) = scatter_wide([], late, columns_ref, rows_ref, 6)
    field = advance(cells_ref, 1, field_ref[...], wide_halo(me, got_ref, FIRST, 20), flow + cells_ref[6, 2:22])
    new_field_ref[...] = field
    new_frac_ref[...] = frac
    resf_ref[...] = resf
    res_fracture_ref[...] = unfold(resf)
    halo_inverse_ref[...] = wide_halo(me, got_ref, FIRST_INVERSE, 16)
    ends = get_entries(got_ref, after(me), FIRST_ENDS, 12)
    ends = [ends[3 * k : 3 * k + 3] for k in range(4)]
    lane = iota((8, 128), 1)
    held = jnp.zeros((8, 128), f32)
    for k in range(4):
        for i in range(3):
            held = jnp.where(lane == 3 * k + i, ends[k][i], held)
    ends_ref[...] = held

    send_wide(me, out_ref, 2, code, edges, ends, seg_ref, cells_ref, index_ref, field, frac, resf)


def even_kernel(
    k, me_ref, got_ref, cells_ref, field_ref, index_ref, columns_ref, rows_ref, seg_ref, edge_ref,
    frac_ref, resf_ref, ends_ref, halo_inverse_ref, beside_ref,
    out_ref, third_ref, new_field_ref, new_frac_ref,
):
    me = me_ref[0]
    slots = load_slots(got_ref, 256)
    code = seg_code().astype(f32)
    tnext, inverse_f, _, fm, mf, owner, rank = (seg_ref[i] for i in range(7))
    edge = edge_ref[0:1]
    edges = own_edges(seg_ref)
    targets = edges[1]
    resf = resf_ref[...]
    frac = frac_ref[...]
    entries, further = wide_lanes(k)
    coming = get_entries(got_ref, before(me), entries, 4)
    gain = resf + chain(tnext, frac) + mf * look_up(slots[0:16], rank.astype(i32), owner.astype(i32))
    gain = gain + arrive(code, targets, edge_terms(code, edges, frac))
    gain = gain + arrive(code, [edge_in(edge, b, 0) for b in range(4)], coming)
    frac = inverse_f * gain
    terms = edge_terms(code, edges, frac)
    ahead = inverse_f * (resf + chain(tnext, frac) + arrive(code, targets, terms))
    new_frac_ref[...] = frac

    tables = [[slots[first + side * CAP : first + CAP + side * CAP] for side in range(3)] for first in (16, 64)]
    late = [slots[112 + 8 * side : 120 + 8 * side] for side in range(3)]
    flow, later = scatter_wide(tables, late, columns_ref, rows_ref, 7 - k)
    beside = []
    for side in range(3):
        height = ROWS if side == 1 else 8 * (6 - k)
        level = iota((height, 128), 0) + (ROWS - height if side == 0 else 0)
        lane = iota((height, 128), 1)
        column = jnp.zeros((height, 128), f32)
        for i, at in enumerate((0, 127)):
            first = 48 * i + CAP * side
            held = jnp.zeros((height, 128), f32)
            for r in range(first, first + CAP):
                held = held + jnp.where(level == beside_ref[r : r + 1], slots[136 + r : 137 + r], 0.0)
            column = jnp.where(lane == at, jnp.sum(held, axis=1, keepdims=True), column)
        beside.append(column.reshape(-1, 8, 128))
    beside = jnp.concatenate(beside, axis=0)
    second = field_ref[...]
    third = advance(cells_ref, k, second, wide_halo(me, got_ref, WIDE, 22 - 2 * k), flow)
    inner = second[2:-2]
    lane = iota(inner.shape, 2)
    joint = jnp.where(lane == 0, cells_ref[3, k + 2 : 22 - k], jnp.where(lane == 127, cells_ref[1, k + 2 : 22 - k], 0.0))
    halo = wide_halo(me, got_ref, further, 20 - 2 * k) + halo_inverse_ref[k - 2 : 18 - k] * (joint * inner + beside)
    field = advance(cells_ref, k + 1, third, halo, later[1:-1] + cells_ref[7, k + 2 : 22 - k] * inner)
    third_ref[...] = third
    new_field_ref[...] = field

    position = jnp.concatenate([seg_ref[8], seg_ref[9]], axis=0).astype(i32)
    ends = ends_of(ends_ref)
    own_third = find(own_tile(third, k + 1), index_ref[...])
    rows = [own_third, find(own_tile(field, k + 2), index_ref[...]), spread(own_third, 1)] + to_three(find(fm * ahead, position))
    rows += to_three(late_rows(edges, ends, terms))
    store_slots(out_ref, jnp.concatenate(rows + [jnp.zeros((8, 128), f32)], axis=0))
    put_faces(me, out_ref, SLIM, *faces_of(field[1:-1].reshape(-1, 128)))
    to_next = jnp.where(me + 1 < TILES, me + 1, me)
    put_entries(out_ref, to_next, SLIM + 8 * (18 - 2 * k), terms + edge_terms(code, edges, ahead))
    put_entries(out_ref, jnp.where(me + 2 < TILES, me + 2, me), SLIM_TWO, terms + edges[2])


def odd_kernel(
    k, final, me_ref, got_ref, cells_ref, field_ref, index_ref, columns_ref, rows_ref, seg_ref, edge_ref,
    frac_ref, resf_ref, ends_ref, third_ref, *outs,
):
    me = me_ref[0]
    slots = load_slots(got_ref, 128)
    code = seg_code().astype(f32)
    tnext, inverse_f, _, _, mf, owner, rank = (seg_ref[i] for i in range(7))
    owner = owner.astype(i32)
    rank = rank.astype(i32)
    edge = edge_ref[0:1]
    edges = own_edges(seg_ref)
    targets = edges[1]
    resf = resf_ref[...]
    frac = frac_ref[...]
    coming = get_entries(got_ref, before(me), SLIM + 8 * (22 - 2 * k), 8)
    two = jnp.where(me > 1, got_ref[jnp.maximum(me - 2, 0), :, 128:256], -1.0)
    lane = iota((1, 128), 1)
    codes = jnp.where((lane >= SLIM_TWO - 128) & (lane < SLIM_TWO - 124), pltpu.roll(two, 124, 1), -2.0)
    meets = jnp.concatenate([jnp.where(codes == edge_in(edge, b, 7), two, 0.0) for b in range(4)], axis=0)
    meets = jnp.sum(meets, axis=1, keepdims=True)
    begun = starts_of(edge, slots[32:48])
    heres = [edge_in(edge, b, 0) for b in range(4)]
    gain = resf + chain(tnext, frac) + mf * look_up(slots[0:16], rank, owner)
    gain = gain + arrive(code, targets, edge_terms(code, edges, frac))
    frac = inverse_f * (gain + arrive(code, heres, coming[:4]))
    terms = [
        coming[4 + b] + edge_in(edge, b, 6) * begun[b] + edge_in(edge, b, 8) * meets[b : b + 1] for b in range(4)
    ]
    gain = resf + chain(tnext, frac) + mf * look_up(slots[16:32], rank, owner)
    gain = gain + arrive(code, targets, edge_terms(code, edges, frac))
    frac = inverse_f * (gain + arrive(code, heres, terms))

    late = [slots[96 + 8 * side : 104 + 8 * side] for side in range(3)]
    tables = [[slots[48 + side * CAP : 64 + side * CAP] for side in range(3)]]
    (flow,) = scatter_wide(tables, late, columns_ref, rows_ref, 7 - k)
    flow = flow + cells_ref[7, k + 1 : 23 - k] * third_ref[2:-2]
    field = advance(cells_ref, k, field_ref[...], wide_halo(me, got_ref, SLIM, 22 - 2 * k), flow)
    if final:
        adj_matrix_ref, adj_fracture_ref = outs
        adj_matrix_ref[...] = swap_x(field)
        adj_fracture_ref[...] = unfold(frac)
        return
    out_ref, new_field_ref, new_frac_ref = outs
    new_field_ref[...] = field
    new_frac_ref[...] = frac
    send_wide(me, out_ref, k + 1, code, edges, ends_of(ends_ref), seg_ref, cells_ref, index_ref, field, frac, resf)


def hold_kernel(given_ref, out_ref):
    out_ref[:15] = given_ref[:15]
    for i in range(15, 39, 8):
        out_ref[i : i + 8] = swap_x(given_ref[i : i + 8])


def call(kernel, name, scalars, arrays, outs, space=pltpu.VMEM, scratch=(), limit=20 * 1024 * 1024, out_spaces=None):
    spec = [pl.BlockSpec(memory_space=pltpu.SMEM)] * len(scalars)
    spec += [pl.BlockSpec(memory_space=space)] * len(arrays)
    return pl.pallas_call(
        kernel,
        name=name,
        out_shape=[jax.ShapeDtypeStruct(shape, kind) for shape, kind in outs],
        in_specs=spec,
        out_specs=[pl.BlockSpec(memory_space=out) for out in out_spaces or [pltpu.VMEM] * len(outs)],
        scratch_shapes=list(scratch),
        compiler_params=pltpu.CompilerParams(vmem_limit_bytes=limit),
    )(*scalars, *arrays)


def exchange(message):
    return lax.all_to_all(message, ALL, split_axis=0, concat_axis=0, tiled=True)


def swapped(block, first):
    pairs = [(i, i + 1) for i in range(first, lax.axis_size("gx") - 1, 2)]
    return lax.ppermute(block, "gx", pairs + [(j, i) for i, j in pairs])


def body(
    press_matrix, cond_matrix, accum_matrix, press_frac, accum_frac, trans_chain, couple_mf, couple_fm,
    conn_tile, conn_layer, conn_cell, inter_delta, inter_from, inter_to, inter_trans, well_tile, well_cell, well_rate,
):
    me = lax.axis_index(ALL).astype(i32).reshape(1)
    wide = (EXT, 8, 128)
    tile = (LAYERS, 8, 128)
    seg = (8, 128)

    given = (
        conn_tile, conn_layer, conn_cell, press_frac, accum_frac, trans_chain, couple_mf, couple_fm,
        press_matrix, cond_matrix, accum_matrix,
        inter_delta, inter_from, inter_to, inter_trans, well_tile, well_cell, well_rate,
    )
    message, segs, stacked = call(
        begin_kernel,
        "begin",
        (me,),
        given,
        [((TILES, 1, 512), f32), ((39, *seg), f32), ((3, *tile), f32)],
        pl.ANY,
        [(pltpu.VMEM if a.ndim > 1 else pltpu.SMEM)(a.shape, a.dtype) for a in given] + [pltpu.SemaphoreType.DMA((len(given) + 3,))],
        64 * 1024 * 1024,
        [pltpu.VMEM, pltpu.VMEM, pl.ANY],
    )
    inside = swapped(stacked, 0)
    across = swapped(stacked, 1)
    (segs,) = call(hold_kernel, "hold", (), (segs,), [(segs.shape, f32)])
    got = exchange(message)
    message, cells, field, index, columns, rows, edge, beside, res_matrix = call(
        cells_kernel,
        "cells",
        (me,),
        (got, inside, across, segs),
        [((TILES, 1, 384), f32), ((8, *wide), f32), ((22, 8, 128), f32), ((CAP, 128), i32), ((3, 128, SLOTS), bf16),
         ((3, ROWS, SLOTS), bf16), (seg, f32), ((96, 128), i32), (tile, f32)],
    )
    kept = (index, columns, rows, segs, edge)

    def after_sweeps(k):
        return ((EXT - 2 * k, 8, 128), f32)

    wide_message = ((TILES, 1, 512), f32)
    slim_message = ((TILES, 1, 256), f32)
    got = exchange(message)
    message, field, frac, resf, ends, halo_inverse, res_fracture = call(
        first_kernel,
        "first",
        (me,),
        (got, cells, field, *kept),
        [wide_message, after_sweeps(2), (seg, f32), (seg, f32), (seg, f32), ((16, 8, 128), f32), ((4, 256), f32)],
    )
    for k, final in ((2, False), (5, True)):
        got = exchange(message)
        message, third, field, frac = call(
            functools.partial(even_kernel, k),
            "even",
            (me,),
            (got, cells, field, *kept, frac, resf, ends, halo_inverse, beside),
            [slim_message, after_sweeps(k + 1), after_sweeps(k + 2), (seg, f32)],
        )
        got = exchange(message)
        outs = [(tile, f32), ((4, 256), f32)] if final else [wide_message, after_sweeps(k + 3), (seg, f32)]
        results = call(
            functools.partial(odd_kernel, k + 2, final),
            "odd",
            (me,),
            (got, cells, field, *kept, frac, resf, ends, third),
            outs,
        )
        if not final:
            message, field, frac = results
    adj_matrix, adj_fracture = results
    return res_matrix, res_fracture, adj_matrix, adj_fracture


def solution(mesh):
    cells = P(None, "gx", YA)
    segs = P(ALL, None)
    blocks = P(ALL)
    in_specs = (cells,) * 3 + (segs,) * 8 + (blocks,) * 4 + (P(),) * 3
    return jax.shard_map(body, mesh=mesh, in_specs=in_specs, out_specs=(cells, segs, cells, segs), check_vma=False)
```
